32 devices in a mesh: dp: 16 (over z, y, x), mp: 2 (over core).
Axes of the slice: x: 2, y: 2, z: 4, core: 2. Of those that a mesh axis runs over, the one named last changes fastest.
Arguments:
- text_in: bfloat16 [16, 1024, 1024], P('dp'), may hold values from -6 to 6
- patch_in: bfloat16 [16, 256, 1024], P('dp'), may hold values from -6 to 6
- cot_text: bfloat16 [16, 1024, 1024], P('dp'), may hold values from -6 to 6
- cot_patch: bfloat16 [16, 256, 1024], P('dp'), may hold values from -6 to 6
- text_count: int32 [16], replicated, may hold values from 50 to 1024, as said below
- intersection: int32 [16, 4, 1024], P('dp'), may hold values from 0 to 196, as said below
- text_cell: int32 [16, 2, 1024], replicated, may hold values from 0 to 13
- wq: bfloat16 [1024, 1024], P('dp', 'mp'), may hold values from -0.1875 to 0.1875
- wk: bfloat16 [1024, 1024], P('dp', 'mp'), may hold values from -0.1875 to 0.1875
- wv: bfloat16 [1024, 1024], P('dp', 'mp'), may hold values from -0.1875 to 0.1875
- wo_t: bfloat16 [1024, 1024], P('dp', 'mp'), may hold values from -1.5 to 1.5
- gain_one: bfloat16 [1024], P('dp'), may hold values from 0.099609375 to 1.8984375
- w_gate: bfloat16 [1024, 2816], P('dp', 'mp'), may hold values from -0.1875 to 0.1875
- w_up: bfloat16 [1024, 2816], P('dp', 'mp'), may hold values from -0.1875 to 0.1875
- w_down_t: bfloat16 [1024, 2816], P('dp', 'mp'), may hold values from -0.21875 to 0.21875
- gain_two: bfloat16 [1024], P('dp'), may hold values from 0.099609375 to 1.8984375
- bias_table: bfloat16 [48, 16], P(None, 'mp'), may hold values from -4 to 4
Outputs:
- text_out: bfloat16 [16, 1024, 1024], P('dp')
- patch_out: bfloat16 [16, 256, 1024], P('dp')
- text_grad: bfloat16 [16, 1024, 1024], P('dp')
- patch_grad: bfloat16 [16, 256, 1024], P('dp')
- wq_grad: float32 [1024, 1024], P('dp', 'mp')
- wk_grad: float32 [1024, 1024], P('dp', 'mp')
- wv_grad: float32 [1024, 1024], P('dp', 'mp')
- wo_grad: float32 [1024, 1024], P('dp', 'mp')
- gain_one_grad: float32 [1024], P('dp')
- gate_grad: float32 [1024, 2816], P('dp', 'mp')
- up_grad: float32 [1024, 2816], P('dp', 'mp')
- down_grad: float32 [1024, 2816], P('dp', 'mp')
- gain_two_grad: float32 [1024], P('dp')
- table_grad: float32 [48, 16], P(None, 'mp')
The draws below stay inside these ranges and needn't reach their ends.
Inputs may be any that keep to these rules, and one draw needn't show every extreme that they name: `text_count`: one page has exactly 1024 text tokens. `intersection`: patches in one grid row that a token's box covers, consecutive from the first entry; the first entry is always a patch, unused entries hold 196.
All inputs are finite; a program needn't handle non-finite values.
Results may differ from the reference program's by a relative error of at most 0.014.
Values may be sent and summed in bfloat16 or wider, within the bound.
No kernel may reach another device: no remote copies, remote signals or barrier semaphores. Data moves between devices by JAX's collectives and lax.ppermute only.
A program may use at most 256 MiB of HBM per device.

```python
import jax
import jax.numpy as jnp
from jax import lax

D = 1024
H = 16
DH = 64
FF = 2816
RB = 32
LQ = 4
GRID = 14
PSLOT = 256
TXT = 1024
TXT_MIN = 50
OVL = 4
HD = 1024
PATCHES = 196
NB = 48
PAGES = 16


def box_layout(key):
    first_key, second_key, third_key = jax.random.split(key, 3)
    row_start = jax.random.randint(first_key, (PAGES, TXT), 0, GRID)
    col_start = jax.random.randint(second_key, (PAGES, TXT), 0, GRID)
    box_span = jax.random.randint(third_key, (PAGES, TXT), 1, OVL + 1)
    return (row_start, col_start, box_span)


def draw_text_count(key, part):
    key = jax.random.fold_in(key, 3)
    first_key, second_key = jax.random.split(key)
    counts = jax.random.randint(first_key, (PAGES,), TXT_MIN, TXT + 1)
    full_page = jax.random.randint(second_key, (), 0, PAGES)
    return jnp.where(jnp.arange(PAGES) == full_page, TXT, counts).astype(jnp.int32)


def draw_intersection(key, part):
    row_start, col_start, box_span = box_layout(key)
    step_ids = jnp.arange(OVL, dtype=jnp.int32)[None, :, None]
    col_each = col_start[:, None, :] + step_ids
    valid = (step_ids < box_span[:, None, :]) & (col_each < GRID)
    return jnp.where(valid, row_start[:, None, :] * GRID + col_each, PATCHES).astype(jnp.int32)


def draw_text_cell(key, part):
    row_start, col_start, box_span = box_layout(key)
    return jnp.stack([row_start, col_start], axis=1).astype(jnp.int32)


def shard_levels(rng, shape, cuts, low, high):
    def one(axis_at, shards_of):
        steps = jax.random.uniform(jax.random.fold_in(jax.random.fold_in(rng, 6), axis_at), (shards_of,), jnp.float32, low / len(cuts), high / len(cuts))
        return jnp.repeat(jnp.exp(steps), shape[axis_at] // shards_of).reshape((-1,) + (1,) * (len(shape) - axis_at - 1))

    loudness = one(*cuts[0])
    for cut in cuts[1:]:
        loudness = loudness * one(*cut)
    return loudness


def centred(own_key, extent, deviation, reach, cuts=(), kind=jnp.bfloat16):
    entries = jax.random.normal(own_key, extent, jnp.float32) * deviation
    if len(cuts) > 0:
        entries = shard_levels(own_key, extent, cuts, -0.22, 0.18) * entries
    return jnp.clip(entries, min=-reach, max=reach).astype(kind)


def setup_inputs(seed: int = 0) -> dict:
    key_of = jax.random.split(jax.random.key(seed), 18)
    return {
        "text_in": centred(key_of[0], (PAGES, TXT, D), 1.0, 6.0, ((0, 16),)),
        "patch_in": centred(key_of[1], (PAGES, PSLOT, D), 1.0, 6.0, ((0, 16),)),
        "cot_text": centred(key_of[2], (PAGES, TXT, D), 1.0, 6.0, ((0, 16),)),
        "cot_patch": centred(key_of[3], (PAGES, PSLOT, D), 1.0, 6.0, ((0, 16),)),
        "text_count": draw_text_count(jax.random.fold_in(key_of[17], 71), 0),
        "intersection": draw_intersection(jax.random.fold_in(key_of[17], 71), 0),
        "text_cell": draw_text_cell(jax.random.fold_in(key_of[17], 71), 0),
        "wq": centred(key_of[7], (D, HD), D ** -0.5, 0.1875, ((0, 16), (1, 2))),
        "wk": centred(key_of[8], (D, HD), D ** -0.5, 0.1875, ((0, 16), (1, 2))),
        "wv": centred(key_of[9], (D, HD), D ** -0.5, 0.1875, ((0, 16), (1, 2))),
        "wo_t": centred(key_of[10], (D, HD), (HD // 64) ** -0.5, 1.5, ((0, 16), (1, 2))),
        "gain_one": jnp.clip(1.0 + 0.18 * jax.random.normal(key_of[11], (D,), jnp.float32), 0.099609375, 1.8984375).astype(jnp.bfloat16),
        "w_gate": centred(key_of[12], (D, FF), D ** -0.5, 0.1875, ((0, 16), (1, 2))),
        "w_up": centred(key_of[13], (D, FF), D ** -0.5, 0.1875, ((0, 16), (1, 2))),
        "w_down_t": centred(key_of[14], (D, FF), (FF // 4) ** -0.5, 0.21875, ((0, 16), (1, 2))),
        "gain_two": jnp.clip(1.0 + 0.18 * jax.random.normal(key_of[15], (D,), jnp.float32), 0.099609375, 1.8984375).astype(jnp.bfloat16),
        "bias_table": centred(key_of[16], (NB, H), 1.0, 4.0, ((1, 2),)),
    }


@jax.custom_vjp
def low(v):
    return lax.optimization_barrier(v.astype(jnp.bfloat16)).astype(jnp.float32)

@jax.custom_vjp
def low_back(v):
    return v

def low_keep(v):
    return (low(v), None)

def low_pass(kept, grad):
    return (grad,)

def back_keep(v):
    return (v, None)

def back_low(kept, grad):
    return (low(grad),)
low.defvjp(low_keep, low_pass)
low_back.defvjp(back_keep, back_low)
EPS = 1e-06
HIGH = lax.Precision.HIGHEST

def rms_scale(row_data, gain):
    scale_inv = lax.rsqrt(lax.optimization_barrier(jnp.mean(row_data * row_data, axis=-1, keepdims=True)) + EPS)
    return row_data * scale_inv * gain

def page_places(page_len, page_cells):
    text_ids = jnp.arange(TXT, dtype=jnp.int32)
    slot_ids = jnp.arange(PSLOT, dtype=jnp.int32)
    positions = jnp.concatenate([text_ids, page_len + slot_ids])
    row_coord = jnp.concatenate([page_cells[0], slot_ids // GRID])
    col_coord = jnp.concatenate([page_cells[1], slot_ids % GRID])
    live_keys = jnp.concatenate([text_ids < page_len, slot_ids < PATCHES])
    return (positions, row_coord, col_coord, live_keys)

def bucket_onehot(positions, row_coord, col_coord):
    rel_bucket = jnp.clip(positions[None, :] - positions[:, None], -(RB // 2), RB // 2 - 1) + RB // 2
    row_gap = jnp.minimum(jnp.abs(row_coord[None, :] - row_coord[:, None]), LQ - 1)
    col_gap = jnp.minimum(jnp.abs(col_coord[None, :] - col_coord[:, None]), LQ - 1)
    lay_bucket = RB + row_gap * LQ + col_gap
    bucket_ids = jnp.arange(NB, dtype=jnp.int32)
    return ((rel_bucket[:, :, None] == bucket_ids) | (lay_bucket[:, :, None] == bucket_ids)).astype(jnp.float32)

def page_layer(weights, text_rows, patch_rows, page_len, page_lists, page_cells):
    wq, wk, wv, wo_t, gain_one, w_gate, w_up, w_down_t, gain_two, bias_table = weights
    slot_ids = jnp.arange(PSLOT, dtype=jnp.int32)
    covering = lax.optimization_barrier(jnp.sum((page_lists[:, :, None] == slot_ids) & (slot_ids < PATCHES), axis=0)).astype(jnp.float32)
    embedded = text_rows + jnp.dot(covering, patch_rows, precision=HIGH)
    rows_all = jnp.concatenate([embedded, patch_rows], axis=0)
    positions, row_coord, col_coord, live_keys = page_places(page_len, page_cells)
    onehot = bucket_onehot(positions, row_coord, col_coord)
    normed_one = low(rms_scale(rows_all, gain_one))
    queries = low_back(low(jnp.dot(normed_one, wq, precision=HIGH))).reshape(-1, H, DH)
    key_rows = low_back(low(jnp.dot(normed_one, wk, precision=HIGH))).reshape(-1, H, DH)
    value_rows = low_back(low(jnp.dot(normed_one, wv, precision=HIGH))).reshape(-1, H, DH)
    scores = jnp.einsum('qhd,khd->hqk', queries, key_rows, precision=HIGH) * DH ** (-0.5)
    scores = low_back(scores + jnp.einsum('qkb,bh->hqk', onehot, bias_table, precision=HIGH))
    scores = jnp.where(live_keys[None, None, :], scores, -1e+30)
    probs = low(jax.nn.softmax(scores, axis=-1))
    mixture = low_back(low(jnp.einsum('hqk,khd->qhd', probs, value_rows, precision=HIGH))).reshape(-1, H * DH)
    attention = low_back(jnp.dot(mixture, wo_t.T, precision=HIGH))
    hidden_rows = rows_all + attention
    normed_two = low(rms_scale(hidden_rows, gain_two))
    gate_act = low_back(low(jnp.dot(normed_two, w_gate, precision=HIGH)))
    up_act = low_back(low(jnp.dot(normed_two, w_up, precision=HIGH)))
    activated = low(jax.nn.gelu(gate_act, approximate=True) * up_act)
    ffn_sum = low_back(jnp.dot(activated, w_down_t.T, precision=HIGH))
    result = jnp.where(live_keys[:, None], hidden_rows + ffn_sum, 0.0)
    return (result[:TXT], result[TXT:])

def reference(text_in, patch_in, cot_text, cot_patch, text_count, intersection, text_cell, wq, wk, wv, wo_t, gain_one, w_gate, w_up, w_down_t, gain_two, bias_table):
    weights = tuple((item.astype(jnp.float32) for item in (wq, wk, wv, wo_t, gain_one, w_gate, w_up, w_down_t, gain_two, bias_table)))
    patch_own = jnp.roll(patch_in, PAGES // 2, axis=0).astype(jnp.float32)
    cot_own = jnp.roll(cot_patch, PAGES // 2, axis=0).astype(jnp.float32)

    def forward(text_rows, patch_rows, weight_set):

        def one_page(inputs):
            text_page, patch_page, page_len, page_lists, page_cells = inputs
            return page_layer(weight_set, text_page, patch_page, page_len, page_lists, page_cells)
        return lax.map(jax.checkpoint(one_page), (text_rows, patch_rows, text_count, intersection, text_cell))
    outputs, pullback = jax.vjp(forward, text_in.astype(jnp.float32), patch_own, weights)
    text_back, patch_back, weight_back = pullback((cot_text.astype(jnp.float32), cot_own))
    text_out = outputs[0].astype(jnp.bfloat16)
    patch_out = jnp.roll(outputs[1], -(PAGES // 2), axis=0).astype(jnp.bfloat16)
    patch_grad = jnp.roll(patch_back, -(PAGES // 2), axis=0).astype(jnp.bfloat16)
    return (text_out, patch_out, text_back.astype(jnp.bfloat16), patch_grad, weight_back[0], weight_back[1], weight_back[2], weight_back[3], weight_back[4], weight_back[5], weight_back[6], weight_back[7], weight_back[8], weight_back[9])
```

```python
import functools

import jax
import jax.numpy as jnp
from jax import lax
from jax.experimental import pallas as pl
from jax.experimental.pallas import tpu as pltpu
from jax.sharding import PartitionSpec as P

DH = 64
RB = 32
LQ = 4
GRID = 14
PATCHES = 196
EPS = 1e-06

BQ = 256
PAD = 128
WIN = BQ + 2 * PAD
CELLS = 256
TILE0 = PATCHES
DEAD = 206
QROW0 = PATCHES
FEAT_ROWS = 208
MASKED = -1e30
VMEM = 60 * 1024 * 1024
F32 = jnp.float32
BF16 = jnp.bfloat16


def nt(left, right):
    return lax.dot_general(left, right, (((1,), (1,)), ((), ())), preferred_element_type=F32)


def nn(left, right):
    return lax.dot_general(left, right, (((1,), (0,)), ((), ())), preferred_element_type=F32)


def tn(left, right):
    return lax.dot_general(left, right, (((0,), (0,)), ((), ())), preferred_element_type=F32)


def params(**more):
    return pltpu.CompilerParams(vmem_limit_bytes=VMEM, **more)


def grid_of(devices):
    side = max(1, round((devices / 4) ** 0.5))
    return (devices // (side * side), side, side)


class Chips:
    def __init__(self):
        self.count = lax.axis_size("dp")
        self.sizes = grid_of(self.count)
        self.strides = (self.sizes[1] * self.sizes[2], self.sizes[2], 1)
        me = lax.axis_index("dp")
        self.coords = tuple((me // s) % m for s, m in zip(self.strides, self.sizes))

    def send(self, block, axis, distance):
        size, stride = self.sizes[axis], self.strides[axis]
        route = []
        for i in range(self.count):
            c = (i // stride) % size
            route.append((i, i + ((c + distance) % size - c) * stride))
        return lax.ppermute(block, "dp", route)

    def scatter_axis(self, block, dim, axis):
        size, at = self.sizes[axis], self.coords[axis]
        total = lax.dynamic_index_in_dim(block, at, dim, keepdims=False).astype(F32)
        for k in range(1, size):
            part = lax.dynamic_index_in_dim(block, (at + k) % size, dim, keepdims=False)
            total = total + self.send(part, axis, k).astype(F32)
        return total

    def scatter_rows(self, block):
        rows, columns = block.shape
        z, y, x = self.sizes
        part = block.reshape(z, y, x, rows // self.count, columns)
        half = columns // 256 * 128
        one = self.scatter_axis(part[..., :half], 2, 2).astype(BF16)
        two = self.scatter_axis(part[..., half:], 1, 1).astype(BF16)
        one = self.scatter_axis(one, 1, 1).astype(BF16)
        two = self.scatter_axis(two, 1, 2).astype(BF16)
        return self.scatter_axis(jnp.concatenate([one, two], axis=-1), 0, 0)


def other_core(block):
    return lax.ppermute(block, "mp", [(0, 1), (1, 0)])


def half_way(block):
    count = lax.axis_size("dp")
    route = [(i, (i + count // 2) % count) for i in range(count)]
    rows = block.shape[0] // 2
    core = lax.axis_index("mp")
    mine = lax.ppermute(lax.dynamic_slice_in_dim(block, core * rows, rows, 0), "dp", route)
    theirs = other_core(mine)
    first = core == 0
    return jnp.concatenate([jnp.where(first, mine, theirs), jnp.where(first, theirs, mine)], axis=0)


def attend_kernel(table, q_ref, k_ref, v_ref, cell_ref, cells_ref, lay_ref, mix_ref, prob_ref, keys, layout, near, score):
    pair, block = pl.program_id(0), pl.program_id(1)
    start = block * BQ

    @pl.when(block == 0)
    def _():
        keys[:, :128] = k_ref[...]
        keys[:, 128:] = cells_ref[...]
        gap = lax.broadcasted_iota(jnp.int32, (8, 896), 1) - (BQ + PAD)
        gap = jnp.clip(gap, -(RB // 2), RB // 2 - 1) + RB // 2
        for h in range(2):
            head = pair * 2 + h
            lay = lay_ref[...]
            grid = jnp.zeros(lay.shape, F32)
            for b in range(LQ * LQ):
                grid = jnp.where(lay == b, table[RB + b, head], grid)
            layout[h] = grid.astype(BF16)
            line = jnp.zeros(gap.shape, F32)
            for b in range(RB):
                line = jnp.where(gap == b, table[b, head], line)
            spread = jnp.broadcast_to(line[:1], (BQ, 896))
            spread = pltpu.roll(spread, 0, 1, stride=1, stride_axis=0)
            near[h] = spread[:, BQ : BQ + WIN]

    lane = lax.broadcasted_iota(jnp.int32, (1, 128), 1)
    feature = lax.broadcasted_iota(jnp.int32, (1, CELLS), 1)
    tile = feature - TILE0
    is_tile = (tile >= 0) & (tile < 10)
    left = is_tile & ((tile + 2) * 128 <= start)
    right = is_tile & (tile * 128 >= start + BQ + PAD)
    queries = q_ref[...].astype(F32) * DH ** (-0.5)
    length = k_ref.shape[0]
    mixed = []
    for h in range(2):
        head = pair * 2 + h
        far = jnp.where(left, table[0, head], jnp.where(right, table[RB - 1, head], 0.0))
        far = jnp.where(feature == DEAD, MASKED, far)
        bias = (nn(cell_ref[...], layout[h]) + far).astype(BF16)
        mine = jnp.where((lane // DH) == h, queries, 0.0).astype(BF16)
        score[h, :, PAD : PAD + length] = nt(jnp.concatenate([mine, bias], axis=1), keys[...])
        window = pl.ds(pl.multiple_of(start, 128), WIN)
        score[h, :, window] += near[h]
        scores = score[h, :, PAD : PAD + length]
        top = jnp.max(scores, axis=1, keepdims=True)
        weight = jnp.exp(scores - top)
        total = jnp.sum(weight, axis=1, keepdims=True)
        prob = (weight * (1.0 / total)).astype(BF16)
        prob_ref[h] = prob
        mixed.append(nn(prob, v_ref[...]))
    mix_ref[...] = jnp.where(lane < DH, mixed[0], mixed[1]).astype(BF16)


def attend(table, queries, keys, values, cells, lay):
    rows, width = queries.shape
    pairs, blocks = width // 128, rows // BQ
    pair_spec = pl.BlockSpec((rows, 128), lambda p, b: (0, p))
    block_spec = pl.BlockSpec((BQ, 128), lambda p, b: (b, p))
    return pl.pallas_call(
        attend_kernel,
        grid=(pairs, blocks),
        in_specs=[
            pl.BlockSpec(memory_space=pltpu.SMEM),
            block_spec,
            pair_spec,
            pair_spec,
            pl.BlockSpec((BQ, CELLS), lambda p, b: (b, 0)),
            pl.BlockSpec((rows, CELLS), lambda p, b: (0, 0)),
            pl.BlockSpec((CELLS, CELLS), lambda p, b: (0, 0)),
        ],
        out_specs=[block_spec, pl.BlockSpec((2, BQ, rows), lambda p, b: (p, b, 0))],
        out_shape=[
            jax.ShapeDtypeStruct((rows, width), BF16),
            jax.ShapeDtypeStruct((2 * pairs, rows, rows), BF16),
        ],
        scratch_shapes=[
            pltpu.VMEM((rows, 128 + CELLS), BF16),
            pltpu.VMEM((2, CELLS, CELLS), BF16),
            pltpu.VMEM((2, BQ, WIN), F32),
            pltpu.VMEM((2, BQ, rows + 2 * PAD), F32),
        ],
        compiler_params=params(),
        cost_estimate=pl.CostEstimate(
            flops=2 * 2 * pairs * rows * rows * 512 * 3 // 2,
            bytes_accessed=2 * 2 * pairs * rows * rows,
            transcendentals=2 * pairs * rows * rows,
        ),
        name="attend",
    )(table, queries, keys, values, cells, cells, lay)


def attend_back_kernel(
    q_ref, k_ref, v_ref, gm_ref, mix_ref, prob_ref, cells_ref, cells_t_ref, lay_ref,
    gq_ref, gk_ref, gv_ref, lay_out, far_out, near_out,
    grads, key_acc, value_acc, near_acc,
):
    pair, block = pl.program_id(0), pl.program_id(1)
    start = block * BQ
    length = k_ref.shape[0]

    @pl.when((pair == 0) & (block == 0))
    def _():
        grads[...] = jnp.zeros(grads.shape, BF16)

    @pl.when(block == 0)
    def _():
        key_acc[...] = jnp.zeros(key_acc.shape, F32)
        value_acc[...] = jnp.zeros(value_acc.shape, F32)
        near_acc[...] = jnp.zeros(near_acc.shape, F32)

    lane = lax.broadcasted_iota(jnp.int32, (1, 128), 1)
    grad_mix = gm_ref[...].astype(F32)
    weighted = grad_mix * mix_ref[...].astype(F32)
    queries_t = q_ref[...].astype(F32).T.astype(BF16)
    grad_mix_t = grad_mix.T.astype(BF16)
    found = []
    for h in range(2):
        own = (lane // DH) == h
        mine = jnp.where(own, grad_mix, 0.0).astype(BF16)
        inner = jnp.sum(jnp.where(own, weighted, 0.0), axis=1, keepdims=True)
        grad_prob = nt(mine, v_ref[...])
        prob = prob_ref[h]
        grad_score = (prob.astype(F32) * (grad_prob - inner)).astype(BF16)
        grads[h, :, PAD : PAD + length] = grad_score
        found.append(nn(grad_score, k_ref[...]))
        left = jnp.concatenate([queries_t[h * DH : (h + 1) * DH], cells_t_ref[...]], axis=0)
        key_acc[h] += nn(left, grad_score)
        value_acc[h] += nn(grad_mix_t[h * DH : (h + 1) * DH], prob)
        window = pl.ds(pl.multiple_of(start, 128), WIN)
        near_acc[h] += grads[h, :, window].astype(F32)
    gq_ref[...] = (jnp.where(lane < DH, found[0], found[1]) * DH ** (-0.5)).astype(BF16)

    @pl.when(block == pl.num_programs(1) - 1)
    def _():
        both = jnp.concatenate([key_acc[0, :DH], key_acc[1, :DH]], axis=0)
        gk_ref[...] = (both.T * DH ** (-0.5)).astype(BF16)
        both = jnp.concatenate([value_acc[0], value_acc[1]], axis=0)
        gv_ref[...] = both.T.astype(BF16)
        for h in range(2):
            by_cell = key_acc[h, DH:]
            high = by_cell.astype(BF16)
            low = (by_cell - high.astype(F32)).astype(BF16)
            pairs = nn(high, cells_ref[...]) + nn(low, cells_ref[...])
            lay = lay_ref[:FEAT_ROWS]
            sums = [
                jnp.sum(jnp.where(lay == b, pairs, 0.0), axis=0, keepdims=True)
                for b in range(LQ * LQ)
            ]
            lay_out[h] = jnp.concatenate(sums, axis=0)
            far_out[h] = key_acc[h, DH + QROW0 - 4 :]
            near_out[h] = near_acc[h]


def attend_back(queries, keys, values, grad_mix, mixture, probs, cells, cells_t, lay):
    rows, width = queries.shape
    pairs, blocks = width // 128, rows // BQ
    pair_spec = pl.BlockSpec((rows, 128), lambda p, b: (0, p))
    block_spec = pl.BlockSpec((BQ, 128), lambda p, b: (b, p))
    small = lambda *shape: pl.BlockSpec((2,) + shape, lambda p, b: (p, 0, 0))
    wide = jax.ShapeDtypeStruct((rows, width), BF16)
    return pl.pallas_call(
        attend_back_kernel,
        grid=(pairs, blocks),
        in_specs=[
            block_spec,
            pair_spec,
            pair_spec,
            block_spec,
            block_spec,
            pl.BlockSpec((2, BQ, rows), lambda p, b: (p, b, 0)),
            pl.BlockSpec((rows, CELLS), lambda p, b: (0, 0)),
            pl.BlockSpec((FEAT_ROWS, BQ), lambda p, b: (0, b)),
            pl.BlockSpec((CELLS, CELLS), lambda p, b: (0, 0)),
        ],
        out_specs=[
            block_spec,
            pair_spec,
            pair_spec,
            small(LQ * LQ, CELLS),
            small(FEAT_ROWS - QROW0 + 4, rows),
            small(BQ, WIN),
        ],
        out_shape=[
            wide,
            wide,
            wide,
            jax.ShapeDtypeStruct((2 * pairs, LQ * LQ, CELLS), F32),
            jax.ShapeDtypeStruct((2 * pairs, FEAT_ROWS - QROW0 + 4, rows), F32),
            jax.ShapeDtypeStruct((2 * pairs, BQ, WIN), F32),
        ],
        scratch_shapes=[
            pltpu.VMEM((2, BQ, rows + 2 * PAD), BF16),
            pltpu.VMEM((2, DH + FEAT_ROWS, rows), F32),
            pltpu.VMEM((2, DH, rows), F32),
            pltpu.VMEM((2, BQ, WIN), F32),
        ],
        compiler_params=params(),
        cost_estimate=pl.CostEstimate(
            flops=2 * 2 * pairs * rows * rows * 256 * 4,
            bytes_accessed=2 * 2 * pairs * rows * rows,
            transcendentals=0,
        ),
        name="attend_back",
    )(queries, keys, values, grad_mix, mixture, probs, cells, cells_t, lay)


def table_sums(lay_sums, far_sums, near_sums, rows):
    heads = lay_sums.shape[0]
    lay_part = jnp.sum(lay_sums, axis=-1)
    blocks = rows // BQ
    far = far_sums[:, 4 : 4 + blocks]
    key = jnp.arange(rows)[None, :]
    first = (jnp.arange(blocks) * BQ)[:, None]
    far_left = jnp.sum(jnp.where(key < first - PAD, far, 0.0), axis=(1, 2))
    far_right = jnp.sum(jnp.where(key >= first + BQ + PAD, far, 0.0), axis=(1, 2))
    flat = jnp.pad(near_sums.reshape(heads, BQ * WIN), ((0, 0), (0, BQ)))
    skew = flat.reshape(heads, BQ, WIN + 1)
    middle = jnp.sum(skew[:, :, PAD - RB // 2 + 1 : PAD + RB // 2 - 1], axis=1)
    gap = jnp.arange(WIN)[None, :] - PAD - jnp.arange(BQ)[:, None]
    near_left = jnp.sum(jnp.where(gap <= -(RB // 2), near_sums, 0.0), axis=(1, 2))
    near_right = jnp.sum(jnp.where(gap >= RB // 2 - 1, near_sums, 0.0), axis=(1, 2))
    rel_part = jnp.concatenate(
        [(far_left + near_left)[:, None], middle, (far_right + near_right)[:, None]], axis=1
    )
    return jnp.concatenate([rel_part, lay_part], axis=1).T


def ffn_kernel(first, *refs):
    if first:
        x_ref, g_ref, wg_ref, wu_ref, wd_ref = refs[:5]
        refs = refs[5:]
    else:
        x_ref, g_ref, wg_ref, wu_ref, wd_ref, out_in, grad_in = refs[:7]
        refs = refs[7:]
    out_ref, grad_ref, gate_ref, up_ref, down_ref, gate_acc, up_acc, down_acc = refs
    step = pl.program_id(0)

    @pl.when(step == 0)
    def _():
        for acc in (gate_acc, up_acc, down_acc):
            acc[...] = jnp.zeros(acc.shape, F32)

    rows_in, grad_in_rows = x_ref[...], g_ref[...]
    gate = nn(rows_in, wg_ref[...]).astype(BF16).astype(F32)
    up = nn(rows_in, wu_ref[...]).astype(BF16).astype(F32)
    grad_act = nn(grad_in_rows, wd_ref[...])
    square = gate * gate
    slope = (2 / jnp.pi) ** 0.5
    tanh = jnp.tanh(slope * gate * (1.0 + 0.044715 * square))
    half = 0.5 * (1.0 + tanh)
    value = gate * half
    deriv = half + 0.5 * gate * (1.0 - tanh * tanh) * slope * (1.0 + 3 * 0.044715 * square)
    act = (value * up).astype(BF16)
    grad_gate = (deriv * up * grad_act).astype(BF16)
    grad_up = (value * grad_act).astype(BF16)
    out = nt(act, wd_ref[...])
    grad = nt(grad_gate, wg_ref[...]) + nt(grad_up, wu_ref[...])
    if not first:
        out = out + out_in[...]
        grad = grad + grad_in[...]
    out_ref[...] = out.astype(out_ref.dtype)
    grad_ref[...] = grad.astype(grad_ref.dtype)
    rows_t = rows_in.astype(F32).T.astype(BF16)
    grads_t = grad_in_rows.astype(F32).T.astype(BF16)
    gate_acc[...] += nn(rows_t, grad_gate)
    up_acc[...] += nn(rows_t, grad_up)
    down_acc[...] += nn(grads_t, act)

    @pl.when(step == pl.num_programs(0) - 1)
    def _():
        gate_ref[...] = gate_acc[...].astype(BF16)
        up_ref[...] = up_acc[...].astype(BF16)
        down_ref[...] = down_acc[...].astype(BF16)


def ffn(normed, grad_ffn, w_gate, w_up, w_down, before=None):
    rows, model = normed.shape
    hidden = w_gate.shape[1]
    first = before is None
    row_spec = pl.BlockSpec((BQ, model), lambda r: (r, 0))
    whole = pl.BlockSpec((model, hidden), lambda r: (0, 0))
    kind = F32 if first else BF16
    part = jax.ShapeDtypeStruct((rows, model), kind)
    grad = jax.ShapeDtypeStruct((model, hidden), BF16)
    return pl.pallas_call(
        functools.partial(ffn_kernel, first),
        grid=(rows // BQ,),
        in_specs=[row_spec] * 2 + [whole] * 3 + ([] if first else [row_spec] * 2),
        out_specs=[row_spec] * 2 + [whole] * 3,
        out_shape=[part] * 2 + [grad] * 3,
        scratch_shapes=[pltpu.VMEM((model, hidden), F32)] * 3,
        compiler_params=params(),
        cost_estimate=pl.CostEstimate(
            flops=18 * rows * model * hidden,
            bytes_accessed=12 * model * hidden + 12 * rows * model,
            transcendentals=rows * hidden,
        ),
        name="ffn_first" if first else "ffn_last",
    )(normed, grad_ffn, w_gate, w_up, w_down, *(() if first else before))


def back_kernel(parts, *refs):
    x_ref = refs[0]
    grads = refs[1 : 1 + parts]
    weights = refs[1 + parts : 1 + 2 * parts]
    out_ref = refs[1 + 2 * parts]
    sums = refs[2 + 2 * parts : 2 + 3 * parts]
    accs = refs[2 + 3 * parts :]
    step = pl.program_id(0)

    @pl.when(step == 0)
    def _():
        for acc in accs:
            acc[...] = jnp.zeros(acc.shape, F32)

    rows_t = x_ref[...].astype(F32).T.astype(BF16)
    out = None
    for grad, weight, acc in zip(grads, weights, accs):
        term = nt(grad[...], weight[...])
        out = term if out is None else out + term
        acc[...] += nn(rows_t, grad[...])
    out_ref[...] = out.astype(BF16)

    @pl.when(step == pl.num_programs(0) - 1)
    def _():
        for total, acc in zip(sums, accs):
            total[...] = acc[...].astype(BF16)


def project_back(normed, grads, weights):
    rows, model = normed.shape
    width = weights[0].shape[1]
    parts = len(grads)
    row_spec = pl.BlockSpec((BQ, model), lambda r: (r, 0))
    grad_spec = pl.BlockSpec((BQ, width), lambda r: (r, 0))
    whole = pl.BlockSpec((model, width), lambda r: (0, 0))
    return pl.pallas_call(
        functools.partial(back_kernel, parts),
        grid=(rows // BQ,),
        in_specs=[row_spec] + [grad_spec] * parts + [whole] * parts,
        out_specs=[row_spec] + [whole] * parts,
        out_shape=[jax.ShapeDtypeStruct((rows, model), BF16)]
        + [jax.ShapeDtypeStruct((model, width), BF16)] * parts,
        scratch_shapes=[pltpu.VMEM((model, width), F32)] * parts,
        compiler_params=params(),
        cost_estimate=pl.CostEstimate(
            flops=4 * parts * rows * model * width,
            bytes_accessed=4 * parts * model * width + 4 * rows * model,
            transcendentals=0,
        ),
        name="project_back",
    )(normed, *grads, *weights)


def norm_rows(row_data):
    scale_inv = lax.rsqrt(jnp.mean(row_data * row_data, axis=-1, keepdims=True) + EPS)
    return (row_data * scale_inv, scale_inv)


def norm_back(grad_normed, unit_rows, scale_inv, gain):
    grad_unit = grad_normed * gain
    return scale_inv * (
        grad_unit - unit_rows * jnp.mean(grad_unit * unit_rows, axis=-1, keepdims=True)
    )


def lay_index():
    cell = jnp.arange(CELLS, dtype=jnp.int32)
    row, col = cell // GRID, cell % GRID
    row_gap = jnp.minimum(jnp.abs(row[:, None] - row[None, :]), LQ - 1)
    col_gap = jnp.minimum(jnp.abs(col[:, None] - col[None, :]), LQ - 1)
    real = (cell < PATCHES)[:, None] & (cell < PATCHES)[None, :]
    return jnp.where(real, row_gap * LQ + col_gap, LQ * LQ)


def exact_split(rows):
    high = rows.astype(BF16)
    return high, (rows - high.astype(F32)).astype(BF16)


def body(
    text_in, patch_in, cot_text, cot_patch, text_count, intersection, text_cell,
    wq, wk, wv, wo_t, gain_one, w_gate, w_up, w_down_t, gain_two, bias_table,
):
    chips = Chips()
    me = lax.axis_index("dp")
    text_slots, model = text_in.shape[1:]
    patch_slots = patch_in.shape[1]
    rows_count = text_slots + patch_slots
    width = wq.shape[1]
    hidden = w_gate.shape[1]

    count = lax.dynamic_index_in_dim(text_count, me, 0, keepdims=False)
    place = lax.dynamic_index_in_dim(text_cell, me, 0, keepdims=False)
    slot = jnp.arange(rows_count, dtype=jnp.int32)
    is_text, live = slot < count, slot < count + PATCHES
    pad_text = lambda a: jnp.pad(a, ((0, patch_slots), (0, 0)))
    patch_id = jnp.arange(patch_slots, dtype=jnp.int32)
    covers = jnp.zeros((rows_count, patch_slots), F32)
    for k in range(intersection.shape[1]):
        listed = jnp.pad(intersection[0, k], (0, patch_slots))
        covers = covers + (listed[:, None] == patch_id).astype(F32)
    pick = ((slot - count)[:, None] == patch_id) & (patch_id < PATCHES)
    spread = jnp.where(is_text[:, None] & (patch_id < PATCHES), covers, pick.astype(F32))
    spread = spread.astype(BF16)
    pick = pick.astype(BF16)

    cell = jnp.pad(place[0] * GRID + place[1], (0, patch_slots))
    cell = jnp.where(is_text, cell, slot - count)
    feature = jnp.arange(CELLS, dtype=jnp.int32)
    key_tile = slot // 128 + TILE0
    cells = (live[:, None] & (cell[:, None] == feature) & (feature < PATCHES)).astype(BF16)
    cells = cells + (key_tile[:, None] == feature).astype(BF16)
    cells = cells + (~live[:, None] & (feature == DEAD)).astype(BF16)
    feature = feature[:FEAT_ROWS, None]
    cells_t = (live & (cell == feature) & (feature < PATCHES)) | (slot // BQ + QROW0 == feature)
    cells_t = cells_t.astype(BF16)
    lay = lay_index()
    table = bias_table.astype(F32)

    gather = lambda w: lax.all_gather(w, "dp", axis=0, tiled=True)
    qkv = gather(jnp.concatenate([wq, wk, wv], axis=1))
    wq_all, wk_all, wv_all = qkv[:, :width], qkv[:, width : 2 * width], qkv[:, 2 * width :]
    gains = gather(jnp.stack([gain_one, gain_two], axis=1)).astype(F32)
    gain_first, gain_second = gains[:, 0], gains[:, 1]
    wo_all = gather(wo_t)
    gate_all, up_all, down_all = gather(w_gate), gather(w_up), gather(w_down_t)

    patches = half_way(patch_in[0])
    patch_cot = half_way(cot_patch[0])
    rows = jnp.where(is_text[:, None], pad_text(text_in[0]).astype(F32), 0.0) + nn(spread, patches)
    grad_out = jnp.where(is_text[:, None], pad_text(cot_text[0]).astype(F32), 0.0)
    grad_ffn = (grad_out + nn(pick, patch_cot)).astype(BF16)
    grad_out = grad_ffn.astype(F32)

    unit_one, inv_one = norm_rows(rows)
    normed_one = (unit_one * gain_first).astype(BF16)
    queries = nn(normed_one, wq_all).astype(BF16)
    keys = nn(normed_one, wk_all).astype(BF16)
    values = nn(normed_one, wv_all).astype(BF16)
    mixture, probs = attend(table, queries, keys, values, cells, lay)
    part = nt(mixture, wo_all).astype(BF16)
    hidden_rows = rows + (part.astype(F32) + other_core(part).astype(F32))
    unit_two, inv_two = norm_rows(hidden_rows)
    normed_two = (unit_two * gain_second).astype(BF16)

    cut = (hidden // 256 + 1) // 2 * 256
    ffn_part, grad_part, gate_one, up_one, down_one = ffn(
        normed_two, grad_ffn, gate_all[:, :cut], up_all[:, :cut], down_all[:, :cut]
    )
    ffn_part, grad_part, gate_two, up_two, down_two = ffn(
        normed_two, grad_ffn, gate_all[:, cut:], up_all[:, cut:], down_all[:, cut:],
        (ffn_part, grad_part),
    )
    sum_one = chips.scatter_rows(jnp.concatenate([gate_one, up_one, down_one], axis=1))
    sum_two = chips.scatter_rows(jnp.concatenate([gate_two, up_two, down_two], axis=1))
    one, two = cut, hidden - cut
    join = lambda i: jnp.concatenate(
        [sum_one[:, i * one : (i + 1) * one], sum_two[:, i * two : (i + 1) * two]], axis=1
    )
    gate_sum, up_sum, down_sum = join(0), join(1), join(2)

    normed_grad_two = grad_part.astype(F32) + other_core(grad_part).astype(F32)
    hidden_grad = grad_out + norm_back(normed_grad_two, unit_two, inv_two, gain_second)
    grad_attn = hidden_grad.astype(BF16)
    grad_mix = nn(grad_attn, wo_all).astype(BF16)
    wo_grad = tn(grad_attn, mixture).astype(BF16)
    grad_q, grad_k, grad_v, lay_sums, far_sums, near_sums = attend_back(
        queries, keys, values, grad_mix, mixture, probs, cells, cells_t, lay
    )
    table_sum = lax.psum(table_sums(lay_sums, far_sums, near_sums, rows_count), "dp")
    normed_part, wq_grad, wk_grad, wv_grad = project_back(
        normed_one, (grad_q, grad_k, grad_v), (wq_all, wk_all, wv_all)
    )
    sums = chips.scatter_rows(jnp.concatenate([wq_grad, wk_grad, wv_grad, wo_grad], axis=1))
    wq_sum, wk_sum, wv_sum, wo_sum = (sums[:, i * width : (i + 1) * width] for i in range(4))

    own_first = sum(
        jnp.sum(w.astype(F32) * g, axis=1) for w, g in ((wq, wq_sum), (wk, wk_sum), (wv, wv_sum))
    )
    own_second = sum(jnp.sum(w.astype(F32) * g, axis=1) for w, g in ((w_gate, gate_sum), (w_up, up_sum)))
    own = jnp.stack([own_first, own_second])
    own = (own + other_core(own)) / jnp.stack([gain_one, gain_two]).astype(F32)
    gain_one_sum, gain_two_sum = own[0], own[1]

    normed_grad_one = normed_part.astype(F32) + other_core(normed_part).astype(F32)
    rows_grad = hidden_grad + norm_back(normed_grad_one, unit_one, inv_one, gain_first)
    text_grad = jnp.where(is_text[:, None], rows_grad, 0.0)[:text_slots].astype(BF16)
    high, low = exact_split(rows_grad)
    patch_grad = half_way((tn(spread, high) + tn(spread, low)).astype(BF16))

    ffn_sum = ffn_part.astype(F32) + other_core(ffn_part).astype(F32)
    result = jnp.where(live[:, None], hidden_rows + ffn_sum, 0.0).astype(BF16)
    text_out = jnp.where(is_text[:, None], result, 0)[:text_slots]
    patch_out = half_way(tn(pick, result).astype(BF16))
    return (
        text_out[None], patch_out[None], text_grad[None], patch_grad[None],
        wq_sum, wk_sum, wv_sum, wo_sum, gain_one_sum, gate_sum, up_sum, down_sum, gain_two_sum,
        table_sum,
    )


def solution(mesh):
    page, weight, vector = P("dp", None, None), P("dp", "mp"), P("dp")
    return jax.shard_map(
        body,
        mesh=mesh,
        in_specs=(page,) * 4
        + (P(), page, P())
        + (weight,) * 4
        + (vector,)
        + (weight,) * 3
        + (vector, P(None, "mp")),
        out_specs=(page,) * 4
        + (weight,) * 4
        + (vector,)
        + (weight,) * 3
        + (vector, P(None, "mp")),
        check_vma=False,
    )
```

```python
import functools

import jax
import jax.numpy as jnp
from jax import lax
from jax.experimental import pallas as pl
from jax.experimental.pallas import tpu as pltpu
from jax.sharding import PartitionSpec as P

DH = 64
RB = 32
LQ = 4
GRID = 14
PATCHES = 196
EPS = 1e-06

BQ = 256
PAD = 128
WIN = BQ + 2 * PAD
CELLS = 256
TILE0 = PATCHES
DEAD = 206
FEAT_ROWS = 208
MASKED = -1e30
VMEM = 60 * 1024 * 1024
ATTEND_WEIGHT = 4
ROW_VMEM = 24 * 1024 * 1024
F32 = jnp.float32
BF16 = jnp.bfloat16


def nt(left, right):
    return lax.dot_general(left, right, (((1,), (1,)), ((), ())), preferred_element_type=F32)


def nn(left, right):
    return lax.dot_general(left, right, (((1,), (0,)), ((), ())), preferred_element_type=F32)


def tn(left, right):
    return lax.dot_general(left, right, (((0,), (0,)), ((), ())), preferred_element_type=F32)


def params(**more):
    return pltpu.CompilerParams(vmem_limit_bytes=VMEM, **more)


def grid_of(devices):
    side = max(1, round((devices / 4) ** 0.5))
    return (devices // (side * side), side, side)


class Chips:
    def __init__(self):
        self.count = lax.axis_size("dp")
        self.sizes = grid_of(self.count)
        self.plane = self.sizes[1] * self.sizes[2]
        self.strides = (self.plane, self.sizes[2], 1)
        self.me = lax.axis_index("dp")
        layers = range(self.sizes[0])
        self.planes = [[z * self.plane + i for i in range(self.plane)] for z in layers]
        self.columns = [[z * self.plane + i for z in layers] for i in range(self.plane)]

    def send(self, block, axis, distance):
        size, stride = self.sizes[axis], self.strides[axis]
        route = []
        for i in range(self.count):
            c = (i // stride) % size
            route.append((i, i + ((c + distance) % size - c) * stride))
        return lax.ppermute(block, "dp", route)

    def gather_rows(self, block, fast, cuts, after=(), plane_after=(), aside=None):
        block = tie(block, *after)
        if self.sizes[1:] != (2, 2):
            whole = lax.all_gather(block, "dp", axis=0, tiled=True)
            ends = [sum(cuts[: i + 1]) for i in range(len(cuts))]
            whole = [whole[:, end - cut : end] for cut, end in zip(cuts, ends)]
            return whole, (block,), (block,), (block,)
        half = block.shape[0] // 2
        size = self.sizes[0]
        if fast:
            layers = tuple(self.send(block, 0, k) for k in range(1, size))
            own = jnp.stack((block,) + layers)
        else:
            copies = jnp.concatenate([block] * size)
            own = lax.all_to_all(copies, "dp", 0, 0, axis_index_groups=self.columns, tiled=True)
            own = own.reshape((size,) + block.shape)
            layers = (own,)
        own = tie(own, *plane_after)
        by_x, by_y = self.send(own, 2, 1), self.send(own, 1, 1)
        waits = () if aside is None else aside(layers)
        far_top = self.send(tie(by_y[:, :half], *waits), 2, 1)
        far_low = self.send(by_x[:, half:], 1, 1)
        whole = assemble(self.me, size, fast, cuts, own, by_x, by_y, far_top, far_low)
        return whole, layers, (by_x, by_y), (far_top, far_low)

    def order(self, rows):
        part = rows // self.count
        return [(z * self.plane + i) * part for i in range(self.plane) for z in range(self.sizes[0])]

    def exchange(self, block, groups):
        heard = lax.all_to_all(block, "dp", 0, 0, axis_index_groups=groups, tiled=True)
        count = len(groups[0])
        heard = heard.reshape(count, block.shape[0] // count, block.shape[1])
        total = heard[0].astype(F32)
        for i in range(1, count):
            total = total + heard[i].astype(F32)
        return total


    def trade(self, block, groups):
        count = block.shape[0]
        at = self.me % self.plane if groups is self.planes else self.me // self.plane
        total = lax.dynamic_index_in_dim(block, at, 0, keepdims=False).astype(F32)
        for k in range(1, count):
            part = lax.dynamic_index_in_dim(block, at ^ k, 0, keepdims=False)
            route = [(g[i], g[i ^ k]) for g in groups for i in range(count)]
            total = total + lax.ppermute(part, "dp", route).astype(F32)
        return total


def tie_kernel(*refs):
    pass


def tie(block, *others):
    if not others:
        return block
    anywhere = pl.BlockSpec(memory_space=pl.ANY)
    return pl.pallas_call(
        tie_kernel,
        in_specs=[anywhere] * (1 + len(others)),
        out_specs=anywhere,
        out_shape=jax.ShapeDtypeStruct(block.shape, block.dtype),
        input_output_aliases={0: 0},
        name="tie",
    )(block, *others)


def assemble_kernel(me, own, by_x, by_y, far_top, far_low, *outs):
    y, x = (me[0] // 2) % 2, me[0] % 2
    half = far_top.shape[1]
    start = 0
    for out in outs:
        cols = slice(start, start + out.shape[3])
        start = start + out.shape[3]
        out[0, 2 * y + x] = own[0, :, cols]
        out[0, 2 * y + 1 - x] = by_x[0, :, cols]
        out[0, 2 * (1 - y) + x] = by_y[0, :, cols]
        out[0, 2 * (1 - y) + 1 - x, :half] = far_top[0, :, cols]
        out[0, 2 * (1 - y) + 1 - x, half:] = far_low[0, :, cols]


def assemble(me, layers, turned, cuts, *parts):
    rows, columns = parts[0].shape[1:]
    whole = pl.BlockSpec((1, rows, columns), lambda k, me: (k, 0, 0))
    half = pl.BlockSpec((1, rows // 2, columns), lambda k, me: (k, 0, 0))
    place = lambda k, me: (lax.rem(me[0] // 4 - k + layers, layers) if turned else k, 0, 0, 0)
    outs = pl.pallas_call(
        assemble_kernel,
        grid_spec=pltpu.PrefetchScalarGridSpec(
            num_scalar_prefetch=1,
            grid=(layers,),
            in_specs=[whole] * 3 + [half] * 2,
            out_specs=[pl.BlockSpec((1, 4, rows, cut), place) for cut in cuts],
        ),
        out_shape=[jax.ShapeDtypeStruct((layers, 4, rows, cut), BF16) for cut in cuts],
        compiler_params=params(),
        name="assemble",
    )(me[None].astype(jnp.int32), *parts)
    return [out.reshape(4 * layers * rows, out.shape[3]) for out in outs]


def other_core(block):
    return lax.ppermute(block, "mp", [(0, 1), (1, 0)])


def send_half(block, after=()):
    count = lax.axis_size("dp")
    route = [(i, (i + count // 2) % count) for i in range(count)]
    rows = block.shape[0] // 2
    core = lax.axis_index("mp")
    mine = tie(lax.dynamic_slice_in_dim(block, core * rows, rows, 0), *after)
    return lax.ppermute(mine, "dp", route)


def join_halves(mine):
    theirs = other_core(mine)
    first = lax.axis_index("mp") == 0
    return jnp.concatenate([jnp.where(first, mine, theirs), jnp.where(first, theirs, mine)], axis=0)


def attend_kernel(first, extra, table, q_ref, k_ref, v_ref, cells_ref, lay_ref, *refs):
    mix_ref, prob_ref, inv_ref, keys, values, layout, near, *score = refs[extra:]
    pair = pl.program_id(0) + first
    length = k_ref.shape[0]
    keys[:, :128] = k_ref[...]
    keys[:, 128:] = cells_ref[...]
    values_t = v_ref[...].astype(F32).T.astype(BF16)
    for h in range(2):
        values[h, :DH] = values_t[h * DH : (h + 1) * DH]
        values[h, DH:] = jnp.ones((16, length), BF16)
    gap = WIN - lax.broadcasted_iota(jnp.int32, (8, BQ + WIN), 1) - PAD
    gap = jnp.clip(gap, -(RB // 2), RB // 2 - 1) + RB // 2
    for h in range(2):
        head = pair * 2 + h
        lay = lay_ref[...]
        grid = jnp.zeros(lay.shape, F32)
        for b in range(LQ * LQ):
            grid = jnp.where(lay == b, table[RB + b, head], grid)
        layout[h] = grid.astype(BF16)
        line = jnp.zeros(gap.shape, F32)
        for b in range(RB):
            line = jnp.where(gap == b, table[b, head], line)
        spread = jnp.broadcast_to(line[:1], (WIN, BQ + WIN))
        near[h] = pltpu.roll(spread, 0, 1, stride=1, stride_axis=0)[:, WIN:]

    lane = lax.broadcasted_iota(jnp.int32, (1, 128), 1)
    feature = lax.broadcasted_iota(jnp.int32, (1, CELLS), 1)
    tile = feature - TILE0
    is_tile = (tile >= 0) & (tile < 10)

    def fill(item, buffer):
        block, h = divmod(item, 2)
        start, head = block * BQ, pair * 2 + h
        rows = slice(start, start + BQ)
        left = is_tile & ((tile + 2) * 128 <= start)
        right = is_tile & (tile * 128 >= start + BQ + PAD)
        far = jnp.where(left, table[0, head], jnp.where(right, table[RB - 1, head], 0.0))
        far = jnp.where(feature == DEAD, MASKED, far)
        bias = (nn(cells_ref[rows], layout[h]) + far).astype(BF16)
        mine = jnp.where((lane // DH) == h, q_ref[rows] * DH ** (-0.5), 0.0).astype(BF16)
        buffer[...] = nt(keys[...], jnp.concatenate([mine, bias], axis=1))
        low, high = max(start - PAD, 0), min(start + BQ + PAD, length)
        shift = low - (start - PAD)
        buffer[low:high] += near[h, shift : shift + high - low]

    def use(item, buffer):
        block, h = divmod(item, 2)
        scores = buffer[...]
        top = jnp.max(scores, axis=0, keepdims=True)
        weight = jnp.exp(scores - top).astype(BF16)
        prob_ref[h, block] = weight
        summed = nn(values[h], weight)
        inverse = 1.0 / summed[DH : DH + 1]
        inv_ref[h, :, block * BQ : (block + 1) * BQ] = inverse
        return summed[:DH] * inverse

    items = 2 * (length // BQ)
    depth = len(score)
    for item in range(min(depth - 1, items)):
        fill(item, score[item % depth])
    mixed = []
    for item in range(items):
        if item + depth - 1 < items:
            fill(item + depth - 1, score[(item + depth - 1) % depth])
        mixed.append(use(item, score[item % depth]))
        if item % 2:
            start = item // 2 * BQ
            mix_ref[start : start + BQ] = jnp.concatenate(mixed[-2:], axis=0).T.astype(BF16)


def attend(table, projected, cells, lay, first, pairs, width, into=(), after=()):
    rows = projected.shape[0]
    blocks, all_pairs = rows // BQ, width // 128
    pair_spec = lambda i: pl.BlockSpec((rows, 128), lambda p: (0, i * all_pairs + first + p))
    anywhere = pl.BlockSpec(memory_space=pl.ANY)
    extra = len(into) + len(after)
    return pl.pallas_call(
        functools.partial(attend_kernel, first, extra),
        grid=(pairs,),
        in_specs=[
            pl.BlockSpec(memory_space=pltpu.SMEM),
            pair_spec(0),
            pair_spec(1),
            pair_spec(2),
            pl.BlockSpec((rows, CELLS), lambda p: (0, 0)),
            pl.BlockSpec((CELLS, CELLS), lambda p: (0, 0)),
        ]
        + [anywhere] * extra,
        out_specs=[
            pair_spec(0),
            pl.BlockSpec((2, blocks, rows, BQ), lambda p: (first + p, 0, 0, 0)),
            pl.BlockSpec((2, 1, rows), lambda p: (first + p, 0, 0)),
        ],
        out_shape=[
            jax.ShapeDtypeStruct((rows, width), BF16),
            jax.ShapeDtypeStruct((2 * all_pairs, blocks, rows, BQ), BF16),
            jax.ShapeDtypeStruct((2 * all_pairs, 1, rows), F32),
        ],
        input_output_aliases={6 + i: i for i in range(len(into))},
        scratch_shapes=[
            pltpu.VMEM((rows, 128 + CELLS), BF16),
            pltpu.VMEM((2, DH + 16, rows), BF16),
            pltpu.VMEM((2, CELLS, CELLS), BF16),
            pltpu.VMEM((2, WIN, BQ), F32),
        ]
        + [pltpu.VMEM((rows, BQ), F32)] * 3,
        compiler_params=params(),
        cost_estimate=pl.CostEstimate(
            flops=2 * 2 * pairs * rows * rows * 512 * 3 * ATTEND_WEIGHT,
            bytes_accessed=2 * 2 * pairs * rows * rows,
            transcendentals=2 * pairs * rows * rows,
        ),
        name="attend",
    )(table, projected, projected, projected, cells, lay, *into, *after)


def attend_back_kernel(
    extra, q_ref, k_ref, v_ref, gm_ref, mix_ref, prob_ref, inv_ref, cells_ref, cells_t_ref, lay_ref, *refs
):
    gq_ref, gk_ref, gv_ref, lay_out, rel_out = refs[extra : extra + 5]
    left, queries, grads, query_acc, key_acc, value_acc, by_cell, near_acc, *buffers = refs[extra + 5 :]
    length = k_ref.shape[0]
    blocks = length // BQ
    keys_t = k_ref[...].astype(F32).T.astype(BF16)
    queries[...] = q_ref[...].astype(F32).T.astype(BF16)
    grad_mix = gm_ref[...].astype(F32)
    grad_mix_t = grad_mix.T
    weighted_t = (grad_mix * mix_ref[...].astype(F32)).T
    inner = []
    for h in range(2):
        own = slice(h * DH, (h + 1) * DH)
        left[h, :DH] = keys_t[own]
        left[h, DH:] = cells_t_ref[...]
        inverse = inv_ref[h]
        grads[h] = jnp.zeros(grads.shape[1:], BF16)
        grads[h, own] = (grad_mix_t[own] * inverse).astype(BF16)
        inner.append(jnp.sum(weighted_t[own], axis=0, keepdims=True) * inverse)

    def fill(item, buffer):
        block, h = divmod(item, 2)
        buffer[...] = nn(v_ref[...], grads[h, :, block * BQ : (block + 1) * BQ])

    far_left, far_right = [[], []], [[], []]

    def use(item, buffer):
        block, h = divmod(item, 2)
        start = block * BQ
        cols = slice(start, start + BQ)
        own = slice(h * DH, (h + 1) * DH)
        prob = prob_ref[h, block]
        grad_score = (prob.astype(F32) * (buffer[...] - inner[h][:, cols])).astype(BF16)
        both = nn(left[h], grad_score)
        query_acc[own, cols] = both[:DH]
        by_cell[h, :, cols] = both[DH:].astype(BF16)
        tiles = both[DH + TILE0 : DH + TILE0 + length // 128]
        for t in range(length // 128):
            if (t + 2) * 128 <= start:
                far_left[h].append(tiles[t : t + 1])
            elif t * 128 >= start + BQ + PAD:
                far_right[h].append(tiles[t : t + 1])
        key_part = nt(queries[own, cols], grad_score)
        value_part = nt(grads[h, own, cols], prob)
        low, high = max(start - PAD, 0), min(start + BQ + PAD, length)
        shift = low - (start - PAD)
        part = grad_score[low:high].astype(F32)
        if block == 0:
            key_acc[own] = key_part
            value_acc[own] = value_part
            near_acc[h, :shift] = jnp.zeros((shift, BQ), F32)
            near_acc[h, shift : shift + high - low] = part
        else:
            key_acc[own] += key_part
            value_acc[own] += value_part
            near_acc[h, shift : shift + high - low] += part

    items = 2 * blocks
    depth = len(buffers)
    for item in range(min(depth - 1, items)):
        fill(item, buffers[item % depth])
    for item in range(items):
        if item + depth - 1 < items:
            fill(item + depth - 1, buffers[(item + depth - 1) % depth])
        use(item, buffers[item % depth])

    gq_ref[...] = (query_acc[...].T * DH ** (-0.5)).astype(BF16)
    gk_ref[...] = (key_acc[...].T * DH ** (-0.5)).astype(BF16)
    gv_ref[...] = value_acc[...].T.astype(BF16)
    turn = lax.broadcasted_iota(jnp.int32, (BQ, BQ), 0) + lax.broadcasted_iota(jnp.int32, (BQ, BQ), 1)
    turn = (turn == BQ - 1).astype(BF16)
    column = lax.broadcasted_iota(jnp.int32, (1, BQ + WIN), 1)
    lay = lay_ref[:FEAT_ROWS]
    for h in range(2):
        pairs = nn(by_cell[h], cells_ref[...])
        sums = [
            jnp.sum(jnp.where(lay == b, pairs, 0.0), axis=0, keepdims=True) for b in range(LQ * LQ)
        ]
        lay_out[h] = jnp.concatenate(sums, axis=0)
        band = near_acc[h]
        high = band.astype(BF16)
        low = (band - high.astype(F32)).astype(BF16)
        band = nn(high, turn) + nn(low, turn)
        band = jnp.concatenate([band, jnp.zeros((WIN, WIN), F32)], axis=1)
        band = pltpu.roll(band, 0, 1, stride=1, stride_axis=0)
        rel = jnp.sum(band, axis=0, keepdims=True)
        rel = rel + jnp.where(column == 0, jnp.sum(sum(far_left[h]), axis=1, keepdims=True), 0.0)
        last = column == BQ + WIN - 1
        rel_out[h] = rel + jnp.where(last, jnp.sum(sum(far_right[h]), axis=1, keepdims=True), 0.0)


def attend_back(projected, grad_mix, mixture, probs, inverse, cells, cells_t, lay, first, pairs, after=()):
    rows, width = grad_mix.shape
    blocks, all_pairs = rows // BQ, width // 128
    pair_spec = lambda i: pl.BlockSpec((rows, 128), lambda p: (0, i * all_pairs + first + p))
    out_spec = pl.BlockSpec((rows, 128), lambda p: (0, p))
    small = lambda *shape: pl.BlockSpec((2,) + shape, lambda p: (p, 0, 0))
    whole = lambda *shape: pl.BlockSpec(shape, lambda p: (0, 0))
    wide = jax.ShapeDtypeStruct((rows, 128 * pairs), BF16)
    return pl.pallas_call(
        functools.partial(attend_back_kernel, len(after)),
        grid=(pairs,),
        in_specs=[pair_spec(0), pair_spec(1), pair_spec(2), pair_spec(0), pair_spec(0)]
        + [
            pl.BlockSpec((2, blocks, rows, BQ), lambda p: (first + p, 0, 0, 0)),
            pl.BlockSpec((2, 1, rows), lambda p: (first + p, 0, 0)),
            whole(rows, CELLS),
            whole(FEAT_ROWS, rows),
            whole(CELLS, CELLS),
        ]
        + [pl.BlockSpec(memory_space=pl.ANY)] * len(after),
        out_specs=[out_spec] * 3 + [small(LQ * LQ, CELLS), small(1, BQ + WIN)],
        out_shape=[
            wide,
            wide,
            wide,
            jax.ShapeDtypeStruct((2 * pairs, LQ * LQ, CELLS), F32),
            jax.ShapeDtypeStruct((2 * pairs, 1, BQ + WIN), F32),
        ],
        scratch_shapes=[
            pltpu.VMEM((2, DH + FEAT_ROWS, rows), BF16),
            pltpu.VMEM((128, rows), BF16),
            pltpu.VMEM((2, 128, rows), BF16),
            pltpu.VMEM((128, rows), F32),
            pltpu.VMEM((128, rows), F32),
            pltpu.VMEM((128, rows), F32),
            pltpu.VMEM((2, FEAT_ROWS, rows), BF16),
            pltpu.VMEM((2, WIN, BQ), F32),
        ]
        + [pltpu.VMEM((rows, BQ), F32)] * 3,
        compiler_params=params(),
        cost_estimate=pl.CostEstimate(
            flops=2 * 2 * pairs * rows * rows * 256 * 4,
            bytes_accessed=2 * 2 * pairs * rows * rows,
            transcendentals=0,
        ),
        name="attend_back",
    )(projected, projected, projected, grad_mix, mixture, probs, inverse, cells, cells_t, lay, *after)


def table_sums(lay_sums, rel_sums):
    gap = jnp.arange(BQ + WIN) - (BQ - 1 + PAD)
    bucket = jnp.clip(gap, -(RB // 2), RB // 2 - 1) + RB // 2
    onehot = (bucket[:, None] == jnp.arange(RB)).astype(F32)
    rel = jnp.einsum("hn,nb->bh", rel_sums[:, 0], onehot, precision=lax.Precision.HIGHEST)
    return jnp.concatenate([rel, jnp.sum(lay_sums, axis=-1).T], axis=0)


def ffn_kernel(first, extra, base, hidden, order, x_in, g_in, w_in, *refs):
    if not first:
        out_in, grad_in = refs[:2]
    refs = refs[extra:]
    out_to, grad_to, sums_to = refs[:3]
    x, g, w, rows_t, grads_t, act_all, gate_all, up_all, out, grad, sums = refs[3:14]
    sems, sum_sems = refs[14:16]
    total, model = x.shape
    weight = lambda i: w_in.at[:, base + i * hidden : base + (i + 1) * hidden]
    copy = pltpu.make_async_copy
    loads = [
        copy(x_in, x, sems.at[0]),
        copy(weight(0), w.at[0], sems.at[1]),
        copy(weight(1), w.at[1], sems.at[2]),
        copy(g_in, g, sems.at[3]),
        copy(weight(2), w.at[2], sems.at[4]),
    ]
    if not first:
        out_old, grad_old = refs[16:18]
        loads += [copy(out_in, out_old, sems.at[5]), copy(grad_in, grad_old, sems.at[6])]
    for load in loads:
        load.start()
    loads[0].wait()
    rows_t[...] = x[...].astype(F32).T.astype(BF16)
    for load in loads[1:4]:
        load.wait()
    grads_t[...] = g[...].astype(F32).T.astype(BF16)
    for load in loads[4:]:
        load.wait()
    slope = (2 / jnp.pi) ** 0.5
    for cut in range(2):
        rows = slice(cut * (total // 2), (cut + 1) * (total // 2))
        gate = nn(x[rows], w[0]).astype(BF16).astype(F32)
        up = nn(x[rows], w[1]).astype(BF16).astype(F32)
        grad_act = nn(g[rows], w[2])
        square = gate * gate
        tanh = jnp.tanh(gate * (slope + slope * 0.044715 * square))
        half = 0.5 + 0.5 * tanh
        value = gate * half
        deriv = half + (0.5 * gate) * (1.0 - tanh * tanh) * (slope + 3 * 0.044715 * slope * square)
        act_all[rows] = (value * up).astype(BF16)
        gate_all[rows] = (deriv * up * grad_act).astype(BF16)
        up_all[rows] = (value * grad_act).astype(BF16)
    for cut in range(2):
        rows = slice(cut * (total // 2), (cut + 1) * (total // 2))
        out_part = nt(act_all[rows], w[2])
        grad_part = nt(gate_all[rows], w[0]) + nt(up_all[rows], w[1])
        if not first:
            out_part = out_part + out_old[rows].astype(F32)
            grad_part = grad_part + grad_old[rows].astype(F32)
        out[rows] = out_part.astype(BF16)
        grad[rows] = grad_part.astype(BF16)
    stores = [copy(grad, grad_to, sems.at[0]), copy(out, out_to, sems.at[1])]
    for store in stores:
        store.start()
    part = model // len(order)
    for i, (left, right) in enumerate(((rows_t, gate_all), (rows_t, up_all), (grads_t, act_all))):
        sums[i] = nn(left[...], right[...]).astype(BF16)
        for k, row in enumerate(order):
            store = copy(
                sums.at[i, row : row + part],
                sums_to.at[k * part : (k + 1) * part, i * hidden : (i + 1) * hidden],
                sum_sems.at[i, k],
            )
            store.start()
            stores.append(store)
    for store in stores:
        store.wait()


def ffn(normed, grad_ffn, weights, base, hidden, order, before=()):
    rows, model = normed.shape
    first = not before
    extra = len(before)
    anywhere = pl.BlockSpec(memory_space=pl.ANY)
    part = jax.ShapeDtypeStruct((rows, model), BF16)
    vmem = lambda *shape: pltpu.VMEM(shape, BF16)
    return pl.pallas_call(
        functools.partial(ffn_kernel, first, extra, base, hidden, order),
        in_specs=[anywhere] * (3 + extra),
        out_specs=[anywhere] * 3,
        out_shape=[part, part, jax.ShapeDtypeStruct((model, 3 * hidden), BF16)],
        scratch_shapes=[vmem(rows, model)] * 2
        + [vmem(3, model, hidden)]
        + [vmem(model, rows)] * 2
        + [vmem(rows, hidden)] * 3
        + [vmem(rows, model)] * 2
        + [vmem(3, model, hidden)]
        + [pltpu.SemaphoreType.DMA((7,)), pltpu.SemaphoreType.DMA((3, len(order)))]
        + ([] if first else [vmem(rows, model)] * 2),
        compiler_params=params(),
        cost_estimate=pl.CostEstimate(
            flops=18 * rows * model * hidden,
            bytes_accessed=12 * model * hidden + 8 * rows * model,
            transcendentals=rows * hidden,
        ),
        name="ffn_first" if first else "ffn_last",
    )(normed, grad_ffn, weights, *before)


def back_kernel(order, kind, rows_t, *refs):
    grads = jnp.concatenate([r[...] for r in refs[:3]], axis=1)
    weights = jnp.concatenate([r[...] for r in refs[3:6]], axis=1)
    if kind == "first":
        carry, (out_ref, sums) = refs[6], refs[-2:]
        out = nt(grads, weights)
    else:
        before, table, (out_ref, sums) = *refs[6:8], refs[-2:]
        out = nt(grads, weights) + before[...].astype(F32)
    out_ref[...] = out.astype(BF16)
    found = nn(rows_t[...], grads).astype(BF16)
    model, width = found.shape
    part = model // len(order)
    chunk = model // sums.shape[0]
    for k, start in enumerate(order):
        place, at = divmod(k * part, chunk)
        sums[place, at : at + part, :width] = found[start : start + part]
        if kind == "first":
            sums[place, at : at + part, width:] = carry[k * part : (k + 1) * part]
    if kind != "first":
        for place in range(sums.shape[0]):
            sums[place, chunk:] = table[...]


def project_back(rows_t, grads, weights, width, first, order, plane, carry=None, before=None, table=None, after=()):
    model, rows = rows_t.shape
    half = grads[0].shape[1]
    whole = lambda *shape: pl.BlockSpec(shape, lambda j: (0,) * len(shape), pipeline_mode=pl.Buffered(1))
    at = lambda i: pl.BlockSpec((model, half), lambda j: (0, (i * width + first) // half))
    kind = "first" if before is None else "last"
    if kind == "first":
        more, shape = (carry,), (plane, model // plane, 3 * half + carry.shape[1])
    else:
        more, shape = (before, table), (plane, model // plane + table.shape[0], 3 * half)
    return pl.pallas_call(
        functools.partial(back_kernel, order, kind),
        grid=(1,),
        in_specs=[whole(model, rows)]
        + [whole(rows, half)] * 3
        + [at(0), at(1), at(2)]
        + [whole(*m.shape) for m in more]
        + [pl.BlockSpec(memory_space=pl.ANY)] * len(after),
        out_specs=[whole(rows, model), whole(*shape)],
        out_shape=[jax.ShapeDtypeStruct((rows, model), BF16), jax.ShapeDtypeStruct(shape, BF16)],
        compiler_params=params(),
        cost_estimate=pl.CostEstimate(
            flops=12 * rows * model * half,
            bytes_accessed=12 * model * half + 4 * rows * model,
            transcendentals=0,
        ),
        name="project_back",
    )(rows_t, *grads, weights, weights, weights, *more, *after)


def rows_spec(columns, limit=None):
    if limit is None:
        return pl.BlockSpec((BQ, columns), lambda r: (r, 0))
    return pl.BlockSpec((BQ, columns), lambda r: (jnp.minimum(r, limit // BQ - 1), 0))


def fixed_spec(*shape):
    return pl.BlockSpec(shape, lambda r: (0,) * len(shape))


SCALAR = pl.BlockSpec(memory_space=pltpu.SMEM)


def is_text(count):
    row = lax.broadcasted_iota(jnp.int32, (BQ, 1), 0) + pl.program_id(0) * BQ
    return row < count[0]


def row_call(kernel, name, rows, in_specs, out, scratch, flops, *operands):
    out_specs, out_shape = zip(*out)
    return pl.pallas_call(
        kernel,
        grid=(rows // BQ,),
        in_specs=in_specs,
        out_specs=out_specs,
        out_shape=[jax.ShapeDtypeStruct(*o) for o in out_shape],
        scratch_shapes=scratch,
        compiler_params=pltpu.CompilerParams(vmem_limit_bytes=ROW_VMEM),
        cost_estimate=pl.CostEstimate(flops=flops, bytes_accessed=20 * rows * 1024, transcendentals=0),
        name=name,
    )(*operands)


def embed_kernel(count, text, spread, patches, rows):
    own = jnp.where(is_text(count), text[...].astype(F32), 0.0)
    rows[...] = (own + nn(spread[...], patches[...])).astype(rows.dtype)


def embed(count, text, spread, patches, kind=F32):
    rows, slots = spread.shape
    texts, model = text.shape
    return row_call(
        embed_kernel, "embed", rows,
        [SCALAR, rows_spec(model, texts), rows_spec(slots), fixed_spec(slots, model)],
        [(rows_spec(model), ((rows, model), kind))],
        [], 2 * rows * slots * model, count, text, spread, patches,
    )[0]


def norm(rows):
    inv = lax.rsqrt(jnp.mean(rows * rows, axis=1, keepdims=True) + EPS)
    return rows * inv, inv


def norm_back(grad_normed, rows, gain):
    unit, inv = norm(rows)
    grad_unit = grad_normed * gain
    return inv * (grad_unit - unit * jnp.mean(grad_unit * unit, axis=1, keepdims=True))


def project_kernel(rows, weights, projected, normed_t, gains):
    width = projected.shape[1]

    @pl.when(pl.program_id(0) == 0)
    def _():
        gains[...] = weights[:, width:].astype(F32).T[:8]

    normed = norm(rows[...])[0] * gains[:1]
    normed_t[...] = normed.T.astype(BF16)
    projected[...] = nn(normed.astype(BF16), weights[:, :width]).astype(BF16)


def project(rows, weights):
    count, model = rows.shape
    width = weights.shape[1] - 128
    return row_call(
        project_kernel, "project", count,
        [rows_spec(model), pl.BlockSpec(weights.shape, lambda r: (0, 0), pipeline_mode=pl.Buffered(1))],
        [
            (rows_spec(width), ((count, width), BF16)),
            (pl.BlockSpec((model, BQ), lambda r: (0, r)), ((model, count), BF16)),
            (fixed_spec(8, model), ((8, model), F32)),
        ],
        [], 2 * count * model * width, rows, weights,
    )


def mix_out_kernel(mixture, weight, out):
    out[...] = nt(mixture[...], weight[...]).astype(BF16)


def mix_out(mixture, weights):
    rows, width = mixture.shape
    model = weights.shape[0]
    return row_call(
        mix_out_kernel, "mix_out", rows,
        [rows_spec(width), fixed_spec(model, width)],
        [(rows_spec(model), ((rows, model), BF16))],
        [], 2 * rows * model * width, mixture, weights,
    )[0]


def middle_kernel(rows, own, other, gains, hidden, normed):
    total = rows[...] + (own[...].astype(F32) + other[...].astype(F32))
    hidden[...] = total
    normed[...] = (norm(total)[0] * gains[1:2]).astype(BF16)


def middle(rows, own, other, gains):
    count, model = rows.shape
    return row_call(
        middle_kernel, "middle", count,
        [rows_spec(model)] * 3 + [fixed_spec(8, model)],
        [(rows_spec(model), ((count, model), F32)), (rows_spec(model), ((count, model), BF16))],
        [], 0, rows, own, other, gains,
    )


def after_kernel(order, hidden, own, other, grad_out, gains, weight, mixture, *refs):
    grad_attn, grad_mix, sums, acc = refs[-4:]
    step = pl.program_id(0)

    @pl.when(step == 0)
    def _():
        acc[...] = jnp.zeros(acc.shape, F32)

    grad = own[...].astype(F32) + other[...].astype(F32)
    grad = grad_out[...].astype(F32) + norm_back(grad, hidden[...], gains[1:2])
    low = grad.astype(BF16)
    grad_attn[...] = low
    grad_mix[...] = nn(low, weight[...]).astype(BF16)
    acc[...] += nn(grad.T.astype(BF16), mixture[...])

    @pl.when(step == pl.num_programs(0) - 1)
    def _():
        part = acc.shape[0] // len(order)
        for k, start in enumerate(order):
            sums[k * part : (k + 1) * part] = acc[start : start + part].astype(BF16)


def after_ffn(hidden, own, other, grad_out, gains, weights, mixture, order, after=()):
    rows, model = hidden.shape
    width = mixture.shape[1]
    return row_call(
        functools.partial(after_kernel, order), "after_ffn", rows,
        [rows_spec(model)] * 4
        + [fixed_spec(8, model), fixed_spec(model, width), rows_spec(width)]
        + [pl.BlockSpec(memory_space=pl.ANY)] * len(after),
        [
            (rows_spec(model), ((rows, model), BF16)),
            (rows_spec(width), ((rows, width), BF16)),
            (fixed_spec(model, width), ((model, width), BF16)),
        ],
        [pltpu.VMEM((model, width), F32)], 4 * rows * model * width,
        hidden, own, other, grad_out, gains, weights, mixture, *after,
    )


def last_kernel(count, rows, own, other, grad, gains, spread, *refs):
    text_grad, patch_grad, acc = refs[-3:]
    step = pl.program_id(0)

    @pl.when(step == 0)
    def _():
        acc[...] = jnp.zeros(acc.shape, F32)

    total = own[...].astype(F32) + other[...].astype(F32)
    total = grad[...].astype(F32) + norm_back(total, rows[...], gains[:1])

    @pl.when(step < pl.num_programs(0) - 1)
    def _():
        text_grad[...] = jnp.where(is_text(count), total, 0.0).astype(BF16)

    high = total.astype(BF16)
    low = (total - high.astype(F32)).astype(BF16)
    places = spread[...].astype(F32).T.astype(BF16)
    acc[...] += nn(places, high) + nn(places, low)

    @pl.when(step == pl.num_programs(0) - 1)
    def _():
        patch_grad[...] = acc[...].astype(BF16)


def last(count, rows, own, other, grad, gains, spread, texts, after=()):
    length, model = rows.shape
    slots = spread.shape[1]
    return row_call(
        last_kernel, "last", length,
        [SCALAR] + [rows_spec(model)] * 4 + [fixed_spec(8, model), rows_spec(slots)]
        + [pl.BlockSpec(memory_space=pl.ANY)] * len(after),
        [(rows_spec(model, texts), ((texts, model), BF16)), (fixed_spec(slots, model), ((slots, model), BF16))],
        [pltpu.VMEM((slots, model), F32)], 4 * length * model * slots,
        count, rows, own, other, grad, gains, spread, *after,
    )


def result_kernel(count, hidden, own, other, pick, *refs):
    text_out, patch_out, acc = refs[-3:]
    step = pl.program_id(0)

    @pl.when(step == 0)
    def _():
        acc[...] = jnp.zeros(acc.shape, F32)

    total = hidden[...] + (own[...].astype(F32) + other[...].astype(F32))

    @pl.when(step < pl.num_programs(0) - 1)
    def _():
        text_out[...] = jnp.where(is_text(count), total, 0.0).astype(BF16)

    acc[...] += nn(pick[...].astype(F32).T.astype(BF16), total.astype(BF16))

    @pl.when(step == pl.num_programs(0) - 1)
    def _():
        patch_out[...] = acc[...].astype(BF16)


def result(count, hidden, own, other, pick, texts, after=()):
    length, model = hidden.shape
    slots = pick.shape[1]
    return row_call(
        result_kernel, "result", length,
        [SCALAR] + [rows_spec(model)] * 3 + [rows_spec(slots)]
        + [pl.BlockSpec(memory_space=pl.ANY)] * len(after),
        [(rows_spec(model, texts), ((texts, model), BF16)), (fixed_spec(slots, model), ((slots, model), BF16))],
        [pltpu.VMEM((slots, model), F32)], 2 * length * model * slots,
        count, hidden, own, other, pick, *after,
    )


def lay_index():
    cell = jnp.arange(CELLS, dtype=jnp.int32)
    row, col = cell // GRID, cell % GRID
    row_gap = jnp.minimum(jnp.abs(row[:, None] - row[None, :]), LQ - 1)
    col_gap = jnp.minimum(jnp.abs(col[:, None] - col[None, :]), LQ - 1)
    real = (cell < PATCHES)[:, None] & (cell < PATCHES)[None, :]
    return jnp.where(real, row_gap * LQ + col_gap, LQ * LQ)


def body(
    text_in, patch_in, cot_text, cot_patch, text_count, intersection, text_cell,
    wq, wk, wv, wo_t, gain_one, w_gate, w_up, w_down_t, gain_two, bias_table,
):
    chips = Chips()
    me = lax.axis_index("dp")
    text_slots, model = text_in.shape[1:]
    patch_slots = patch_in.shape[1]
    rows_count = text_slots + patch_slots
    live_slots = (PATCHES + 15) // 16 * 16
    width = wq.shape[1]
    hidden = w_gate.shape[1]

    count = lax.dynamic_slice_in_dim(text_count, me, 1, 0)
    place = lax.dynamic_index_in_dim(text_cell, me, 0, keepdims=False)
    slot = jnp.arange(rows_count, dtype=jnp.int32)
    is_text, live = slot < count, slot < count + PATCHES
    patch_id = jnp.arange(live_slots, dtype=jnp.int32)
    covers = jnp.zeros((rows_count, live_slots), F32)
    for k in range(intersection.shape[1]):
        listed = jnp.pad(intersection[0, k], (0, patch_slots))
        covers = covers + (listed[:, None] == patch_id).astype(F32)
    pick = ((slot - count)[:, None] == patch_id) & (patch_id < PATCHES)
    spread = jnp.where(is_text[:, None] & (patch_id < PATCHES), covers, pick.astype(F32))
    spread = spread.astype(BF16)
    pick = pick.astype(BF16)

    cell = jnp.pad(place[0] * GRID + place[1], (0, patch_slots))
    cell = jnp.where(is_text, cell, slot - count)
    feature = jnp.arange(CELLS, dtype=jnp.int32)
    key_tile = slot // 128 + TILE0
    cells = (live[:, None] & (cell[:, None] == feature) & (feature < PATCHES)).astype(BF16)
    cells = cells + (key_tile[:, None] == feature).astype(BF16)
    cells = cells + (~live[:, None] & (feature == DEAD)).astype(BF16)
    feature = feature[:FEAT_ROWS, None]
    cells_t = (live & (cell == feature) & (feature < PATCHES)) | (key_tile == feature)
    cells_t = cells_t.astype(BF16)
    lay = lay_index()
    table = bias_table.astype(F32)

    cut = hidden // 3 // 256 * 256 + 256
    gains = jnp.pad(jnp.stack([gain_one, gain_two], axis=1), ((0, 0), (0, 126)))
    sent = []
    (qkv,), layers, planes, corners = chips.gather_rows(
        jnp.concatenate([wq, wk, wv, gains], axis=1), True, (3 * width + 128,),
        aside=lambda layers: (sent.append(send_half(patch_in[0, :live_slots], layers)), sent[0])[1:],
    )
    sent = sent or [send_half(patch_in[0, :live_slots])]
    patches = join_halves(sent[0])
    (wo_all, first_set), layers, planes, _ = chips.gather_rows(
        jnp.concatenate([wo_t, w_gate[:, :cut], w_up[:, :cut], w_down_t[:, :cut]], axis=1),
        True, (width, 3 * cut), planes, corners,
    )
    patch_cot = join_halves(send_half(cot_patch[0, :live_slots], layers))
    last_set = lax.all_gather(
        tie(jnp.concatenate([w_gate[:, cut:], w_up[:, cut:], w_down_t[:, cut:]], axis=1), *corners),
        "dp", axis=0, tiled=True,
    )
    rows = embed(count, text_in[0], spread, patches)
    grad_ffn = embed(count, cot_text[0], pick, patch_cot, BF16)

    projected, normed_t, gains = project(rows, qkv)
    half = width // 256
    seen = attend(table, projected, cells, lay, 0, half, width)
    mixture, probs, inverse = attend(table, projected, cells, lay, half, half, width, seen, (*planes, patch_cot))
    part = mix_out(mixture, wo_all)
    hidden_rows, normed_two = middle(rows, part, other_core(part), gains)

    order = chips.order(model)
    ffn_part, grad_part, grads_one = ffn(normed_two, grad_ffn, first_set, 0, cut, order)
    ffn_part, grad_part, grads_two = ffn(
        normed_two, grad_ffn, last_set, 0, hidden - cut, order, (ffn_part, grad_part)
    )
    scatter = lambda a, groups: lax.psum_scatter(
        a, "dp", scatter_dimension=0, axis_index_groups=groups, tiled=True
    )
    sum_one, sum_two = scatter(grads_one, chips.planes), scatter(grads_two, chips.planes)
    grad_attn, grad_mix, wo_grad = after_ffn(
        hidden_rows, grad_part, other_core(grad_part), grad_ffn, gains, wo_all, mixture, order
    )
    sum_one = chips.exchange(tie(sum_one, grad_mix), chips.columns)
    args = (projected, grad_mix, mixture, probs, inverse, cells, cells_t, lay)
    *grads_a, lay_a, rel_a = attend_back(*args, 0, half)
    normed_a, grads_a = project_back(
        normed_t, grads_a, qkv, width, 0, order, chips.plane, carry=wo_grad, after=(sum_one,)
    )
    sum_a = chips.exchange(grads_a.reshape(model, -1), chips.planes).astype(BF16)
    *grads_b, lay_b, rel_b = attend_back(*args, half, half, (normed_a,))
    table_part = table_sums(jnp.concatenate([lay_a, lay_b]), jnp.concatenate([rel_a, rel_b]))
    normed_part, grads_b = project_back(
        normed_t, grads_b, qkv, width, width // 2, order, chips.plane,
        before=normed_a, table=wide_row(table_part, 3 * width // 2),
    )
    sum_two = scatter(tie(jnp.concatenate([sum_two, sum_a], axis=1), normed_part), chips.columns).astype(F32)
    sum_a = sum_two[:, 3 * (hidden - cut) :]
    ffn_other = other_core(ffn_part)
    text_grad, patch_grad = last(
        count, rows, normed_part, other_core(normed_part), grad_attn, gains, spread, text_slots
    )
    text_out, patch_out = result(
        count, hidden_rows, ffn_part, ffn_other, pick, text_slots, (normed_part,)
    )
    sum_b = chips.trade(grads_b, chips.planes)
    chunk = model // chips.plane
    table_row = wide_row(narrow_row(sum_b[chunk], table.shape), sum_b.shape[1])
    layers = chips.sizes[0]
    sum_b = sum_b[:chunk].astype(BF16).reshape(layers, chunk // layers, -1)
    sum_b = jnp.concatenate([sum_b, jnp.broadcast_to(table_row, (layers,) + table_row.shape)], axis=1)
    sum_b = chips.trade(tie(sum_b, patch_grad, patch_out), chips.columns)
    sum_b, table_sum = sum_b[: chunk // layers], narrow_row(sum_b[chunk // layers], table.shape)
    fill = lambda a: jnp.pad(a, ((0, patch_slots - live_slots), (0, 0)))
    back = fill(join_halves(send_half(jnp.concatenate([patch_out, patch_grad], axis=1))))
    patch_out, patch_grad = back[:, :model], back[:, model:]

    rest = hidden - cut
    join = lambda i: jnp.concatenate(
        [
            sum_one[:, i * cut : (i + 1) * cut], sum_two[:, i * rest : (i + 1) * rest],
        ],
        axis=1,
    )
    gate_sum, up_sum, down_sum = join(0), join(1), join(2)
    cols = width // 2
    wq_sum, wk_sum, wv_sum = (
        jnp.concatenate([a[:, i * cols : (i + 1) * cols] for a in (sum_a, sum_b)], axis=1)
        for i in range(3)
    )
    wo_sum = sum_a[:, 3 * cols :]

    own_first = sum(
        jnp.sum(w.astype(F32) * g, axis=1) for w, g in ((wq, wq_sum), (wk, wk_sum), (wv, wv_sum))
    )
    own_second = sum(jnp.sum(w.astype(F32) * g, axis=1) for w, g in ((w_gate, gate_sum), (w_up, up_sum)))
    own = jnp.stack([own_first, own_second])
    own = (own + other_core(own)) / jnp.stack([gain_one, gain_two]).astype(F32)
    return (
        text_out[None], patch_out[None], text_grad[None], patch_grad[None],
        wq_sum, wk_sum, wv_sum, wo_sum, own[0], gate_sum, up_sum, down_sum, own[1],
        table_sum,
    )


def wide_row(values, columns):
    flat = values.reshape(-1)
    high = flat.astype(BF16)
    low = (flat - high.astype(F32)).astype(BF16)
    both = jnp.concatenate([high, low])
    return jnp.pad(both[None], ((0, 15), (0, columns - both.shape[0])))


def narrow_row(row, shape):
    size = shape[0] * shape[1]
    return (row[:size] + row[size : 2 * size]).reshape(shape)


def solution(mesh):
    page, weight, vector = P("dp", None, None), P("dp", "mp"), P("dp")
    return jax.shard_map(
        body,
        mesh=mesh,
        in_specs=(page,) * 4
        + (P(), page, P())
        + (weight,) * 4
        + (vector,)
        + (weight,) * 3
        + (vector, P(None, "mp")),
        out_specs=(page,) * 4
        + (weight,) * 4
        + (vector,)
        + (weight,) * 3
        + (vector, P(None, "mp")),
        check_vma=False,
    )
```

```python
import functools

import jax
import jax.numpy as jnp
from jax import lax
from jax.experimental import pallas as pl
from jax.experimental.pallas import tpu as pltpu
from jax.sharding import PartitionSpec as P

DH = 64
RB = 32
LQ = 4
GRID = 14
PATCHES = 196
EPS = 1e-06

BQ = 256
PAD = 128
WIN = BQ + 2 * PAD
CELLS = 256
TILE0 = PATCHES
DEAD = 206
FEAT_ROWS = 208
MASKED = -1e30
ATTEND_WEIGHT = 4
STREAMED = ("after_ffn", "result", "last")
F32 = jnp.float32
BF16 = jnp.bfloat16


def nt(left, right):
    return lax.dot_general(left, right, (((1,), (1,)), ((), ())), preferred_element_type=F32)


def nn(left, right):
    return lax.dot_general(left, right, (((1,), (0,)), ((), ())), preferred_element_type=F32)


def tn(left, right):
    return lax.dot_general(left, right, (((0,), (0,)), ((), ())), preferred_element_type=F32)


def params(mebibytes):
    return pltpu.CompilerParams(vmem_limit_bytes=mebibytes * 1024 * 1024)


def grid_of(devices):
    side = max(1, round((devices / 4) ** 0.5))
    return (devices // (side * side), side, side)


class Chips:
    def __init__(self):
        self.count = lax.axis_size("dp")
        self.sizes = grid_of(self.count)
        self.plane = self.sizes[1] * self.sizes[2]
        self.strides = (self.plane, self.sizes[2], 1)
        self.me = lax.axis_index("dp")
        layers = range(self.sizes[0])
        self.planes = [[z * self.plane + i for i in range(self.plane)] for z in layers]
        self.columns = [[z * self.plane + i for z in layers] for i in range(self.plane)]

    def send(self, block, axis, distance):
        size, stride = self.sizes[axis], self.strides[axis]
        route = []
        for i in range(self.count):
            c = (i // stride) % size
            route.append((i, i + ((c + distance) % size - c) * stride))
        return lax.ppermute(block, "dp", route)

    def gather_rows(self, block, after=(), plane_after=(), aside=None):
        block = tie(block, *after)
        if self.sizes[1:] != (2, 2):
            whole = lax.all_gather(block, "dp", axis=0, tiled=True)
            return (whole,), (block,), (block,), (block,)
        half = block.shape[0] // 2
        layers = tuple(self.send(block, 0, k) for k in range(1, self.sizes[0]))
        own = jnp.stack((block,) + layers)
        own = tie(own, *plane_after)
        by_x, by_y = self.send(own, 2, 1), self.send(own, 1, 1)
        waits = () if aside is None else aside(layers)
        far_top = self.send(tie(by_y[:, :half], *waits), 2, 1)
        far_low = self.send(by_x[:, half:], 1, 1)
        return (own, by_x, by_y, far_top, far_low), layers, (by_x, by_y), (far_top, far_low)

    def order(self, rows):
        part = rows // self.count
        return [(z * self.plane + i) * part for i in range(self.plane) for z in range(self.sizes[0])]

    def exchange(self, block, groups):
        heard = lax.all_to_all(block, "dp", 0, 0, axis_index_groups=groups, tiled=True)
        count = len(groups[0])
        heard = heard.reshape(count, block.shape[0] // count, block.shape[1])
        total = heard[0].astype(F32)
        for i in range(1, count):
            total = total + heard[i].astype(F32)
        return total


    def trade(self, block, groups, after=()):
        count = block.shape[0]
        at = self.me % self.plane if groups is self.planes else self.me // self.plane
        total = tie(lax.dynamic_index_in_dim(block, at, 0, keepdims=False), *after).astype(F32)
        for k in range(1, count):
            part = lax.dynamic_index_in_dim(block, at ^ k, 0, keepdims=False)
            route = [(g[i], g[i ^ k]) for g in groups for i in range(count)]
            total = total + lax.ppermute(part, "dp", route).astype(F32)
        return total


def tie_kernel(*refs):
    pass


def tie(block, *others):
    if not others:
        return block
    anywhere = pl.BlockSpec(memory_space=pl.ANY)
    return pl.pallas_call(
        tie_kernel,
        in_specs=[anywhere] * (1 + len(others)),
        out_specs=anywhere,
        out_shape=jax.ShapeDtypeStruct(block.shape, block.dtype),
        input_output_aliases={0: 0},
        name="tie",
    )(block, *others)


def load_parts(me, parts, columns, target, sems):
    copy = pltpu.make_async_copy
    if len(parts) == 1:
        return [copy(parts[0].at[:, columns], target, sems.at[0])]
    z, y, x = me[0] // 4, lax.rem(me[0] // 2, 2), lax.rem(me[0], 2)
    layers, rows = parts[0].shape[:2]
    places = (2 * y + x, 2 * y + 1 - x, 2 * (1 - y) + x) + (2 * (1 - y) + 1 - x,) * 2
    copies = []
    for k in range(layers):
        layer = lax.rem(z - k + layers, layers)
        for i, (part, place) in enumerate(zip(parts, places)):
            start = (layer * 4 + place) * rows + (rows // 2 if i == 4 else 0)
            rows_at = pl.ds(pl.multiple_of(start, rows // 2), part.shape[1])
            copies.append(copy(part.at[k, :, columns], target.at[rows_at], sems.at[len(copies)]))
    return copies


PARTS = 20


def other_core(block):
    return lax.ppermute(block, "mp", [(0, 1), (1, 0)])


def send_half(block, after=()):
    count = lax.axis_size("dp")
    route = [(i, (i + count // 2) % count) for i in range(count)]
    rows = block.shape[0] // 2
    core = lax.axis_index("mp")
    mine = tie(lax.dynamic_slice_in_dim(block, core * rows, rows, 0), *after)
    return lax.ppermute(mine, "dp", route)


def join_halves(mine):
    theirs = other_core(mine)
    first = lax.axis_index("mp") == 0
    return jnp.concatenate([jnp.where(first, mine, theirs), jnp.where(first, theirs, mine)], axis=0)


SCALAR = pl.BlockSpec(memory_space=pltpu.SMEM)


def attend_kernel(first, extra, table, q_ref, k_ref, v_ref, cells_ref, lay_ref, *refs):
    mix_ref, prob_to, inv_ref, keys, values, layout, near, prob_ref, sems, *score = refs[extra:]
    step = pl.program_id(0)
    pair = step + first
    length = k_ref.shape[0]
    keys[:, :128] = k_ref[...]
    keys[:, 128:] = cells_ref[...]
    values_t = v_ref[...].astype(F32).T.astype(BF16)
    for h in range(2):
        values[h, :DH] = values_t[h * DH : (h + 1) * DH]
        values[h, DH:] = jnp.ones((16, length), BF16)
    gap = WIN - lax.broadcasted_iota(jnp.int32, (8, BQ + WIN), 1) - PAD
    gap = jnp.clip(gap, -(RB // 2), RB // 2 - 1) + RB // 2
    for h in range(2):
        head = pair * 2 + h
        lay = lay_ref[...]
        grid = jnp.zeros(lay.shape, F32)
        for b in range(LQ * LQ):
            grid = jnp.where(lay == b, table[RB + b, head], grid)
        layout[h] = grid.astype(BF16)
        line = jnp.zeros(gap.shape, F32)
        for b in range(RB):
            line = jnp.where(gap == b, table[b, head], line)
        spread = jnp.broadcast_to(line[:1], (WIN, BQ + WIN))
        near[h] = pltpu.roll(spread, 0, 1, stride=1, stride_axis=0)[:, WIN:]

    lane = lax.broadcasted_iota(jnp.int32, (1, 128), 1)
    feature = lax.broadcasted_iota(jnp.int32, (1, CELLS), 1)
    tile = feature - TILE0
    is_tile = (tile >= 0) & (tile < 10)

    def fill(item, buffer):
        block, h = divmod(item, 2)
        start, head = block * BQ, pair * 2 + h
        rows = slice(start, start + BQ)
        left = is_tile & ((tile + 2) * 128 <= start)
        right = is_tile & (tile * 128 >= start + BQ + PAD)
        far = jnp.where(left, table[0, head], jnp.where(right, table[RB - 1, head], 0.0))
        far = jnp.where(feature == DEAD, MASKED, far)
        bias = (nn(cells_ref[rows], layout[h]) + far).astype(BF16)
        mine = jnp.where((lane // DH) == h, q_ref[rows] * DH ** (-0.5), 0.0).astype(BF16)
        buffer[...] = nt(keys[...], jnp.concatenate([mine, bias], axis=1))
        low, high = max(start - PAD, 0), min(start + BQ + PAD, length)
        shift = low - (start - PAD)
        buffer[low:high] += near[h, shift : shift + high - low]

    def use(item, buffer):
        block, h = divmod(item, 2)
        scores = buffer[...]
        top = jnp.max(scores, axis=0, keepdims=True)
        weight = jnp.exp(scores - top).astype(BF16)
        prob_ref[step, h, block] = weight
        out_copy(step, h, block).start()
        summed = nn(values[h], weight)
        inverse = 1.0 / summed[DH : DH + 1]
        inv_ref[h, :, block * BQ : (block + 1) * BQ] = inverse
        return summed[:DH] * inverse

    def out_copy(at, h, block):
        place = prob_to.at[2 * (first + at) + h, block]
        return pltpu.make_async_copy(prob_ref.at[at, h, block], place, sems.at[at, h, block])

    items = 2 * (length // BQ)
    depth = len(score)
    for item in range(min(depth - 1, items)):
        fill(item, score[item % depth])
    mixed = []
    for item in range(items):
        if item + depth - 1 < items:
            fill(item + depth - 1, score[(item + depth - 1) % depth])
        mixed.append(use(item, score[item % depth]))
        if item % 2:
            start = item // 2 * BQ
            mix_ref[start : start + BQ] = jnp.concatenate(mixed[-2:], axis=0).T.astype(BF16)

    @pl.when(step == pl.num_programs(0) - 1)
    def _():
        for at in range(prob_ref.shape[0]):
            for item in range(items):
                out_copy(at, item % 2, item // 2).wait()


def attend(table, projected, cells, lay, first, pairs, width, into=(), after=()):
    rows = projected.shape[0]
    blocks, all_pairs = rows // BQ, width // 128
    pair_spec = lambda i: pl.BlockSpec((rows, 128), lambda p: (0, i * all_pairs + first + p))
    anywhere = pl.BlockSpec(memory_space=pl.ANY)
    extra = len(into) + len(after)
    return pl.pallas_call(
        functools.partial(attend_kernel, first, extra),
        grid=(pairs,),
        in_specs=[
            pl.BlockSpec(memory_space=pltpu.SMEM),
            pair_spec(0),
            pair_spec(1),
            pair_spec(2),
            pl.BlockSpec((rows, CELLS), lambda p: (0, 0)),
            pl.BlockSpec((CELLS, CELLS), lambda p: (0, 0)),
        ]
        + [anywhere] * extra,
        out_specs=[
            pair_spec(0),
            anywhere,
            pl.BlockSpec((2, 1, rows), lambda p: (first + p, 0, 0)),
        ],
        out_shape=[
            jax.ShapeDtypeStruct((rows, width), BF16),
            jax.ShapeDtypeStruct((2 * all_pairs, blocks, rows, BQ), BF16),
            jax.ShapeDtypeStruct((2 * all_pairs, 1, rows), F32),
        ],
        input_output_aliases={6 + i: i for i in range(len(into))},
        scratch_shapes=[
            pltpu.VMEM((rows, 128 + CELLS), BF16),
            pltpu.VMEM((2, DH + 16, rows), BF16),
            pltpu.VMEM((2, CELLS, CELLS), BF16),
            pltpu.VMEM((2, WIN, BQ), F32),
            pltpu.VMEM((pairs, 2, blocks, rows, BQ), BF16),
            pltpu.SemaphoreType.DMA((pairs, 2, blocks)),
        ]
        + [pltpu.VMEM((rows, BQ), F32)] * 3,
        compiler_params=params(36),
        cost_estimate=pl.CostEstimate(
            flops=2 * 2 * pairs * rows * rows * 512 * 3 * ATTEND_WEIGHT,
            bytes_accessed=2 * 2 * pairs * rows * rows,
            transcendentals=2 * pairs * rows * rows,
        ),
        name="attend",
    )(table, projected, projected, projected, cells, lay, *into, *after)


def heads_back_kernel(
    order, first, starts, q_ref, k_ref, v_ref, gm_ref, mix_ref, inv_ref, cells_ref, cells_t_ref, lay_ref,
    table_in, prob_from, rows_from, weights_from, more_from, *refs
):
    out_to, sums_to, table_ref = refs[-23:-20]
    left, queries, grads, query_acc, key_acc, value_acc, by_cell, near_acc = refs[-20:-12]
    prob_ref, found, rows_t, weights, more, out, sums, prob_sems, sems = refs[-12:-3]
    buffers = refs[-3:]
    step = pl.program_id(0)
    copy = pltpu.make_async_copy
    length = k_ref.shape[0]
    blocks = length // BQ
    half = found.shape[2]

    def prob_copy(at, h, block):
        place = prob_from.at[2 * (first + at) + h, block]
        return copy(place, prob_ref.at[at, h, block], prob_sems.at[at, h, block])

    loads = [copy(rows_from, rows_t, sems.at[0]), copy(more_from, more, sems.at[1])] + [
        copy(weights_from.at[:, start : start + half], weights.at[i], sems.at[2 + i])
        for i, start in enumerate(starts)
    ]

    @pl.when(step == 0)
    def _():
        for at in range(prob_ref.shape[0]):
            for item in range(2 * blocks):
                prob_copy(at, item % 2, item // 2).start()
        for load in loads:
            load.start()
        table_ref[...] = table_in[...]

    keys_t = k_ref[...].astype(F32).T.astype(BF16)
    queries[...] = q_ref[...].astype(F32).T.astype(BF16)
    grad_mix = gm_ref[...].astype(F32)
    grad_mix_t = grad_mix.T
    weighted_t = (grad_mix * mix_ref[...].astype(F32)).T
    inner = []
    for h in range(2):
        own = slice(h * DH, (h + 1) * DH)
        left[h, :DH] = keys_t[own]
        left[h, DH:] = cells_t_ref[...]
        inverse = inv_ref[h]
        grads[h] = jnp.zeros(grads.shape[1:], BF16)
        grads[h, own] = (grad_mix_t[own] * inverse).astype(BF16)
        inner.append(jnp.sum(weighted_t[own], axis=0, keepdims=True) * inverse)

    def fill(item, buffer):
        block, h = divmod(item, 2)
        buffer[...] = nn(v_ref[...], grads[h, :, block * BQ : (block + 1) * BQ])

    far_left, far_right = [[], []], [[], []]

    def use(item, buffer):
        block, h = divmod(item, 2)
        start = block * BQ
        cols = slice(start, start + BQ)
        own = slice(h * DH, (h + 1) * DH)
        prob_copy(step, h, block).wait()
        prob = prob_ref[step, h, block]
        grad_score = (prob.astype(F32) * (buffer[...] - inner[h][:, cols])).astype(BF16)
        both = nn(left[h], grad_score)
        query_acc[own, cols] = both[:DH]
        by_cell[h, :, cols] = both[DH:].astype(BF16)
        tiles = both[DH + TILE0 : DH + TILE0 + length // 128]
        for t in range(length // 128):
            if (t + 2) * 128 <= start:
                far_left[h].append(tiles[t : t + 1])
            elif t * 128 >= start + BQ + PAD:
                far_right[h].append(tiles[t : t + 1])
        key_part = nt(queries[own, cols], grad_score)
        value_part = nt(grads[h, own, cols], prob)
        low, high = max(start - PAD, 0), min(start + BQ + PAD, length)
        shift = low - (start - PAD)
        part = grad_score[low:high].astype(F32)
        if block == 0:
            key_acc[own] = key_part
            value_acc[own] = value_part
            near_acc[h, :shift] = jnp.zeros((shift, BQ), F32)
            near_acc[h, shift : shift + high - low] = part
        else:
            key_acc[own] += key_part
            value_acc[own] += value_part
            near_acc[h, shift : shift + high - low] += part

    items = 2 * blocks
    depth = len(buffers)
    for item in range(min(depth - 1, items)):
        fill(item, buffers[item % depth])
    for item in range(items):
        if item + depth - 1 < items:
            fill(item + depth - 1, buffers[(item + depth - 1) % depth])
        use(item, buffers[item % depth])

    place = pl.ds(pl.multiple_of(step * 128, 128), 128)
    found[0, :, place] = (query_acc[...].T * DH ** (-0.5)).astype(BF16)
    found[1, :, place] = (key_acc[...].T * DH ** (-0.5)).astype(BF16)
    found[2, :, place] = value_acc[...].T.astype(BF16)
    turn = lax.broadcasted_iota(jnp.int32, (BQ, BQ), 0) + lax.broadcasted_iota(jnp.int32, (BQ, BQ), 1)
    turn = (turn == BQ - 1).astype(BF16)
    column = lax.broadcasted_iota(jnp.int32, (1, BQ + WIN), 1)
    bucket = jnp.clip(column - (BQ - 1 + PAD), -(RB // 2), RB // 2 - 1) + RB // 2
    lower = lax.broadcasted_iota(jnp.int32, (16, 1), 0)
    table_lane = lax.broadcasted_iota(jnp.int32, (1, 128), 1)
    lay = lay_ref[:FEAT_ROWS]
    for h in range(2):
        pairs = nn(by_cell[h], cells_ref[...])
        bucket_sums = [
            jnp.sum(jnp.where(lay == b, pairs, 0.0), axis=0, keepdims=True) for b in range(LQ * LQ)
        ]
        lay_part = jnp.sum(jnp.concatenate(bucket_sums, axis=0), axis=1, keepdims=True)
        band = near_acc[h]
        high = band.astype(BF16)
        low = (band - high.astype(F32)).astype(BF16)
        band = nn(high, turn) + nn(low, turn)
        band = jnp.concatenate([band, jnp.zeros((WIN, WIN), F32)], axis=1)
        band = pltpu.roll(band, 0, 1, stride=1, stride_axis=0)
        rel = jnp.sum(band, axis=0, keepdims=True)
        rel = rel + jnp.where(column == 0, jnp.sum(sum(far_left[h]), axis=1, keepdims=True), 0.0)
        last = column == BQ + WIN - 1
        rel = rel + jnp.where(last, jnp.sum(sum(far_right[h]), axis=1, keepdims=True), 0.0)
        head = 2 * (first + step) + h
        for t, part in enumerate(
            (
                jnp.sum(jnp.where(bucket == lower, rel, 0.0), axis=1, keepdims=True),
                jnp.sum(jnp.where(bucket == lower + 16, rel, 0.0), axis=1, keepdims=True),
                lay_part,
            )
        ):
            table_ref[...] += jnp.where(table_lane == t * 16 + head, part, 0.0)

    @pl.when(step == pl.num_programs(0) - 1)
    def _():
        for load in loads:
            load.wait()
        result = nt(found[0], weights[0]) + nt(found[1], weights[1]) + nt(found[2], weights[2])
        if first:
            result = result + more[...].astype(F32)
        out[...] = result.astype(BF16)
        store = copy(out, out_to, sems.at[0])
        store.start()
        model = rows_t.shape[0]
        part = model // len(order)
        places = sums.shape[0]
        chunk = model // places
        for i in range(3):
            grad = nn(rows_t[...], found[i]).astype(BF16)
            for k, start in enumerate(order):
                place, at = divmod(k * part, chunk)
                sums[place, at : at + part, i * half : (i + 1) * half] = grad[start : start + part]
        if first:
            high = table_ref[...].astype(BF16)
            low = (table_ref[...] - high.astype(F32)).astype(BF16)
            rest = jnp.zeros((16, 3 * half - 256), BF16)
            for place in range(places):
                sums[place, chunk:] = jnp.concatenate([high, low, rest], axis=1)
        else:
            for place in range(places):
                sums[place, :, 3 * half :] = more[place * chunk : (place + 1) * chunk]
        last_store = copy(sums, sums_to, sems.at[1])
        last_store.start()
        store.wait()
        last_store.wait()


def heads_back(
    projected, grad_mix, mixture, probs, inverse, cells, cells_t, lay, rows_t, weights, first, pairs, order, plane,
    table, more, after=()
):
    rows, width = grad_mix.shape
    model = rows_t.shape[0]
    blocks, all_pairs, half = rows // BQ, width // 128, 128 * pairs
    pair_spec = lambda i: pl.BlockSpec((rows, 128), lambda p: (0, i * all_pairs + first + p))
    whole = lambda *shape: pl.BlockSpec(shape, lambda p: (0, 0))
    anywhere = pl.BlockSpec(memory_space=pl.ANY)
    if first:
        shape = (plane, model // plane + 16, 3 * half)
    else:
        shape = (plane, model // plane, 3 * half + more.shape[1])
    vmem = lambda *shape: pltpu.VMEM(shape, BF16)
    starts = [i * width + 128 * first for i in range(3)]
    return pl.pallas_call(
        functools.partial(heads_back_kernel, order, first, starts),
        grid=(pairs,),
        in_specs=[pair_spec(0), pair_spec(1), pair_spec(2), pair_spec(0), pair_spec(0)]
        + [
            pl.BlockSpec((2, 1, rows), lambda p: (first + p, 0, 0)),
            whole(rows, CELLS),
            whole(FEAT_ROWS, rows),
            whole(CELLS, CELLS),
            whole(16, 128),
        ]
        + [anywhere] * (4 + len(after)),
        out_specs=[anywhere, anywhere, whole(16, 128)],
        out_shape=[
            jax.ShapeDtypeStruct((rows, model), BF16),
            jax.ShapeDtypeStruct(shape, BF16),
            jax.ShapeDtypeStruct((16, 128), F32),
        ],
        scratch_shapes=[
            vmem(2, DH + FEAT_ROWS, rows),
            vmem(128, rows),
            vmem(2, 128, rows),
            pltpu.VMEM((128, rows), F32),
            pltpu.VMEM((128, rows), F32),
            pltpu.VMEM((128, rows), F32),
            vmem(2, FEAT_ROWS, rows),
            pltpu.VMEM((2, WIN, BQ), F32),
            vmem(pairs, 2, blocks, rows, BQ),
            vmem(3, rows, half),
            vmem(model, rows),
            vmem(3, model, half),
            vmem(*more.shape),
            vmem(rows, model),
            vmem(*shape),
            pltpu.SemaphoreType.DMA((pairs, 2, blocks)),
            pltpu.SemaphoreType.DMA((5,)),
        ]
        + [pltpu.VMEM((rows, BQ), F32)] * 3,
        compiler_params=params(60),
        cost_estimate=pl.CostEstimate(
            flops=2 * pairs * rows * rows * 256 * 2 + 4 * rows * model * half,
            bytes_accessed=2 * pairs * rows * rows,
            transcendentals=0,
        ),
        name="heads_back",
    )(
        projected, projected, projected, grad_mix, mixture, inverse, cells, cells_t, lay,
        table, probs, rows_t, weights, more, *after,
    )


def ffn_kernel(first, count, extra, base, hidden, order, me, x_in, g_in, *refs):
    parts, refs = refs[:count], refs[count:]
    if not first:
        out_in, grad_in = refs[:2]
    refs = refs[extra:]
    out_to, grad_to, sums_to = refs[:3]
    x, g, w, rows_t, grads_t, act_all, gate_all, up_all, out, grad, sums = refs[3:14]
    sems, sum_sems, part_sems = refs[14:17]
    total, model = x.shape
    copy = pltpu.make_async_copy
    weight = lambda i: load_parts(
        me, parts, slice(base + i * hidden, base + (i + 1) * hidden), w.at[i], part_sems.at[i]
    )
    loads = [[copy(x_in, x, sems.at[0])], weight(0), weight(1), [copy(g_in, g, sems.at[3])], weight(2)]
    if not first:
        out_old, grad_old = refs[17:19]
        loads += [[copy(out_in, out_old, sems.at[5])], [copy(grad_in, grad_old, sems.at[6])]]
    for load in sum(loads, []):
        load.start()
    loads[0][0].wait()
    rows_t[...] = x[...].astype(F32).T.astype(BF16)
    for load in sum(loads[1:4], []):
        load.wait()
    grads_t[...] = g[...].astype(F32).T.astype(BF16)
    for load in sum(loads[4:], []):
        load.wait()
    slope = (2 / jnp.pi) ** 0.5
    for cut in range(2):
        rows = slice(cut * (total // 2), (cut + 1) * (total // 2))
        gate = nn(x[rows], w[0]).astype(BF16).astype(F32)
        up = nn(x[rows], w[1]).astype(BF16).astype(F32)
        grad_act = nn(g[rows], w[2])
        square = gate * gate
        tanh = jnp.tanh(gate * (slope + slope * 0.044715 * square))
        half = 0.5 + 0.5 * tanh
        value = gate * half
        deriv = half + (0.5 * gate) * (1.0 - tanh * tanh) * (slope + 3 * 0.044715 * slope * square)
        act_all[rows] = (value * up).astype(BF16)
        gate_all[rows] = (deriv * up * grad_act).astype(BF16)
        up_all[rows] = (value * grad_act).astype(BF16)
    for cut in range(2):
        rows = slice(cut * (total // 2), (cut + 1) * (total // 2))
        out_part = nt(act_all[rows], w[2])
        grad_part = nt(gate_all[rows], w[0]) + nt(up_all[rows], w[1])
        if not first:
            out_part = out_part + out_old[rows].astype(F32)
            grad_part = grad_part + grad_old[rows].astype(F32)
        out[rows] = out_part.astype(BF16)
        grad[rows] = grad_part.astype(BF16)
    stores = [copy(grad, grad_to, sems.at[0]), copy(out, out_to, sems.at[1])]
    for store in stores:
        store.start()
    part = model // len(order)
    for i, (left, right) in enumerate(((rows_t, gate_all), (rows_t, up_all), (grads_t, act_all))):
        sums[i] = nn(left[...], right[...]).astype(BF16)
        for k, row in enumerate(order):
            store = copy(
                sums.at[i, row : row + part],
                sums_to.at[k * part : (k + 1) * part, i * hidden : (i + 1) * hidden],
                sum_sems.at[i, k],
            )
            store.start()
            stores.append(store)
    for store in stores:
        store.wait()


def ffn(me, normed, grad_ffn, parts, base, hidden, order, before=()):
    rows, model = normed.shape
    first = not before
    extra = len(before)
    anywhere = pl.BlockSpec(memory_space=pl.ANY)
    part = jax.ShapeDtypeStruct((rows, model), BF16)
    vmem = lambda *shape: pltpu.VMEM(shape, BF16)
    return pl.pallas_call(
        functools.partial(ffn_kernel, first, len(parts), extra, base, hidden, order),
        in_specs=[SCALAR] + [anywhere] * (2 + len(parts) + extra),
        out_specs=[anywhere] * 3,
        out_shape=[part, part, jax.ShapeDtypeStruct((model, 3 * hidden), BF16)],
        scratch_shapes=[vmem(rows, model)] * 2
        + [vmem(3, model, hidden)]
        + [vmem(model, rows)] * 2
        + [vmem(rows, hidden)] * 3
        + [vmem(rows, model)] * 2
        + [vmem(3, model, hidden)]
        + [pltpu.SemaphoreType.DMA((7,)), pltpu.SemaphoreType.DMA((3, len(order)))]
        + [pltpu.SemaphoreType.DMA((3, PARTS))]
        + ([] if first else [vmem(rows, model)] * 2),
        compiler_params=params(60),
        cost_estimate=pl.CostEstimate(
            flops=18 * rows * model * hidden,
            bytes_accessed=12 * model * hidden + 8 * rows * model,
            transcendentals=rows * hidden,
        ),
        name="ffn_first" if first else "ffn_last",
    )(me, normed, grad_ffn, *parts, *before)


def rows_spec(columns, limit=None):
    if limit is None:
        return pl.BlockSpec((BQ, columns), lambda r: (r, 0))
    return pl.BlockSpec((BQ, columns), lambda r: (jnp.minimum(r, limit // BQ - 1), 0))


def fixed_spec(*shape):
    return pl.BlockSpec(shape, lambda r: (0,) * len(shape))


def is_text(count):
    row = lax.broadcasted_iota(jnp.int32, (BQ, 1), 0) + pl.program_id(0) * BQ
    return row < count[0]


def row_call(kernel, name, rows, in_specs, out, scratch, flops, *operands):
    out_specs, out_shape = zip(*out)
    return pl.pallas_call(
        kernel,
        grid=(rows // BQ,),
        in_specs=in_specs,
        out_specs=out_specs,
        out_shape=[jax.ShapeDtypeStruct(*o) for o in out_shape],
        scratch_shapes=scratch,
        compiler_params=params(60 if name in STREAMED else 20),
        cost_estimate=pl.CostEstimate(flops=flops, bytes_accessed=20 * rows * 1024, transcendentals=0),
        name=name,
    )(*operands)


def embed_kernel(count, text, spread, patches, rows):
    own = jnp.where(is_text(count), text[...].astype(F32), 0.0)
    rows[...] = (own + nn(spread[...], patches[...])).astype(rows.dtype)


def embed(count, text, spread, patches, kind=F32):
    rows, slots = spread.shape
    texts, model = text.shape
    return row_call(
        embed_kernel, "embed", rows,
        [SCALAR, rows_spec(model, texts), rows_spec(slots), fixed_spec(slots, model)],
        [(rows_spec(model), ((rows, model), kind))],
        [], 2 * rows * slots * model, count, text, spread, patches,
    )[0]


def norm(rows):
    inv = lax.rsqrt(jnp.mean(rows * rows, axis=1, keepdims=True) + EPS)
    return rows * inv, inv


def norm_back(grad_normed, rows, gain):
    unit, inv = norm(rows)
    grad_unit = grad_normed * gain
    return inv * (grad_unit - unit * jnp.mean(grad_unit * unit, axis=1, keepdims=True))


def project_kernel(count, me, rows_from, *refs):
    parts = refs[:count]
    projected_to, normed_to, weights_to, gains = refs[count : count + 4]
    rows, weights, projected, normed_t, sems, part_sems = refs[count + 4 :]
    copy = pltpu.make_async_copy
    load = copy(rows_from, rows, sems.at[0])
    loads = load_parts(me, parts, slice(0, weights.shape[1]), weights, part_sems)
    load.start()
    for each in loads:
        each.start()
    for each in loads:
        each.wait()
    store = copy(weights, weights_to, sems.at[1])
    store.start()
    length, width = projected.shape
    gains[...] = weights[:, width:].astype(F32).T[:8]
    load.wait()
    stores = [store]
    for i in range(2):
        part = slice(i * length // 2, (i + 1) * length // 2)
        normed = norm(rows[part])[0] * gains[:1]
        normed_t[:, part] = normed.T.astype(BF16)
        projected[part] = nn(normed.astype(BF16), weights[:, :width]).astype(BF16)
        stores.append(copy(projected.at[part], projected_to.at[part], sems.at[2 + i]))
        stores[-1].start()
    stores.append(copy(normed_t, normed_to, sems.at[4]))
    stores[-1].start()
    for store in stores:
        store.wait()


def project(me, rows, parts):
    length, model = rows.shape
    columns = parts[0].shape[-1]
    width = columns - 128
    anywhere = pl.BlockSpec(memory_space=pl.ANY)
    return pl.pallas_call(
        functools.partial(project_kernel, len(parts)),
        in_specs=[SCALAR] + [anywhere] * (1 + len(parts)),
        out_specs=[anywhere] * 3 + [pl.BlockSpec(memory_space=pltpu.VMEM)],
        out_shape=[
            jax.ShapeDtypeStruct((length, width), BF16),
            jax.ShapeDtypeStruct((model, length), BF16),
            jax.ShapeDtypeStruct((model, columns), BF16),
            jax.ShapeDtypeStruct((8, model), F32),
        ],
        scratch_shapes=[
            pltpu.VMEM((length, model), F32),
            pltpu.VMEM((model, columns), BF16),
            pltpu.VMEM((length, width), BF16),
            pltpu.VMEM((model, length), BF16),
            pltpu.SemaphoreType.DMA((5,)),
            pltpu.SemaphoreType.DMA((PARTS,)),
        ],
        compiler_params=params(40),
        cost_estimate=pl.CostEstimate(
            flops=2 * length * model * width, bytes_accessed=16 * length * model, transcendentals=0
        ),
        name="project",
    )(me, rows, *parts)


def mix_out_kernel(count, me, mixture_from, *refs):
    parts = refs[:count]
    out_to, weight_to, mixture, weight, out, sems, part_sems = refs[count:]
    copy = pltpu.make_async_copy
    loads = load_parts(me, parts, slice(0, weight.shape[1]), weight, part_sems)
    loads.append(copy(mixture_from, mixture, sems.at[0]))
    for each in loads:
        each.start()
    for each in loads:
        each.wait()
    stores = [copy(weight, weight_to, sems.at[1])]
    stores[0].start()
    length = mixture.shape[0]
    for i in range(2):
        part = slice(i * length // 2, (i + 1) * length // 2)
        out[part] = nt(mixture[part], weight[...]).astype(BF16)
        stores.append(copy(out.at[part], out_to.at[part], sems.at[2 + i]))
        stores[-1].start()
    for store in stores:
        store.wait()


def mix_out(me, mixture, parts, model):
    length, width = mixture.shape
    anywhere = pl.BlockSpec(memory_space=pl.ANY)
    vmem = lambda *shape: pltpu.VMEM(shape, BF16)
    return pl.pallas_call(
        functools.partial(mix_out_kernel, len(parts)),
        in_specs=[SCALAR] + [anywhere] * (1 + len(parts)),
        out_specs=[anywhere] * 2,
        out_shape=[
            jax.ShapeDtypeStruct((length, model), BF16),
            jax.ShapeDtypeStruct((model, width), BF16),
        ],
        scratch_shapes=[vmem(length, width), vmem(model, width), vmem(length, model)]
        + [pltpu.SemaphoreType.DMA((4,)), pltpu.SemaphoreType.DMA((PARTS,))],
        compiler_params=params(24),
        cost_estimate=pl.CostEstimate(
            flops=2 * length * model * width, bytes_accessed=4 * length * model, transcendentals=0
        ),
        name="mix_out",
    )(me, mixture, *parts)


def middle_kernel(rows, own, other, gains, hidden, normed):
    total = rows[...] + (own[...].astype(F32) + other[...].astype(F32))
    hidden[...] = total
    normed[...] = (norm(total)[0] * gains[1:2]).astype(BF16)


def middle(rows, own, other, gains):
    count, model = rows.shape
    return row_call(
        middle_kernel, "middle", count,
        [rows_spec(model)] * 3 + [fixed_spec(8, model)],
        [(rows_spec(model), ((count, model), F32)), (rows_spec(model), ((count, model), BF16))],
        [], 0, rows, own, other, gains,
    )


def after_kernel(order, hidden, own, other, grad_out, gains, weight, mixture, *refs):
    grad_attn, grad_mix, sums, acc = refs[-4:]
    step = pl.program_id(0)

    @pl.when(step == 0)
    def _():
        acc[...] = jnp.zeros(acc.shape, F32)

    grad = own[...].astype(F32) + other[...].astype(F32)
    grad = grad_out[...].astype(F32) + norm_back(grad, hidden[...], gains[1:2])
    low = grad.astype(BF16)
    grad_attn[...] = low
    grad_mix[...] = nn(low, weight[...]).astype(BF16)
    acc[...] += nn(grad.T.astype(BF16), mixture[...])

    @pl.when(step == pl.num_programs(0) - 1)
    def _():
        part = acc.shape[0] // len(order)
        for k, start in enumerate(order):
            sums[k * part : (k + 1) * part] = acc[start : start + part].astype(BF16)


def after_ffn(hidden, own, other, grad_out, gains, weights, mixture, order, after=()):
    rows, model = hidden.shape
    width = mixture.shape[1]
    return row_call(
        functools.partial(after_kernel, order), "after_ffn", rows,
        [rows_spec(model)] * 4
        + [fixed_spec(8, model), fixed_spec(model, width), rows_spec(width)]
        + [pl.BlockSpec(memory_space=pl.ANY)] * len(after),
        [
            (rows_spec(model), ((rows, model), BF16)),
            (rows_spec(width), ((rows, width), BF16)),
            (fixed_spec(model, width), ((model, width), BF16)),
        ],
        [pltpu.VMEM((model, width), F32)], 4 * rows * model * width,
        hidden, own, other, grad_out, gains, weights, mixture, *after,
    )


def last_kernel(count, rows, own, other, grad, gains, spread, *refs):
    text_grad, patch_grad, acc = refs[-3:]
    step = pl.program_id(0)

    @pl.when(step == 0)
    def _():
        acc[...] = jnp.zeros(acc.shape, F32)

    total = own[...].astype(F32) + other[...].astype(F32)
    total = grad[...].astype(F32) + norm_back(total, rows[...], gains[:1])

    @pl.when(step < pl.num_programs(0) - 1)
    def _():
        text_grad[...] = jnp.where(is_text(count), total, 0.0).astype(BF16)

    high = total.astype(BF16)
    low = (total - high.astype(F32)).astype(BF16)
    places = spread[...].astype(F32).T.astype(BF16)
    acc[...] += nn(places, high) + nn(places, low)

    @pl.when(step == pl.num_programs(0) - 1)
    def _():
        patch_grad[...] = acc[...].astype(BF16)


def last(count, rows, own, other, grad, gains, spread, texts, after=()):
    length, model = rows.shape
    slots = spread.shape[1]
    return row_call(
        last_kernel, "last", length,
        [SCALAR] + [rows_spec(model)] * 4 + [fixed_spec(8, model), rows_spec(slots)]
        + [pl.BlockSpec(memory_space=pl.ANY)] * len(after),
        [(rows_spec(model, texts), ((texts, model), BF16)), (fixed_spec(slots, model), ((slots, model), BF16))],
        [pltpu.VMEM((slots, model), F32)], 4 * length * model * slots,
        count, rows, own, other, grad, gains, spread, *after,
    )


def result_kernel(count, hidden, own, other, pick, *refs):
    text_out, patch_out, acc = refs[-3:]
    step = pl.program_id(0)

    @pl.when(step == 0)
    def _():
        acc[...] = jnp.zeros(acc.shape, F32)

    total = hidden[...] + (own[...].astype(F32) + other[...].astype(F32))

    @pl.when(step < pl.num_programs(0) - 1)
    def _():
        text_out[...] = jnp.where(is_text(count), total, 0.0).astype(BF16)

    acc[...] += nn(pick[...].astype(F32).T.astype(BF16), total.astype(BF16))

    @pl.when(step == pl.num_programs(0) - 1)
    def _():
        patch_out[...] = acc[...].astype(BF16)


def result(count, hidden, own, other, pick, texts, after=()):
    length, model = hidden.shape
    slots = pick.shape[1]
    return row_call(
        result_kernel, "result", length,
        [SCALAR] + [rows_spec(model)] * 3 + [rows_spec(slots)]
        + [pl.BlockSpec(memory_space=pl.ANY)] * len(after),
        [(rows_spec(model, texts), ((texts, model), BF16)), (fixed_spec(slots, model), ((slots, model), BF16))],
        [pltpu.VMEM((slots, model), F32)], 2 * length * model * slots,
        count, hidden, own, other, pick, *after,
    )


def finish_kernel(cuts, ffn_one, ffn_two, heads, wq, wk, wv, w_gate, w_up, *outs):
    part, width = wq.shape
    half = width // 2
    start = 0
    for size, source in zip(cuts, (ffn_one, ffn_two)):
        for i, out in enumerate(outs[4:7]):
            out[:, start : start + size] = source[:, i * size : (i + 1) * size].astype(F32)
        start += size
    first = 3 * cuts[1]
    for i, out in enumerate(outs[:3]):
        out[:, :half] = ffn_two[:, first + i * half : first + (i + 1) * half].astype(F32)
        out[:, half:] = heads[:, i * half : (i + 1) * half].astype(F32)
    outs[3][...] = ffn_two[:, first + 3 * half :].astype(F32)
    total = lambda w, out: jnp.sum(w[...].astype(F32) * out[...], axis=1, keepdims=True)
    one = total(wq, outs[0]) + total(wk, outs[1]) + total(wv, outs[2])
    two = total(w_gate, outs[4]) + total(w_up, outs[5])
    lane = lax.broadcasted_iota(jnp.int32, (part, 128), 1)
    outs[7][...] = jnp.where(lane == 0, one, jnp.where(lane == 1, two, 0.0))


def finish(sums, weights, cuts, width):
    part, hidden = weights[-1].shape
    shapes = [(part, width)] * 4 + [(part, hidden)] * 3 + [(part, 128)]
    return pl.pallas_call(
        functools.partial(finish_kernel, cuts),
        out_shape=[jax.ShapeDtypeStruct(shape, F32) for shape in shapes],
        compiler_params=params(20),
        name="finish",
    )(*sums, *weights)


def lay_index():
    cell = jnp.arange(CELLS, dtype=jnp.int32)
    row, col = cell // GRID, cell % GRID
    row_gap = jnp.minimum(jnp.abs(row[:, None] - row[None, :]), LQ - 1)
    col_gap = jnp.minimum(jnp.abs(col[:, None] - col[None, :]), LQ - 1)
    real = (cell < PATCHES)[:, None] & (cell < PATCHES)[None, :]
    return jnp.where(real, row_gap * LQ + col_gap, LQ * LQ)


def body(
    text_in, patch_in, cot_text, cot_patch, text_count, intersection, text_cell,
    wq, wk, wv, wo_t, gain_one, w_gate, w_up, w_down_t, gain_two, bias_table,
):
    chips = Chips()
    me = lax.axis_index("dp")
    text_slots, model = text_in.shape[1:]
    patch_slots = patch_in.shape[1]
    rows_count = text_slots + patch_slots
    live_slots = (PATCHES + 15) // 16 * 16
    width = wq.shape[1]
    hidden = w_gate.shape[1]

    count = lax.dynamic_slice_in_dim(text_count, me, 1, 0)
    place = lax.dynamic_index_in_dim(text_cell, me, 0, keepdims=False)
    slot = jnp.arange(rows_count, dtype=jnp.int32)
    is_text, live = slot < count, slot < count + PATCHES
    patch_id = jnp.arange(live_slots, dtype=jnp.int32)
    covers = jnp.zeros((rows_count, live_slots), F32)
    for k in range(intersection.shape[1]):
        listed = jnp.pad(intersection[0, k], (0, patch_slots))
        covers = covers + (listed[:, None] == patch_id).astype(F32)
    pick = ((slot - count)[:, None] == patch_id) & (patch_id < PATCHES)
    spread = jnp.where(is_text[:, None] & (patch_id < PATCHES), covers, pick.astype(F32))
    spread = spread.astype(BF16)
    pick = pick.astype(BF16)

    cell = jnp.pad(place[0] * GRID + place[1], (0, patch_slots))
    cell = jnp.where(is_text, cell, slot - count)
    feature = jnp.arange(CELLS, dtype=jnp.int32)
    key_tile = slot // 128 + TILE0
    cells = (live[:, None] & (cell[:, None] == feature) & (feature < PATCHES)).astype(BF16)
    cells = cells + (key_tile[:, None] == feature).astype(BF16)
    cells = cells + (~live[:, None] & (feature == DEAD)).astype(BF16)
    feature = feature[:FEAT_ROWS, None]
    cells_t = (live & (cell == feature) & (feature < PATCHES)) | (key_tile == feature)
    cells_t = cells_t.astype(BF16)
    lay = lay_index()
    table = bias_table.astype(F32)

    cut = hidden // 3 // 256 * 256 + 256
    gains = jnp.pad(jnp.stack([gain_one, gain_two], axis=1), ((0, 0), (0, 126)))
    sent = []
    qkv, layers, planes, corners = chips.gather_rows(
        jnp.concatenate([wq, wk, wv, gains], axis=1),
        aside=lambda layers: (sent.append(send_half(patch_in[0, :live_slots], layers)), sent[0])[1:],
    )
    sent = sent or [send_half(patch_in[0, :live_slots])]
    patches = join_halves(sent[0])
    first_set, layers, planes, _ = chips.gather_rows(
        jnp.concatenate([wo_t, w_gate[:, :cut], w_up[:, :cut], w_down_t[:, :cut]], axis=1),
        planes, corners,
    )
    patch_cot = join_halves(send_half(cot_patch[0, :live_slots], layers))
    last_set = lax.all_gather(
        tie(jnp.concatenate([w_gate[:, cut:], w_up[:, cut:], w_down_t[:, cut:]], axis=1), *corners),
        "dp", axis=0, tiled=True,
    )
    rows = embed(count, text_in[0], spread, patches)
    grad_ffn = embed(count, cot_text[0], pick, patch_cot, BF16)

    place = me[None].astype(jnp.int32)
    projected, normed_t, qkv, gains = project(place, rows, qkv)
    half = width // 256
    seen = attend(table, projected, cells, lay, 0, half, width)
    mixture, probs, inverse = attend(table, projected, cells, lay, half, half, width, seen, (*planes, patch_cot))
    part, wo_all = mix_out(place, mixture, first_set, model)
    hidden_rows, normed_two = middle(rows, part, other_core(part), gains)

    order = chips.order(model)
    ffn_part, grad_part, grads_one = ffn(
        place, normed_two, grad_ffn, first_set, width, cut, order
    )
    ffn_part, grad_part, grads_two = ffn(
        place, normed_two, grad_ffn, (last_set,), 0, hidden - cut, order, (ffn_part, grad_part)
    )
    scatter = lambda a, groups: lax.psum_scatter(
        a, "dp", scatter_dimension=0, axis_index_groups=groups, tiled=True
    )
    sum_one, sum_two = scatter(grads_one, chips.planes), scatter(grads_two, chips.planes)
    grad_attn, grad_mix, wo_grad = after_ffn(
        hidden_rows, grad_part, other_core(grad_part), grad_ffn, gains, wo_all, mixture, order
    )
    sum_one = chips.exchange(tie(sum_one, grad_mix), chips.columns)
    args = (projected, grad_mix, mixture, probs, inverse, cells, cells_t, lay, normed_t, qkv)
    normed_a, grads_a, table_part = heads_back(
        *args, 0, half, order, chips.plane, jnp.zeros((16, 128), F32), wo_grad
    )
    sum_a = chips.exchange(grads_a.reshape(model, -1), chips.planes).astype(BF16)
    normed_part, grads_b, _ = heads_back(
        *args, half, half, order, chips.plane, table_part, normed_a, (sum_one,)
    )
    sum_two = scatter(tie(jnp.concatenate([sum_two, sum_a], axis=1), normed_part), chips.columns)
    ffn_other = other_core(ffn_part)
    text_grad, patch_grad = last(
        count, rows, normed_part, other_core(normed_part), grad_attn, gains, spread, text_slots
    )
    sum_b = chips.trade(grads_b, chips.planes, (patch_grad,))
    chunk = model // chips.plane
    layers = chips.sizes[0]
    table_rows = split_table(sum_b[chunk:])
    sum_b = sum_b[:chunk].astype(BF16).reshape(layers, chunk // layers, -1)
    sum_b = jnp.concatenate([sum_b, jnp.broadcast_to(table_rows, (layers,) + table_rows.shape)], axis=1)
    text_out, patch_out = result(
        count, hidden_rows, ffn_part, ffn_other, pick, text_slots, (sum_b,)
    )
    sum_b = chips.trade(sum_b, chips.columns, (patch_out,))
    sum_b, table_sum = sum_b[: chunk // layers], sum_b[chunk // layers :]
    table_sum = table_sum[:, :48] + table_sum[:, 128 : 128 + 48]
    table_sum = table_sum.reshape(16, 3, 16)[:, :, : table.shape[1]].transpose(1, 0, 2).reshape(table.shape)
    fill = lambda a: jnp.pad(a, ((0, patch_slots - live_slots), (0, 0)))
    patch_grad = fill(join_halves(send_half(patch_grad)))
    patch_out = fill(join_halves(send_half(patch_out)))

    *sums, own = finish(
        (sum_one, sum_two, sum_b), (wq, wk, wv, w_gate, w_up), (cut, hidden - cut), width
    )
    wq_sum, wk_sum, wv_sum, wo_sum, gate_sum, up_sum, down_sum = sums
    own = (own + other_core(own))[:, :2] / jnp.stack([gain_one, gain_two], axis=1).astype(F32)
    return (
        text_out[None], patch_out[None], text_grad[None], patch_grad[None],
        wq_sum, wk_sum, wv_sum, wo_sum, own[:, 0], gate_sum, up_sum, down_sum, own[:, 1],
        table_sum,
    )


def split_table(rows):
    values = rows[:, :128] + rows[:, 128:256]
    high = values.astype(BF16)
    low = (values - high.astype(F32)).astype(BF16)
    return jnp.concatenate([high, low, jnp.zeros((16, rows.shape[1] - 256), BF16)], axis=1)


def solution(mesh):
    page, weight, vector = P("dp", None, None), P("dp", "mp"), P("dp")
    return jax.shard_map(
        body,
        mesh=mesh,
        in_specs=(page,) * 4
        + (P(), page, P())
        + (weight,) * 4
        + (vector,)
        + (weight,) * 3
        + (vector, P(None, "mp")),
        out_specs=(page,) * 4
        + (weight,) * 4
        + (vector,)
        + (weight,) * 3
        + (vector, P(None, "mp")),
        check_vma=False,
    )
```

```python
import functools

import jax
import jax.numpy as jnp
from jax import lax
from jax.experimental import pallas as pl
from jax.experimental.pallas import tpu as pltpu
from jax.sharding import PartitionSpec as P

DH = 64
RB = 32
LQ = 4
GRID = 14
PATCHES = 196
EPS = 1e-06

BQ = 256
PAD = 128
WIN = BQ + 2 * PAD
CELLS = 256
TILE0 = PATCHES
DEAD = 206
FEAT_ROWS = 208
MASKED = -1e30
ATTEND_WEIGHT = 4
STREAMED = ("after_ffn", "result", "last")
F32 = jnp.float32
BF16 = jnp.bfloat16


def nt(left, right):
    return lax.dot_general(left, right, (((1,), (1,)), ((), ())), preferred_element_type=F32)


def nn(left, right):
    return lax.dot_general(left, right, (((1,), (0,)), ((), ())), preferred_element_type=F32)


def tn(left, right):
    return lax.dot_general(left, right, (((0,), (0,)), ((), ())), preferred_element_type=F32)


def params(mebibytes):
    return pltpu.CompilerParams(vmem_limit_bytes=mebibytes * 1024 * 1024)


def grid_of(devices):
    side = max(1, round((devices / 4) ** 0.5))
    return (devices // (side * side), side, side)


class Chips:
    def __init__(self):
        self.count = lax.axis_size("dp")
        self.sizes = grid_of(self.count)
        self.plane = self.sizes[1] * self.sizes[2]
        self.strides = (self.plane, self.sizes[2], 1)
        self.me = lax.axis_index("dp")
        layers = range(self.sizes[0])
        self.planes = [[z * self.plane + i for i in range(self.plane)] for z in layers]
        self.columns = [[z * self.plane + i for z in layers] for i in range(self.plane)]

    def send(self, block, axis, distance):
        size, stride = self.sizes[axis], self.strides[axis]
        route = []
        for i in range(self.count):
            c = (i // stride) % size
            route.append((i, i + ((c + distance) % size - c) * stride))
        return lax.ppermute(block, "dp", route)

    def gather_rows(self, block, after=(), plane_after=(), aside=None):
        block = tie(block, *after)
        if self.sizes[1:] != (2, 2):
            whole = lax.all_gather(block, "dp", axis=0, tiled=True)
            return (whole,), (block,), (block,), (block,)
        half = block.shape[0] // 2
        layers = tuple(self.send(block, 0, k) for k in range(1, self.sizes[0]))
        own = jnp.stack((block,) + layers)
        own = tie(own, *plane_after)
        by_x, by_y = self.send(own, 2, 1), self.send(own, 1, 1)
        waits = () if aside is None else aside(layers)
        far_top = self.send(tie(by_y[:, :half], *waits), 2, 1)
        far_low = self.send(by_x[:, half:], 1, 1)
        return (own, by_x, by_y, far_top, far_low), layers, (by_x, by_y), (far_top, far_low)

    def order(self, rows):
        part = rows // self.count
        return [(z * self.plane + i) * part for i in range(self.plane) for z in range(self.sizes[0])]

    def exchange(self, block, groups):
        heard = lax.all_to_all(block, "dp", 0, 0, axis_index_groups=groups, tiled=True)
        count = len(groups[0])
        heard = heard.reshape(count, block.shape[0] // count, block.shape[1])
        total = heard[0].astype(F32)
        for i in range(1, count):
            total = total + heard[i].astype(F32)
        return total


    def trade(self, block, groups, after=()):
        count = block.shape[0]
        at = self.me % self.plane if groups is self.planes else self.me // self.plane
        total = tie(lax.dynamic_index_in_dim(block, at, 0, keepdims=False), *after).astype(F32)
        for k in range(1, count):
            part = lax.dynamic_index_in_dim(block, at ^ k, 0, keepdims=False)
            route = [(g[i], g[i ^ k]) for g in groups for i in range(count)]
            total = total + lax.ppermute(part, "dp", route).astype(F32)
        return total


def tie_kernel(*refs):
    pass


def tie(block, *others):
    if not others:
        return block
    anywhere = pl.BlockSpec(memory_space=pl.ANY)
    return pl.pallas_call(
        tie_kernel,
        in_specs=[anywhere] * (1 + len(others)),
        out_specs=anywhere,
        out_shape=jax.ShapeDtypeStruct(block.shape, block.dtype),
        input_output_aliases={0: 0},
        name="tie",
    )(block, *others)


def load_parts(me, parts, columns, target, sems):
    copy = pltpu.make_async_copy
    if len(parts) == 1:
        return [copy(parts[0].at[:, columns], target, sems.at[0])]
    z, y, x = me[0] // 4, lax.rem(me[0] // 2, 2), lax.rem(me[0], 2)
    layers, rows = parts[0].shape[:2]
    places = (2 * y + x, 2 * y + 1 - x, 2 * (1 - y) + x) + (2 * (1 - y) + 1 - x,) * 2
    copies = []
    for k in range(layers):
        layer = lax.rem(z - k + layers, layers)
        for i, (part, place) in enumerate(zip(parts, places)):
            start = (layer * 4 + place) * rows + (rows // 2 if i == 4 else 0)
            rows_at = pl.ds(pl.multiple_of(start, rows // 2), part.shape[1])
            copies.append(copy(part.at[k, :, columns], target.at[rows_at], sems.at[len(copies)]))
    return copies


PARTS = 20


def other_core(block):
    return lax.ppermute(block, "mp", [(0, 1), (1, 0)])


def send_half(block, after=()):
    count = lax.axis_size("dp")
    route = [(i, (i + count // 2) % count) for i in range(count)]
    rows = block.shape[0] // 2
    core = lax.axis_index("mp")
    mine = tie(lax.dynamic_slice_in_dim(block, core * rows, rows, 0), *after)
    return lax.ppermute(mine, "dp", route)


def join_halves(mine):
    theirs = other_core(mine)
    first = lax.axis_index("mp") == 0
    return jnp.concatenate([jnp.where(first, mine, theirs), jnp.where(first, theirs, mine)], axis=0)


SCALAR = pl.BlockSpec(memory_space=pltpu.SMEM)


def attend_kernel(first, extra, table, q_ref, k_ref, v_ref, cells_ref, lay_ref, *refs):
    mix_ref, prob_to, inv_ref, keys, values, layout, near, prob_ref, sems, *score = refs[extra:]
    step = pl.program_id(0)
    pair = step + first
    length = k_ref.shape[0]
    keys[:, :128] = k_ref[...]
    keys[:, 128:] = cells_ref[...]
    values_t = v_ref[...].astype(F32).T.astype(BF16)
    for h in range(2):
        values[h, :DH] = values_t[h * DH : (h + 1) * DH]
        values[h, DH:] = jnp.ones((16, length), BF16)
    gap = WIN - lax.broadcasted_iota(jnp.int32, (8, BQ + WIN), 1) - PAD
    gap = jnp.clip(gap, -(RB // 2), RB // 2 - 1) + RB // 2
    for h in range(2):
        head = pair * 2 + h
        lay = lay_ref[...]
        grid = jnp.zeros(lay.shape, F32)
        for b in range(LQ * LQ):
            grid = jnp.where(lay == b, table[RB + b, head], grid)
        layout[h] = grid.astype(BF16)
        line = jnp.zeros(gap.shape, F32)
        for b in range(RB):
            line = jnp.where(gap == b, table[b, head], line)
        spread = jnp.broadcast_to(line[:1], (WIN, BQ + WIN))
        near[h] = pltpu.roll(spread, 0, 1, stride=1, stride_axis=0)[:, WIN:]

    lane = lax.broadcasted_iota(jnp.int32, (1, 128), 1)
    feature = lax.broadcasted_iota(jnp.int32, (1, CELLS), 1)
    tile = feature - TILE0
    is_tile = (tile >= 0) & (tile < 10)

    def fill(item, buffer):
        block, h = divmod(item, 2)
        start, head = block * BQ, pair * 2 + h
        rows = slice(start, start + BQ)
        left = is_tile & ((tile + 2) * 128 <= start)
        right = is_tile & (tile * 128 >= start + BQ + PAD)
        far = jnp.where(left, table[0, head], jnp.where(right, table[RB - 1, head], 0.0))
        far = jnp.where(feature == DEAD, MASKED, far)
        bias = (nn(cells_ref[rows], layout[h]) + far).astype(BF16)
        mine = jnp.where((lane // DH) == h, q_ref[rows] * DH ** (-0.5), 0.0).astype(BF16)
        buffer[...] = nt(keys[...], jnp.concatenate([mine, bias], axis=1))
        low, high = max(start - PAD, 0), min(start + BQ + PAD, length)
        shift = low - (start - PAD)
        buffer[low:high] += near[h, shift : shift + high - low]

    def use(item, buffer):
        block, h = divmod(item, 2)
        scores = buffer[...]
        top = jnp.max(scores, axis=0, keepdims=True)
        weight = jnp.exp(scores - top).astype(BF16)
        prob_ref[step, h, block] = weight
        out_copy(step, h, block).start()
        summed = nn(values[h], weight)
        inverse = 1.0 / summed[DH : DH + 1]
        inv_ref[h, :, block * BQ : (block + 1) * BQ] = inverse
        return summed[:DH] * inverse

    def out_copy(at, h, block):
        place = prob_to.at[2 * (first + at) + h, block]
        return pltpu.make_async_copy(prob_ref.at[at, h, block], place, sems.at[at, h, block])

    items = 2 * (length // BQ)
    depth = len(score)
    for item in range(min(depth - 1, items)):
        fill(item, score[item % depth])
    mixed = []
    for item in range(items):
        if item + depth - 1 < items:
            fill(item + depth - 1, score[(item + depth - 1) % depth])
        mixed.append(use(item, score[item % depth]))
        if item % 2:
            start = item // 2 * BQ
            mix_ref[start : start + BQ] = jnp.concatenate(mixed[-2:], axis=0).T.astype(BF16)

    @pl.when(step == pl.num_programs(0) - 1)
    def _():
        for at in range(prob_ref.shape[0]):
            for item in range(items):
                out_copy(at, item % 2, item // 2).wait()


def attend(table, projected, cells, lay, first, pairs, width, into=(), after=()):
    rows = projected.shape[0]
    blocks, all_pairs = rows // BQ, width // 128
    pair_spec = lambda i: pl.BlockSpec((rows, 128), lambda p: (0, i * all_pairs + first + p))
    anywhere = pl.BlockSpec(memory_space=pl.ANY)
    extra = len(into) + len(after)
    return pl.pallas_call(
        functools.partial(attend_kernel, first, extra),
        grid=(pairs,),
        in_specs=[
            pl.BlockSpec(memory_space=pltpu.SMEM),
            pair_spec(0),
            pair_spec(1),
            pair_spec(2),
            pl.BlockSpec((rows, CELLS), lambda p: (0, 0)),
            pl.BlockSpec((CELLS, CELLS), lambda p: (0, 0)),
        ]
        + [anywhere] * extra,
        out_specs=[
            pair_spec(0),
            anywhere,
            pl.BlockSpec((2, 1, rows), lambda p: (first + p, 0, 0)),
        ],
        out_shape=[
            jax.ShapeDtypeStruct((rows, width), BF16),
            jax.ShapeDtypeStruct((2 * all_pairs, blocks, rows, BQ), BF16),
            jax.ShapeDtypeStruct((2 * all_pairs, 1, rows), F32),
        ],
        input_output_aliases={6 + i: i for i in range(len(into))},
        scratch_shapes=[
            pltpu.VMEM((rows, 128 + CELLS), BF16),
            pltpu.VMEM((2, DH + 16, rows), BF16),
            pltpu.VMEM((2, CELLS, CELLS), BF16),
            pltpu.VMEM((2, WIN, BQ), F32),
            pltpu.VMEM((pairs, 2, blocks, rows, BQ), BF16),
            pltpu.SemaphoreType.DMA((pairs, 2, blocks)),
        ]
        + [pltpu.VMEM((rows, BQ), F32)] * 3,
        compiler_params=params(36),
        cost_estimate=pl.CostEstimate(
            flops=2 * 2 * pairs * rows * rows * 512 * 3 * ATTEND_WEIGHT,
            bytes_accessed=2 * 2 * pairs * rows * rows,
            transcendentals=2 * pairs * rows * rows,
        ),
        name="attend",
    )(table, projected, projected, projected, cells, lay, *into, *after)


def heads_back_kernel(
    order, first, starts, q_ref, k_ref, v_ref, gm_ref, mix_ref, inv_ref, cells_ref, cells_t_ref, lay_ref,
    table_in, prob_from, rows_from, weights_from, more_from, *refs
):
    out_to, sums_to, table_ref = refs[-23:-20]
    left, queries, grads, query_acc, key_acc, value_acc, by_cell, near_acc = refs[-20:-12]
    prob_ref, found, rows_t, weights, more, out, sums, prob_sems, sems = refs[-12:-3]
    buffers = refs[-3:]
    step = pl.program_id(0)
    copy = pltpu.make_async_copy
    length = k_ref.shape[0]
    blocks = length // BQ
    half = found.shape[2]

    def prob_copy(at, h, block):
        place = prob_from.at[2 * (first + at) + h, block]
        return copy(place, prob_ref.at[at, h, block], prob_sems.at[at, h, block])

    loads = [copy(rows_from, rows_t, sems.at[0]), copy(more_from, more, sems.at[1])] + [
        copy(weights_from.at[:, start : start + half], weights.at[i], sems.at[2 + i])
        for i, start in enumerate(starts)
    ]

    @pl.when(step == 0)
    def _():
        for at in range(prob_ref.shape[0]):
            for item in range(2 * blocks):
                prob_copy(at, item % 2, item // 2).start()
        for load in loads:
            load.start()
        table_ref[...] = table_in[...]

    keys_t = k_ref[...].astype(F32).T.astype(BF16)
    queries[...] = q_ref[...].astype(F32).T.astype(BF16)
    grad_mix = gm_ref[...].astype(F32)
    grad_mix_t = grad_mix.T
    weighted_t = (grad_mix * mix_ref[...].astype(F32)).T
    inner = []
    for h in range(2):
        own = slice(h * DH, (h + 1) * DH)
        left[h, :DH] = keys_t[own]
        left[h, DH:] = cells_t_ref[...]
        inverse = inv_ref[h]
        grads[h] = jnp.zeros(grads.shape[1:], BF16)
        grads[h, own] = (grad_mix_t[own] * inverse).astype(BF16)
        inner.append(jnp.sum(weighted_t[own], axis=0, keepdims=True) * inverse)

    def fill(item, buffer):
        block, h = divmod(item, 2)
        buffer[...] = nn(v_ref[...], grads[h, :, block * BQ : (block + 1) * BQ])

    far_left, far_right = [[], []], [[], []]

    def use(item, buffer):
        block, h = divmod(item, 2)
        start = block * BQ
        cols = slice(start, start + BQ)
        own = slice(h * DH, (h + 1) * DH)
        prob_copy(step, h, block).wait()
        prob = prob_ref[step, h, block]
        grad_score = (prob.astype(F32) * (buffer[...] - inner[h][:, cols])).astype(BF16)
        both = nn(left[h], grad_score)
        query_acc[own, cols] = both[:DH]
        by_cell[h, :, cols] = both[DH:].astype(BF16)
        tiles = both[DH + TILE0 : DH + TILE0 + length // 128]
        for t in range(length // 128):
            if (t + 2) * 128 <= start:
                far_left[h].append(tiles[t : t + 1])
            elif t * 128 >= start + BQ + PAD:
                far_right[h].append(tiles[t : t + 1])
        key_part = nt(queries[own, cols], grad_score)
        value_part = nt(grads[h, own, cols], prob)
        low, high = max(start - PAD, 0), min(start + BQ + PAD, length)
        shift = low - (start - PAD)
        part = grad_score[low:high].astype(F32)
        if block == 0:
            key_acc[own] = key_part
            value_acc[own] = value_part
            near_acc[h, :shift] = jnp.zeros((shift, BQ), F32)
            near_acc[h, shift : shift + high - low] = part
        else:
            key_acc[own] += key_part
            value_acc[own] += value_part
            near_acc[h, shift : shift + high - low] += part

    items = 2 * blocks
    depth = len(buffers)
    for item in range(min(depth - 1, items)):
        fill(item, buffers[item % depth])
    for item in range(items):
        if item + depth - 1 < items:
            fill(item + depth - 1, buffers[(item + depth - 1) % depth])
        use(item, buffers[item % depth])

    place = pl.ds(pl.multiple_of(step * 128, 128), 128)
    found[0, :, place] = (query_acc[...].T * DH ** (-0.5)).astype(BF16)
    found[1, :, place] = (key_acc[...].T * DH ** (-0.5)).astype(BF16)
    found[2, :, place] = value_acc[...].T.astype(BF16)
    turn = lax.broadcasted_iota(jnp.int32, (BQ, BQ), 0) + lax.broadcasted_iota(jnp.int32, (BQ, BQ), 1)
    turn = (turn == BQ - 1).astype(BF16)
    column = lax.broadcasted_iota(jnp.int32, (1, BQ + WIN), 1)
    bucket = jnp.clip(column - (BQ - 1 + PAD), -(RB // 2), RB // 2 - 1) + RB // 2
    lower = lax.broadcasted_iota(jnp.int32, (16, 1), 0)
    table_lane = lax.broadcasted_iota(jnp.int32, (1, 128), 1)
    lay = lay_ref[:FEAT_ROWS]
    for h in range(2):
        pairs = nn(by_cell[h], cells_ref[...])
        bucket_sums = [
            jnp.sum(jnp.where(lay == b, pairs, 0.0), axis=0, keepdims=True) for b in range(LQ * LQ)
        ]
        lay_part = jnp.sum(jnp.concatenate(bucket_sums, axis=0), axis=1, keepdims=True)
        band = near_acc[h]
        high = band.astype(BF16)
        low = (band - high.astype(F32)).astype(BF16)
        band = nn(high, turn) + nn(low, turn)
        band = jnp.concatenate([band, jnp.zeros((WIN, WIN), F32)], axis=1)
        band = pltpu.roll(band, 0, 1, stride=1, stride_axis=0)
        rel = jnp.sum(band, axis=0, keepdims=True)
        rel = rel + jnp.where(column == 0, jnp.sum(sum(far_left[h]), axis=1, keepdims=True), 0.0)
        last = column == BQ + WIN - 1
        rel = rel + jnp.where(last, jnp.sum(sum(far_right[h]), axis=1, keepdims=True), 0.0)
        head = 2 * (first + step) + h
        for t, part in enumerate(
            (
                jnp.sum(jnp.where(bucket == lower, rel, 0.0), axis=1, keepdims=True),
                jnp.sum(jnp.where(bucket == lower + 16, rel, 0.0), axis=1, keepdims=True),
                lay_part,
            )
        ):
            table_ref[...] += jnp.where(table_lane == t * 16 + head, part, 0.0)

    @pl.when(step == pl.num_programs(0) - 1)
    def _():
        for load in loads:
            load.wait()
        result = nt(found[0], weights[0]) + nt(found[1], weights[1]) + nt(found[2], weights[2])
        if first:
            result = result + more[...].astype(F32)
        out[...] = result.astype(BF16)
        store = copy(out, out_to, sems.at[0])
        store.start()
        model = rows_t.shape[0]
        part = model // len(order)
        places = sums.shape[0]
        chunk = model // places
        for i in range(3):
            grad = nn(rows_t[...], found[i]).astype(BF16)
            for k, start in enumerate(order):
                place, at = divmod(k * part, chunk)
                sums[place, at : at + part, i * half : (i + 1) * half] = grad[start : start + part]
        if first:
            high = table_ref[...].astype(BF16)
            low = (table_ref[...] - high.astype(F32)).astype(BF16)
            rest = jnp.zeros((16, 3 * half - 256), BF16)
            for place in range(places):
                sums[place, chunk:] = jnp.concatenate([high, low, rest], axis=1)
        else:
            for place in range(places):
                sums[place, :, 3 * half :] = more[place * chunk : (place + 1) * chunk]
        last_store = copy(sums, sums_to, sems.at[1])
        last_store.start()
        store.wait()
        last_store.wait()


def heads_back(
    projected, grad_mix, mixture, probs, inverse, cells, cells_t, lay, rows_t, weights, first, pairs, order, plane,
    table, more, after=()
):
    rows, width = grad_mix.shape
    model = rows_t.shape[0]
    blocks, all_pairs, half = rows // BQ, width // 128, 128 * pairs
    pair_spec = lambda i: pl.BlockSpec((rows, 128), lambda p: (0, i * all_pairs + first + p))
    whole = lambda *shape: pl.BlockSpec(shape, lambda p: (0, 0))
    anywhere = pl.BlockSpec(memory_space=pl.ANY)
    if first:
        shape = (plane, model // plane + 16, 3 * half)
    else:
        shape = (plane, model // plane, 3 * half + more.shape[1])
    vmem = lambda *shape: pltpu.VMEM(shape, BF16)
    starts = [i * width + 128 * first for i in range(3)]
    return pl.pallas_call(
        functools.partial(heads_back_kernel, order, first, starts),
        grid=(pairs,),
        in_specs=[pair_spec(0), pair_spec(1), pair_spec(2), pair_spec(0), pair_spec(0)]
        + [
            pl.BlockSpec((2, 1, rows), lambda p: (first + p, 0, 0)),
            whole(rows, CELLS),
            whole(FEAT_ROWS, rows),
            whole(CELLS, CELLS),
            whole(16, 128),
        ]
        + [anywhere] * (4 + len(after)),
        out_specs=[anywhere, anywhere, whole(16, 128)],
        out_shape=[
            jax.ShapeDtypeStruct((rows, model), BF16),
            jax.ShapeDtypeStruct(shape, BF16),
            jax.ShapeDtypeStruct((16, 128), F32),
        ],
        scratch_shapes=[
            vmem(2, DH + FEAT_ROWS, rows),
            vmem(128, rows),
            vmem(2, 128, rows),
            pltpu.VMEM((128, rows), F32),
            pltpu.VMEM((128, rows), F32),
            pltpu.VMEM((128, rows), F32),
            vmem(2, FEAT_ROWS, rows),
            pltpu.VMEM((2, WIN, BQ), F32),
            vmem(pairs, 2, blocks, rows, BQ),
            vmem(3, rows, half),
            vmem(model, rows),
            vmem(3, model, half),
            vmem(*more.shape),
            vmem(rows, model),
            vmem(*shape),
            pltpu.SemaphoreType.DMA((pairs, 2, blocks)),
            pltpu.SemaphoreType.DMA((5,)),
        ]
        + [pltpu.VMEM((rows, BQ), F32)] * 3,
        compiler_params=params(60),
        cost_estimate=pl.CostEstimate(
            flops=2 * pairs * rows * rows * 256 * 2 + 4 * rows * model * half,
            bytes_accessed=2 * pairs * rows * rows,
            transcendentals=0,
        ),
        name="heads_back",
    )(
        projected, projected, projected, grad_mix, mixture, inverse, cells, cells_t, lay,
        table, probs, rows_t, weights, more, *after,
    )


def ffn_kernel(first, count, extra, base, hidden, order, me, x_in, g_in, *refs):
    parts, refs = refs[:count], refs[count:]
    if not first:
        out_in, grad_in = refs[:2]
    refs = refs[extra:]
    out_to, grad_to, sums_to = refs[:3]
    x, g, w, rows_t, grads_t, act_all, gate_all, up_all, out, grad, sums = refs[3:14]
    sems, sum_sems, part_sems = refs[14:17]
    total, model = x.shape
    copy = pltpu.make_async_copy
    weight = lambda i: load_parts(
        me, parts, slice(base + i * hidden, base + (i + 1) * hidden), w.at[i], part_sems.at[i]
    )
    loads = [[copy(x_in, x, sems.at[0])], weight(0), weight(1), [copy(g_in, g, sems.at[3])], weight(2)]
    if not first:
        out_old, grad_old = refs[17:19]
        loads += [[copy(out_in, out_old, sems.at[5])], [copy(grad_in, grad_old, sems.at[6])]]
    for load in sum(loads, []):
        load.start()
    loads[0][0].wait()
    rows_t[...] = x[...].astype(F32).T.astype(BF16)
    for load in sum(loads[1:4], []):
        load.wait()
    grads_t[...] = g[...].astype(F32).T.astype(BF16)
    for load in sum(loads[4:], []):
        load.wait()
    slope = (2 / jnp.pi) ** 0.5
    for cut in range(2):
        rows = slice(cut * (total // 2), (cut + 1) * (total // 2))
        gate = nn(x[rows], w[0]).astype(BF16).astype(F32)
        up = nn(x[rows], w[1]).astype(BF16).astype(F32)
        grad_act = nn(g[rows], w[2])
        square = gate * gate
        tanh = jnp.tanh(gate * (slope + slope * 0.044715 * square))
        half = 0.5 + 0.5 * tanh
        value = gate * half
        deriv = half + (0.5 * gate) * (1.0 - tanh * tanh) * (slope + 3 * 0.044715 * slope * square)
        act_all[rows] = (value * up).astype(BF16)
        gate_all[rows] = (deriv * up * grad_act).astype(BF16)
        up_all[rows] = (value * grad_act).astype(BF16)
    for cut in range(2):
        rows = slice(cut * (total // 2), (cut + 1) * (total // 2))
        out_part = nt(act_all[rows], w[2])
        grad_part = nt(gate_all[rows], w[0]) + nt(up_all[rows], w[1])
        if not first:
            out_part = out_part + out_old[rows].astype(F32)
            grad_part = grad_part + grad_old[rows].astype(F32)
        out[rows] = out_part.astype(BF16)
        grad[rows] = grad_part.astype(BF16)
    stores = [copy(grad, grad_to, sems.at[0]), copy(out, out_to, sems.at[1])]
    for store in stores:
        store.start()
    part = model // len(order)
    for i, (left, right) in enumerate(((rows_t, gate_all), (rows_t, up_all), (grads_t, act_all))):
        sums[i] = nn(left[...], right[...]).astype(BF16)
        for k, row in enumerate(order):
            store = copy(
                sums.at[i, row : row + part],
                sums_to.at[k * part : (k + 1) * part, i * hidden : (i + 1) * hidden],
                sum_sems.at[i, k],
            )
            store.start()
            stores.append(store)
    for store in stores:
        store.wait()


def ffn(me, normed, grad_ffn, parts, base, hidden, order, before=()):
    rows, model = normed.shape
    first = not before
    extra = len(before)
    anywhere = pl.BlockSpec(memory_space=pl.ANY)
    part = jax.ShapeDtypeStruct((rows, model), BF16)
    vmem = lambda *shape: pltpu.VMEM(shape, BF16)
    return pl.pallas_call(
        functools.partial(ffn_kernel, first, len(parts), extra, base, hidden, order),
        in_specs=[SCALAR] + [anywhere] * (2 + len(parts) + extra),
        out_specs=[anywhere] * 3,
        out_shape=[part, part, jax.ShapeDtypeStruct((model, 3 * hidden), BF16)],
        scratch_shapes=[vmem(rows, model)] * 2
        + [vmem(3, model, hidden)]
        + [vmem(model, rows)] * 2
        + [vmem(rows, hidden)] * 3
        + [vmem(rows, model)] * 2
        + [vmem(3, model, hidden)]
        + [pltpu.SemaphoreType.DMA((7,)), pltpu.SemaphoreType.DMA((3, len(order)))]
        + [pltpu.SemaphoreType.DMA((3, PARTS))]
        + ([] if first else [vmem(rows, model)] * 2),
        compiler_params=params(60),
        cost_estimate=pl.CostEstimate(
            flops=18 * rows * model * hidden,
            bytes_accessed=12 * model * hidden + 8 * rows * model,
            transcendentals=rows * hidden,
        ),
        name="ffn_first" if first else "ffn_last",
    )(me, normed, grad_ffn, *parts, *before)


def rows_spec(columns, limit=None):
    if limit is None:
        return pl.BlockSpec((BQ, columns), lambda r: (r, 0))
    return pl.BlockSpec((BQ, columns), lambda r: (jnp.minimum(r, limit // BQ - 1), 0))


def fixed_spec(*shape):
    return pl.BlockSpec(shape, lambda r: (0,) * len(shape))


def is_text(count):
    row = lax.broadcasted_iota(jnp.int32, (BQ, 1), 0) + pl.program_id(0) * BQ
    return row < count[0]


def row_call(kernel, name, rows, in_specs, out, scratch, flops, *operands):
    out_specs, out_shape = zip(*out)
    return pl.pallas_call(
        kernel,
        grid=(rows // BQ,),
        in_specs=in_specs,
        out_specs=out_specs,
        out_shape=[jax.ShapeDtypeStruct(*o) for o in out_shape],
        scratch_shapes=scratch,
        compiler_params=params(60 if name in STREAMED else 20),
        cost_estimate=pl.CostEstimate(flops=flops, bytes_accessed=20 * rows * 1024, transcendentals=0),
        name=name,
    )(*operands)


def embed_kernel(count, text, spread, patches, rows):
    own = jnp.where(is_text(count), text[...].astype(F32), 0.0)
    rows[...] = (own + nn(spread[...], patches[...])).astype(rows.dtype)


def embed(count, text, spread, patches, kind=F32):
    rows, slots = spread.shape
    texts, model = text.shape
    return row_call(
        embed_kernel, "embed", rows,
        [SCALAR, rows_spec(model, texts), rows_spec(slots), fixed_spec(slots, model)],
        [(rows_spec(model), ((rows, model), kind))],
        [], 2 * rows * slots * model, count, text, spread, patches,
    )[0]


def norm(rows):
    inv = lax.rsqrt(jnp.mean(rows * rows, axis=1, keepdims=True) + EPS)
    return rows * inv, inv


def norm_back(grad_normed, rows, gain):
    unit, inv = norm(rows)
    grad_unit = grad_normed * gain
    return inv * (grad_unit - unit * jnp.mean(grad_unit * unit, axis=1, keepdims=True))


def project_kernel(count, me, rows_from, *refs):
    parts = refs[:count]
    projected_to, normed_to, weights_to, gains = refs[count : count + 4]
    rows, weights, projected, normed_t, sems, part_sems = refs[count + 4 :]
    copy = pltpu.make_async_copy
    load = copy(rows_from, rows, sems.at[0])
    loads = load_parts(me, parts, slice(0, weights.shape[1]), weights, part_sems)
    load.start()
    for each in loads:
        each.start()
    for each in loads:
        each.wait()
    store = copy(weights, weights_to, sems.at[1])
    store.start()
    length, width = projected.shape
    gains[...] = weights[:, width:].astype(F32).T[:8]
    load.wait()
    stores = [store]
    for i in range(2):
        part = slice(i * length // 2, (i + 1) * length // 2)
        normed = norm(rows[part])[0] * gains[:1]
        normed_t[:, part] = normed.T.astype(BF16)
        projected[part] = nn(normed.astype(BF16), weights[:, :width]).astype(BF16)
        stores.append(copy(projected.at[part], projected_to.at[part], sems.at[2 + i]))
        stores[-1].start()
    stores.append(copy(normed_t, normed_to, sems.at[4]))
    stores[-1].start()
    for store in stores:
        store.wait()


def project(me, rows, parts):
    length, model = rows.shape
    columns = parts[0].shape[-1]
    width = columns - 128
    anywhere = pl.BlockSpec(memory_space=pl.ANY)
    return pl.pallas_call(
        functools.partial(project_kernel, len(parts)),
        in_specs=[SCALAR] + [anywhere] * (1 + len(parts)),
        out_specs=[anywhere] * 3 + [pl.BlockSpec(memory_space=pltpu.VMEM)],
        out_shape=[
            jax.ShapeDtypeStruct((length, width), BF16),
            jax.ShapeDtypeStruct((model, length), BF16),
            jax.ShapeDtypeStruct((model, columns), BF16),
            jax.ShapeDtypeStruct((8, model), F32),
        ],
        scratch_shapes=[
            pltpu.VMEM((length, model), F32),
            pltpu.VMEM((model, columns), BF16),
            pltpu.VMEM((length, width), BF16),
            pltpu.VMEM((model, length), BF16),
            pltpu.SemaphoreType.DMA((5,)),
            pltpu.SemaphoreType.DMA((PARTS,)),
        ],
        compiler_params=params(40),
        cost_estimate=pl.CostEstimate(
            flops=2 * length * model * width, bytes_accessed=16 * length * model, transcendentals=0
        ),
        name="project",
    )(me, rows, *parts)


def mix_out_kernel(count, me, mixture_from, *refs):
    parts = refs[:count]
    out_to, weight_to, mixture, weight, out, sems, part_sems = refs[count:]
    copy = pltpu.make_async_copy
    loads = load_parts(me, parts, slice(0, weight.shape[1]), weight, part_sems)
    loads.append(copy(mixture_from, mixture, sems.at[0]))
    for each in loads:
        each.start()
    for each in loads:
        each.wait()
    stores = [copy(weight, weight_to, sems.at[1])]
    stores[0].start()
    length = mixture.shape[0]
    for i in range(2):
        part = slice(i * length // 2, (i + 1) * length // 2)
        out[part] = nt(mixture[part], weight[...]).astype(BF16)
        stores.append(copy(out.at[part], out_to.at[part], sems.at[2 + i]))
        stores[-1].start()
    for store in stores:
        store.wait()


def mix_out(me, mixture, parts, model):
    length, width = mixture.shape
    anywhere = pl.BlockSpec(memory_space=pl.ANY)
    vmem = lambda *shape: pltpu.VMEM(shape, BF16)
    return pl.pallas_call(
        functools.partial(mix_out_kernel, len(parts)),
        in_specs=[SCALAR] + [anywhere] * (1 + len(parts)),
        out_specs=[anywhere] * 2,
        out_shape=[
            jax.ShapeDtypeStruct((length, model), BF16),
            jax.ShapeDtypeStruct((model, width), BF16),
        ],
        scratch_shapes=[vmem(length, width), vmem(model, width), vmem(length, model)]
        + [pltpu.SemaphoreType.DMA((4,)), pltpu.SemaphoreType.DMA((PARTS,))],
        compiler_params=params(24),
        cost_estimate=pl.CostEstimate(
            flops=2 * length * model * width, bytes_accessed=4 * length * model, transcendentals=0
        ),
        name="mix_out",
    )(me, mixture, *parts)


def middle_kernel(rows, own, other, gains, hidden, normed):
    total = rows[...] + (own[...].astype(F32) + other[...].astype(F32))
    hidden[...] = total
    normed[...] = (norm(total)[0] * gains[1:2]).astype(BF16)


def middle(rows, own, other, gains):
    count, model = rows.shape
    return row_call(
        middle_kernel, "middle", count,
        [rows_spec(model)] * 3 + [fixed_spec(8, model)],
        [(rows_spec(model), ((count, model), F32)), (rows_spec(model), ((count, model), BF16))],
        [], 0, rows, own, other, gains,
    )


def after_kernel(order, hidden, own, other, grad_out, gains, weight, mixture, *refs):
    grad_attn, grad_mix, sums, acc = refs[-4:]
    step = pl.program_id(0)

    @pl.when(step == 0)
    def _():
        acc[...] = jnp.zeros(acc.shape, F32)

    grad = own[...].astype(F32) + other[...].astype(F32)
    grad = grad_out[...].astype(F32) + norm_back(grad, hidden[...], gains[1:2])
    low = grad.astype(BF16)
    grad_attn[...] = low
    grad_mix[...] = nn(low, weight[...]).astype(BF16)
    acc[...] += nn(grad.T.astype(BF16), mixture[...])

    @pl.when(step == pl.num_programs(0) - 1)
    def _():
        part = acc.shape[0] // len(order)
        for k, start in enumerate(order):
            sums[k * part : (k + 1) * part] = acc[start : start + part].astype(BF16)


def after_ffn(hidden, own, other, grad_out, gains, weights, mixture, order, after=()):
    rows, model = hidden.shape
    width = mixture.shape[1]
    return row_call(
        functools.partial(after_kernel, order), "after_ffn", rows,
        [rows_spec(model)] * 4
        + [fixed_spec(8, model), fixed_spec(model, width), rows_spec(width)]
        + [pl.BlockSpec(memory_space=pl.ANY)] * len(after),
        [
            (rows_spec(model), ((rows, model), BF16)),
            (rows_spec(width), ((rows, width), BF16)),
            (fixed_spec(model, width), ((model, width), BF16)),
        ],
        [pltpu.VMEM((model, width), F32)], 4 * rows * model * width,
        hidden, own, other, grad_out, gains, weights, mixture, *after,
    )


def last_kernel(count, rows, own, other, grad, gains, spread, *refs):
    text_grad, patch_grad, acc = refs[-3:]
    step = pl.program_id(0)

    @pl.when(step == 0)
    def _():
        acc[...] = jnp.zeros(acc.shape, F32)

    total = own[...].astype(F32) + other[...].astype(F32)
    total = grad[...].astype(F32) + norm_back(total, rows[...], gains[:1])

    @pl.when(step < pl.num_programs(0) - 1)
    def _():
        text_grad[...] = jnp.where(is_text(count), total, 0.0).astype(BF16)

    high = total.astype(BF16)
    low = (total - high.astype(F32)).astype(BF16)
    places = spread[...].astype(F32).T.astype(BF16)
    acc[...] += nn(places, high) + nn(places, low)

    @pl.when(step == pl.num_programs(0) - 1)
    def _():
        patch_grad[...] = acc[...].astype(BF16)


def last(count, rows, own, other, grad, gains, spread, texts, after=()):
    length, model = rows.shape
    slots = spread.shape[1]
    return row_call(
        last_kernel, "last", length,
        [SCALAR] + [rows_spec(model)] * 4 + [fixed_spec(8, model), rows_spec(slots)]
        + [pl.BlockSpec(memory_space=pl.ANY)] * len(after),
        [(rows_spec(model, texts), ((texts, model), BF16)), (fixed_spec(slots, model), ((slots, model), BF16))],
        [pltpu.VMEM((slots, model), F32)], 4 * length * model * slots,
        count, rows, own, other, grad, gains, spread, *after,
    )


def result_kernel(count, hidden, own, other, pick, *refs):
    text_out, patch_out, acc = refs[-3:]
    step = pl.program_id(0)

    @pl.when(step == 0)
    def _():
        acc[...] = jnp.zeros(acc.shape, F32)

    total = hidden[...] + (own[...].astype(F32) + other[...].astype(F32))

    @pl.when(step < pl.num_programs(0) - 1)
    def _():
        text_out[...] = jnp.where(is_text(count), total, 0.0).astype(BF16)

    acc[...] += nn(pick[...].astype(F32).T.astype(BF16), total.astype(BF16))

    @pl.when(step == pl.num_programs(0) - 1)
    def _():
        patch_out[...] = acc[...].astype(BF16)


def result(count, hidden, own, other, pick, texts, after=()):
    length, model = hidden.shape
    slots = pick.shape[1]
    return row_call(
        result_kernel, "result", length,
        [SCALAR] + [rows_spec(model)] * 3 + [rows_spec(slots)]
        + [pl.BlockSpec(memory_space=pl.ANY)] * len(after),
        [(rows_spec(model, texts), ((texts, model), BF16)), (fixed_spec(slots, model), ((slots, model), BF16))],
        [pltpu.VMEM((slots, model), F32)], 2 * length * model * slots,
        count, hidden, own, other, pick, *after,
    )


def finish_kernel(cuts, ffn_one, ffn_two, heads_a, heads, wq, wk, wv, w_gate, w_up, *outs):
    part, width = wq.shape
    half = width // 2
    start = 0
    for size, source in zip(cuts, (ffn_one, ffn_two)):
        for i, out in enumerate(outs[4:7]):
            out[:, start : start + size] = source[:, i * size : (i + 1) * size].astype(F32)
        start += size
    for i, out in enumerate(outs[:3]):
        out[:, :half] = heads_a[:, i * half : (i + 1) * half].astype(F32)
        out[:, half:] = heads[:, i * half : (i + 1) * half].astype(F32)
    outs[3][...] = heads_a[:, 3 * half :].astype(F32)
    total = lambda w, out: jnp.sum(w[...].astype(F32) * out[...], axis=1, keepdims=True)
    one = total(wq, outs[0]) + total(wk, outs[1]) + total(wv, outs[2])
    two = total(w_gate, outs[4]) + total(w_up, outs[5])
    lane = lax.broadcasted_iota(jnp.int32, (part, 128), 1)
    outs[7][...] = jnp.where(lane == 0, one, jnp.where(lane == 1, two, 0.0))


def finish(sums, weights, cuts, width):
    part, hidden = weights[-1].shape
    shapes = [(part, width)] * 4 + [(part, hidden)] * 3 + [(part, 128)]
    return pl.pallas_call(
        functools.partial(finish_kernel, cuts),
        out_shape=[jax.ShapeDtypeStruct(shape, F32) for shape in shapes],
        compiler_params=params(20),
        name="finish",
    )(*sums, *weights)


def lay_index():
    cell = jnp.arange(CELLS, dtype=jnp.int32)
    row, col = cell // GRID, cell % GRID
    row_gap = jnp.minimum(jnp.abs(row[:, None] - row[None, :]), LQ - 1)
    col_gap = jnp.minimum(jnp.abs(col[:, None] - col[None, :]), LQ - 1)
    real = (cell < PATCHES)[:, None] & (cell < PATCHES)[None, :]
    return jnp.where(real, row_gap * LQ + col_gap, LQ * LQ)


def body(
    text_in, patch_in, cot_text, cot_patch, text_count, intersection, text_cell,
    wq, wk, wv, wo_t, gain_one, w_gate, w_up, w_down_t, gain_two, bias_table,
):
    chips = Chips()
    me = lax.axis_index("dp")
    text_slots, model = text_in.shape[1:]
    patch_slots = patch_in.shape[1]
    rows_count = text_slots + patch_slots
    live_slots = (PATCHES + 15) // 16 * 16
    width = wq.shape[1]
    hidden = w_gate.shape[1]

    count = lax.dynamic_slice_in_dim(text_count, me, 1, 0)
    place = lax.dynamic_index_in_dim(text_cell, me, 0, keepdims=False)
    slot = jnp.arange(rows_count, dtype=jnp.int32)
    is_text, live = slot < count, slot < count + PATCHES
    patch_id = jnp.arange(live_slots, dtype=jnp.int32)
    covers = jnp.zeros((rows_count, live_slots), F32)
    for k in range(intersection.shape[1]):
        listed = jnp.pad(intersection[0, k], (0, patch_slots))
        covers = covers + (listed[:, None] == patch_id).astype(F32)
    pick = ((slot - count)[:, None] == patch_id) & (patch_id < PATCHES)
    spread = jnp.where(is_text[:, None] & (patch_id < PATCHES), covers, pick.astype(F32))
    spread = spread.astype(BF16)
    pick = pick.astype(BF16)

    cell = jnp.pad(place[0] * GRID + place[1], (0, patch_slots))
    cell = jnp.where(is_text, cell, slot - count)
    feature = jnp.arange(CELLS, dtype=jnp.int32)
    key_tile = slot // 128 + TILE0
    cells = (live[:, None] & (cell[:, None] == feature) & (feature < PATCHES)).astype(BF16)
    cells = cells + (key_tile[:, None] == feature).astype(BF16)
    cells = cells + (~live[:, None] & (feature == DEAD)).astype(BF16)
    feature = feature[:FEAT_ROWS, None]
    cells_t = (live & (cell == feature) & (feature < PATCHES)) | (key_tile == feature)
    cells_t = cells_t.astype(BF16)
    lay = lay_index()
    table = bias_table.astype(F32)

    cut = hidden // 3 // 256 * 256 + 256
    gains = jnp.pad(jnp.stack([gain_one, gain_two], axis=1), ((0, 0), (0, 126)))
    sent = []
    qkv, layers, planes, corners = chips.gather_rows(
        jnp.concatenate([wq, wk, wv, gains], axis=1),
        aside=lambda layers: (sent.append(send_half(patch_in[0, :live_slots], layers)), sent[0])[1:],
    )
    sent = sent or [send_half(patch_in[0, :live_slots])]
    patches = join_halves(sent[0])
    first_set, layers, planes, _ = chips.gather_rows(
        jnp.concatenate([wo_t, w_gate[:, :cut], w_up[:, :cut], w_down_t[:, :cut]], axis=1),
        planes, corners,
    )
    patch_cot = join_halves(send_half(cot_patch[0, :live_slots], layers))
    last_set = lax.all_gather(
        tie(jnp.concatenate([w_gate[:, cut:], w_up[:, cut:], w_down_t[:, cut:]], axis=1), *corners),
        "dp", axis=0, tiled=True,
    )
    rows = embed(count, text_in[0], spread, patches)
    grad_ffn = embed(count, cot_text[0], pick, patch_cot, BF16)

    place = me[None].astype(jnp.int32)
    projected, normed_t, qkv, gains = project(place, rows, qkv)
    half = width // 256
    seen = attend(table, projected, cells, lay, 0, half, width)
    mixture, probs, inverse = attend(table, projected, cells, lay, half, half, width, seen, (*planes, patch_cot))
    part, wo_all = mix_out(place, mixture, first_set, model)
    hidden_rows, normed_two = middle(rows, part, other_core(part), gains)

    order = chips.order(model)
    ffn_part, grad_part, grads_one = ffn(
        place, normed_two, grad_ffn, first_set, width, cut, order
    )
    ffn_part, grad_part, grads_two = ffn(
        place, normed_two, grad_ffn, (last_set,), 0, hidden - cut, order, (ffn_part, grad_part)
    )
    scatter = lambda a, groups: lax.psum_scatter(
        a, "dp", scatter_dimension=0, axis_index_groups=groups, tiled=True
    )
    sum_one, sum_two = scatter(grads_one, chips.planes), scatter(grads_two, chips.planes)
    grad_attn, grad_mix, wo_grad = after_ffn(
        hidden_rows, grad_part, other_core(grad_part), grad_ffn, gains, wo_all, mixture, order
    )
    sum_one = chips.exchange(tie(sum_one, grad_mix), chips.columns)
    args = (projected, grad_mix, mixture, probs, inverse, cells, cells_t, lay, normed_t, qkv)
    normed_a, grads_a, table_part = heads_back(
        *args, 0, half, order, chips.plane, jnp.zeros((16, 128), F32), wo_grad
    )
    ffn_part = tie(ffn_part, grad_mix)
    text_out, patch_out = result(
        count, hidden_rows, ffn_part, other_core(ffn_part), pick, text_slots, (normed_a,)
    )
    patch_sent = send_half(patch_out)
    sum_two = scatter(tie(sum_two, patch_out), chips.columns)
    sum_a = chips.exchange(tie(grads_a.reshape(model, -1), patch_out), chips.planes).astype(BF16)
    normed_part, grads_b, _ = heads_back(
        *args, half, half, order, chips.plane, table_part, normed_a, (sum_one, patch_out)
    )
    grads_b = tie(grads_b, sum_a)
    sum_a = scatter(tie(sum_a, normed_part), chips.columns)
    text_grad, patch_grad = last(
        count, rows, normed_part, other_core(normed_part), grad_attn, gains, spread, text_slots
    )
    patch_grad = send_half(patch_grad)
    sum_b = chips.trade(grads_b, chips.planes, (text_grad, patch_sent))
    chunk = model // chips.plane
    layers = chips.sizes[0]
    table_rows = split_table(sum_b[chunk:])
    sum_b = sum_b[:chunk].astype(BF16).reshape(layers, chunk // layers, -1)
    sum_b = jnp.concatenate([sum_b, jnp.broadcast_to(table_rows, (layers,) + table_rows.shape)], axis=1)
    sum_b = chips.trade(tie(sum_b, sum_two), chips.columns)
    sum_b, table_sum = sum_b[: chunk // layers], sum_b[chunk // layers :]
    table_sum = table_sum[:, :48] + table_sum[:, 128 : 128 + 48]
    table_sum = table_sum.reshape(16, 3, 16)[:, :, : table.shape[1]].transpose(1, 0, 2).reshape(table.shape)
    fill = lambda a: jnp.pad(a, ((0, patch_slots - live_slots), (0, 0)))
    patch_grad = fill(join_halves(tie(patch_grad, sum_b)))
    patch_out = fill(join_halves(tie(patch_sent, sum_b)))

    *sums, own = finish(
        (sum_one, sum_two, sum_a, sum_b), (wq, wk, wv, w_gate, w_up), (cut, hidden - cut), width
    )
    wq_sum, wk_sum, wv_sum, wo_sum, gate_sum, up_sum, down_sum = sums
    own = (own + other_core(own))[:, :2] / jnp.stack([gain_one, gain_two], axis=1).astype(F32)
    return (
        text_out[None], patch_out[None], text_grad[None], patch_grad[None],
        wq_sum, wk_sum, wv_sum, wo_sum, own[:, 0], gate_sum, up_sum, down_sum, own[:, 1],
        table_sum,
    )


def split_table(rows):
    values = rows[:, :128] + rows[:, 128:256]
    high = values.astype(BF16)
    low = (values - high.astype(F32)).astype(BF16)
    return jnp.concatenate([high, low, jnp.zeros((16, rows.shape[1] - 256), BF16)], axis=1)


def solution(mesh):
    page, weight, vector = P("dp", None, None), P("dp", "mp"), P("dp")
    return jax.shard_map(
        body,
        mesh=mesh,
        in_specs=(page,) * 4
        + (P(), page, P())
        + (weight,) * 4
        + (vector,)
        + (weight,) * 3
        + (vector, P(None, "mp")),
        out_specs=(page,) * 4
        + (weight,) * 4
        + (vector,)
        + (weight,) * 3
        + (vector, P(None, "mp")),
        check_vma=False,
    )
```

```python
import functools

import jax
import jax.numpy as jnp
from jax import lax
from jax.experimental import pallas as pl
from jax.experimental.pallas import tpu as pltpu
from jax.sharding import PartitionSpec as P

DH = 64
RB = 32
LQ = 4
GRID = 14
PATCHES = 196
EPS = 1e-06

BQ = 256
PAD = 128
WIN = BQ + 2 * PAD
CELLS = 256
TILE0 = PATCHES
DEAD = 206
FEAT_ROWS = 208
MASKED = -1e30
ATTEND_WEIGHT = 4
STREAMED = ("after_ffn", "result", "last")
F32 = jnp.float32
BF16 = jnp.bfloat16


def nt(left, right):
    return lax.dot_general(left, right, (((1,), (1,)), ((), ())), preferred_element_type=F32)


def nn(left, right):
    return lax.dot_general(left, right, (((1,), (0,)), ((), ())), preferred_element_type=F32)


def tn(left, right):
    return lax.dot_general(left, right, (((0,), (0,)), ((), ())), preferred_element_type=F32)


def params(mebibytes):
    return pltpu.CompilerParams(vmem_limit_bytes=mebibytes * 1024 * 1024)


def grid_of(devices):
    side = max(1, round((devices / 4) ** 0.5))
    return (devices // (side * side), side, side)


class Chips:
    def __init__(self):
        self.count = lax.axis_size("dp")
        self.sizes = grid_of(self.count)
        self.plane = self.sizes[1] * self.sizes[2]
        self.strides = (self.plane, self.sizes[2], 1)
        self.me = lax.axis_index("dp")
        layers = range(self.sizes[0])
        self.planes = [[z * self.plane + i for i in range(self.plane)] for z in layers]
        self.columns = [[z * self.plane + i for z in layers] for i in range(self.plane)]

    def send(self, block, axis, distance):
        size, stride = self.sizes[axis], self.strides[axis]
        route = []
        for i in range(self.count):
            c = (i // stride) % size
            route.append((i, i + ((c + distance) % size - c) * stride))
        return lax.ppermute(block, "dp", route)

    def gather_rows(self, block, after=(), plane_after=(), aside=None):
        block = tie(block, *after)
        if self.sizes[1:] != (2, 2):
            whole = lax.all_gather(block, "dp", axis=0, tiled=True)
            return (whole,), (block,), (block,), (block,)
        half = block.shape[0] // 2
        layers = tuple(self.send(block, 0, k) for k in range(1, self.sizes[0]))
        own = jnp.stack((block,) + layers)
        own = tie(own, *plane_after)
        by_x, by_y = self.send(own, 2, 1), self.send(own, 1, 1)
        waits = () if aside is None else aside(layers)
        far_top = self.send(tie(by_y[:, :half], *waits), 2, 1)
        far_low = self.send(by_x[:, half:], 1, 1)
        return (own, by_x, by_y, far_top, far_low), layers, (by_x, by_y), (far_top, far_low)

    def order(self, rows):
        part = rows // self.count
        return [(z * self.plane + i) * part for i in range(self.plane) for z in range(self.sizes[0])]

    def exchange(self, block, groups):
        heard = lax.all_to_all(block, "dp", 0, 0, axis_index_groups=groups, tiled=True)
        count = len(groups[0])
        heard = heard.reshape(count, block.shape[0] // count, block.shape[1])
        total = heard[0].astype(F32)
        for i in range(1, count):
            total = total + heard[i].astype(F32)
        return total


    def trade(self, block, groups, after=()):
        count = block.shape[0]
        at = self.me % self.plane if groups is self.planes else self.me // self.plane
        total = tie(lax.dynamic_index_in_dim(block, at, 0, keepdims=False), *after).astype(F32)
        for k in range(1, count):
            part = lax.dynamic_index_in_dim(block, at ^ k, 0, keepdims=False)
            route = [(g[i], g[i ^ k]) for g in groups for i in range(count)]
            total = total + lax.ppermute(part, "dp", route).astype(F32)
        return total


def tie_kernel(*refs):
    pass


def tie(block, *others):
    if not others:
        return block
    anywhere = pl.BlockSpec(memory_space=pl.ANY)
    return pl.pallas_call(
        tie_kernel,
        in_specs=[anywhere] * (1 + len(others)),
        out_specs=anywhere,
        out_shape=jax.ShapeDtypeStruct(block.shape, block.dtype),
        input_output_aliases={0: 0},
        name="tie",
    )(block, *others)


def load_parts(me, parts, columns, target, sems):
    copy = pltpu.make_async_copy
    if len(parts) == 1:
        return [copy(parts[0].at[:, columns], target, sems.at[0])]
    z, y, x = me[0] // 4, lax.rem(me[0] // 2, 2), lax.rem(me[0], 2)
    layers, rows = parts[0].shape[:2]
    places = (2 * y + x, 2 * y + 1 - x, 2 * (1 - y) + x) + (2 * (1 - y) + 1 - x,) * 2
    copies = []
    for k in range(layers):
        layer = lax.rem(z - k + layers, layers)
        for i, (part, place) in enumerate(zip(parts, places)):
            start = (layer * 4 + place) * rows + (rows // 2 if i == 4 else 0)
            rows_at = pl.ds(pl.multiple_of(start, rows // 2), part.shape[1])
            copies.append(copy(part.at[k, :, columns], target.at[rows_at], sems.at[len(copies)]))
    return copies


PARTS = 20


def other_core(block):
    return lax.ppermute(block, "mp", [(0, 1), (1, 0)])


def send_half(block, after=()):
    count = lax.axis_size("dp")
    route = [(i, (i + count // 2) % count) for i in range(count)]
    rows = block.shape[0] // 2
    core = lax.axis_index("mp")
    mine = tie(lax.dynamic_slice_in_dim(block, core * rows, rows, 0), *after)
    return lax.ppermute(mine, "dp", route)


def join_halves(mine):
    theirs = other_core(mine)
    first = lax.axis_index("mp") == 0
    return jnp.concatenate([jnp.where(first, mine, theirs), jnp.where(first, theirs, mine)], axis=0)


SCALAR = pl.BlockSpec(memory_space=pltpu.SMEM)


def attend_kernel(first, extra, table, q_ref, k_ref, v_ref, cells_ref, lay_ref, *refs):
    mix_ref, prob_to, inv_ref, keys, values, layout, near, prob_ref, sems, *score = refs[extra:]
    step = pl.program_id(0)
    pair = step + first
    length = k_ref.shape[0]
    keys[:, :128] = k_ref[...]
    keys[:, 128:] = cells_ref[...]
    values_t = v_ref[...].astype(F32).T.astype(BF16)
    for h in range(2):
        values[h, :DH] = values_t[h * DH : (h + 1) * DH]
        values[h, DH:] = jnp.ones((16, length), BF16)
    gap = WIN - lax.broadcasted_iota(jnp.int32, (8, BQ + WIN), 1) - PAD
    gap = jnp.clip(gap, -(RB // 2), RB // 2 - 1) + RB // 2
    for h in range(2):
        head = pair * 2 + h
        lay = lay_ref[...]
        grid = jnp.zeros(lay.shape, F32)
        for b in range(LQ * LQ):
            grid = jnp.where(lay == b, table[RB + b, head], grid)
        layout[h] = grid.astype(BF16)
        line = jnp.zeros(gap.shape, F32)
        for b in range(RB):
            line = jnp.where(gap == b, table[b, head], line)
        spread = jnp.broadcast_to(line[:1], (WIN, BQ + WIN))
        near[h] = pltpu.roll(spread, 0, 1, stride=1, stride_axis=0)[:, WIN:]

    lane = lax.broadcasted_iota(jnp.int32, (1, 128), 1)
    feature = lax.broadcasted_iota(jnp.int32, (1, CELLS), 1)
    tile = feature - TILE0
    is_tile = (tile >= 0) & (tile < 10)

    def fill(item, buffer):
        block, h = divmod(item, 2)
        start, head = block * BQ, pair * 2 + h
        rows = slice(start, start + BQ)
        left = is_tile & ((tile + 2) * 128 <= start)
        right = is_tile & (tile * 128 >= start + BQ + PAD)
        far = jnp.where(left, table[0, head], jnp.where(right, table[RB - 1, head], 0.0))
        far = jnp.where(feature == DEAD, MASKED, far)
        bias = (nn(cells_ref[rows], layout[h]) + far).astype(BF16)
        mine = jnp.where((lane // DH) == h, q_ref[rows] * DH ** (-0.5), 0.0).astype(BF16)
        buffer[...] = nt(keys[...], jnp.concatenate([mine, bias], axis=1))
        low, high = max(start - PAD, 0), min(start + BQ + PAD, length)
        shift = low - (start - PAD)
        buffer[low:high] += near[h, shift : shift + high - low]

    def use(item, buffer):
        block, h = divmod(item, 2)
        scores = buffer[...]
        top = jnp.max(scores, axis=0, keepdims=True)
        weight = jnp.exp(scores - top).astype(BF16)
        prob_ref[step, h, block] = weight
        out_copy(step, h, block).start()
        summed = nn(values[h], weight)
        inverse = 1.0 / summed[DH : DH + 1]
        inv_ref[h, :, block * BQ : (block + 1) * BQ] = inverse
        return summed[:DH] * inverse

    def out_copy(at, h, block):
        place = prob_to.at[2 * (first + at) + h, block]
        return pltpu.make_async_copy(prob_ref.at[at, h, block], place, sems.at[at, h, block])

    items = 2 * (length // BQ)
    depth = len(score)
    for item in range(min(depth - 1, items)):
        fill(item, score[item % depth])
    mixed = []
    for item in range(items):
        if item + depth - 1 < items:
            fill(item + depth - 1, score[(item + depth - 1) % depth])
        mixed.append(use(item, score[item % depth]))
        if item % 2:
            start = item // 2 * BQ
            mix_ref[start : start + BQ] = jnp.concatenate(mixed[-2:], axis=0).T.astype(BF16)

    @pl.when(step == pl.num_programs(0) - 1)
    def _():
        for at in range(prob_ref.shape[0]):
            for item in range(items):
                out_copy(at, item % 2, item // 2).wait()


def attend(table, projected, cells, lay, first, pairs, width, into=(), after=()):
    rows = projected.shape[0]
    blocks, all_pairs = rows // BQ, width // 128
    pair_spec = lambda i: pl.BlockSpec((rows, 128), lambda p: (0, i * all_pairs + first + p))
    anywhere = pl.BlockSpec(memory_space=pl.ANY)
    extra = len(into) + len(after)
    return pl.pallas_call(
        functools.partial(attend_kernel, first, extra),
        grid=(pairs,),
        in_specs=[
            pl.BlockSpec(memory_space=pltpu.SMEM),
            pair_spec(0),
            pair_spec(1),
            pair_spec(2),
            pl.BlockSpec((rows, CELLS), lambda p: (0, 0)),
            pl.BlockSpec((CELLS, CELLS), lambda p: (0, 0)),
        ]
        + [anywhere] * extra,
        out_specs=[
            pair_spec(0),
            anywhere,
            pl.BlockSpec((2, 1, rows), lambda p: (first + p, 0, 0)),
        ],
        out_shape=[
            jax.ShapeDtypeStruct((rows, width), BF16),
            jax.ShapeDtypeStruct((2 * all_pairs, blocks, rows, BQ), BF16),
            jax.ShapeDtypeStruct((2 * all_pairs, 1, rows), F32),
        ],
        input_output_aliases={6 + i: i for i in range(len(into))},
        scratch_shapes=[
            pltpu.VMEM((rows, 128 + CELLS), BF16),
            pltpu.VMEM((2, DH + 16, rows), BF16),
            pltpu.VMEM((2, CELLS, CELLS), BF16),
            pltpu.VMEM((2, WIN, BQ), F32),
            pltpu.VMEM((pairs, 2, blocks, rows, BQ), BF16),
            pltpu.SemaphoreType.DMA((pairs, 2, blocks)),
        ]
        + [pltpu.VMEM((rows, BQ), F32)] * 3,
        compiler_params=params(36),
        cost_estimate=pl.CostEstimate(
            flops=2 * 2 * pairs * rows * rows * 512 * 3 * ATTEND_WEIGHT,
            bytes_accessed=2 * 2 * pairs * rows * rows,
            transcendentals=2 * pairs * rows * rows,
        ),
        name="attend",
    )(table, projected, projected, projected, cells, lay, *into, *after)


def heads_back_kernel(
    order, first, starts, q_ref, k_ref, v_ref, gm_ref, mix_ref, inv_ref, cells_ref, cells_t_ref, lay_ref,
    table_in, prob_from, rows_from, weights_from, more_from, *refs
):
    out_to, sums_to, table_ref = refs[-23:-20]
    left, queries, grads, query_acc, key_acc, value_acc, by_cell, near_acc = refs[-20:-12]
    prob_ref, found, rows_t, weights, more, out, sums, prob_sems, sems = refs[-12:-3]
    buffers = refs[-3:]
    step = pl.program_id(0)
    copy = pltpu.make_async_copy
    length = k_ref.shape[0]
    blocks = length // BQ
    half = found.shape[2]

    def prob_copy(at, h, block):
        place = prob_from.at[2 * (first + at) + h, block]
        return copy(place, prob_ref.at[at, h, block], prob_sems.at[at, h, block])

    loads = [copy(rows_from, rows_t, sems.at[0]), copy(more_from, more, sems.at[1])] + [
        copy(weights_from.at[:, start : start + half], weights.at[i], sems.at[2 + i])
        for i, start in enumerate(starts)
    ]

    @pl.when(step == 0)
    def _():
        for at in range(prob_ref.shape[0]):
            for item in range(2 * blocks):
                prob_copy(at, item % 2, item // 2).start()
        for load in loads:
            load.start()
        table_ref[...] = table_in[...]

    keys_t = k_ref[...].astype(F32).T.astype(BF16)
    queries[...] = q_ref[...].astype(F32).T.astype(BF16)
    grad_mix = gm_ref[...].astype(F32)
    grad_mix_t = grad_mix.T
    weighted_t = (grad_mix * mix_ref[...].astype(F32)).T
    inner = []
    for h in range(2):
        own = slice(h * DH, (h + 1) * DH)
        left[h, :DH] = keys_t[own]
        left[h, DH:] = cells_t_ref[...]
        inverse = inv_ref[h]
        grads[h] = jnp.zeros(grads.shape[1:], BF16)
        grads[h, own] = (grad_mix_t[own] * inverse).astype(BF16)
        inner.append(jnp.sum(weighted_t[own], axis=0, keepdims=True) * inverse)

    def fill(item, buffer):
        block, h = divmod(item, 2)
        buffer[...] = nn(v_ref[...], grads[h, :, block * BQ : (block + 1) * BQ])

    far_left, far_right = [[], []], [[], []]

    def use(item, buffer):
        block, h = divmod(item, 2)
        start = block * BQ
        cols = slice(start, start + BQ)
        own = slice(h * DH, (h + 1) * DH)
        prob_copy(step, h, block).wait()
        prob = prob_ref[step, h, block]
        grad_score = (prob.astype(F32) * (buffer[...] - inner[h][:, cols])).astype(BF16)
        both = nn(left[h], grad_score)
        query_acc[own, cols] = both[:DH]
        by_cell[h, :, cols] = both[DH:].astype(BF16)
        tiles = both[DH + TILE0 : DH + TILE0 + length // 128]
        for t in range(length // 128):
            if (t + 2) * 128 <= start:
                far_left[h].append(tiles[t : t + 1])
            elif t * 128 >= start + BQ + PAD:
                far_right[h].append(tiles[t : t + 1])
        key_part = nt(queries[own, cols], grad_score)
        value_part = nt(grads[h, own, cols], prob)
        low, high = max(start - PAD, 0), min(start + BQ + PAD, length)
        shift = low - (start - PAD)
        part = grad_score[low:high].astype(F32)
        if block == 0:
            key_acc[own] = key_part
            value_acc[own] = value_part
            near_acc[h, :shift] = jnp.zeros((shift, BQ), F32)
            near_acc[h, shift : shift + high - low] = part
        else:
            key_acc[own] += key_part
            value_acc[own] += value_part
            near_acc[h, shift : shift + high - low] += part

    items = 2 * blocks
    depth = len(buffers)
    for item in range(min(depth - 1, items)):
        fill(item, buffers[item % depth])
    for item in range(items):
        if item + depth - 1 < items:
            fill(item + depth - 1, buffers[(item + depth - 1) % depth])
        use(item, buffers[item % depth])

    place = pl.ds(pl.multiple_of(step * 128, 128), 128)
    found[0, :, place] = (query_acc[...].T * DH ** (-0.5)).astype(BF16)
    found[1, :, place] = (key_acc[...].T * DH ** (-0.5)).astype(BF16)
    found[2, :, place] = value_acc[...].T.astype(BF16)
    turn = lax.broadcasted_iota(jnp.int32, (BQ, BQ), 0) + lax.broadcasted_iota(jnp.int32, (BQ, BQ), 1)
    turn = (turn == BQ - 1).astype(BF16)
    column = lax.broadcasted_iota(jnp.int32, (1, BQ + WIN), 1)
    bucket = jnp.clip(column - (BQ - 1 + PAD), -(RB // 2), RB // 2 - 1) + RB // 2
    lower = lax.broadcasted_iota(jnp.int32, (16, 1), 0)
    table_lane = lax.broadcasted_iota(jnp.int32, (1, 128), 1)
    lay = lay_ref[:FEAT_ROWS]
    for h in range(2):
        pairs = nn(by_cell[h], cells_ref[...])
        bucket_sums = [
            jnp.sum(jnp.where(lay == b, pairs, 0.0), axis=0, keepdims=True) for b in range(LQ * LQ)
        ]
        lay_part = jnp.sum(jnp.concatenate(bucket_sums, axis=0), axis=1, keepdims=True)
        band = near_acc[h]
        high = band.astype(BF16)
        low = (band - high.astype(F32)).astype(BF16)
        band = nn(high, turn) + nn(low, turn)
        band = jnp.concatenate([band, jnp.zeros((WIN, WIN), F32)], axis=1)
        band = pltpu.roll(band, 0, 1, stride=1, stride_axis=0)
        rel = jnp.sum(band, axis=0, keepdims=True)
        rel = rel + jnp.where(column == 0, jnp.sum(sum(far_left[h]), axis=1, keepdims=True), 0.0)
        last = column == BQ + WIN - 1
        rel = rel + jnp.where(last, jnp.sum(sum(far_right[h]), axis=1, keepdims=True), 0.0)
        head = 2 * (first + step) + h
        for t, part in enumerate(
            (
                jnp.sum(jnp.where(bucket == lower, rel, 0.0), axis=1, keepdims=True),
                jnp.sum(jnp.where(bucket == lower + 16, rel, 0.0), axis=1, keepdims=True),
                lay_part,
            )
        ):
            table_ref[...] += jnp.where(table_lane == t * 16 + head, part, 0.0)

    @pl.when(step == pl.num_programs(0) - 1)
    def _():
        for load in loads:
            load.wait()
        result = nt(found[0], weights[0]) + nt(found[1], weights[1]) + nt(found[2], weights[2])
        if first:
            result = result + more[...].astype(F32)
        out[...] = result.astype(BF16)
        store = copy(out, out_to, sems.at[0])
        store.start()
        model = rows_t.shape[0]
        part = model // len(order)
        places = sums.shape[0]
        chunk = model // places
        for i in range(3):
            grad = nn(rows_t[...], found[i]).astype(BF16)
            for k, start in enumerate(order):
                place, at = divmod(k * part, chunk)
                sums[place, at : at + part, i * half : (i + 1) * half] = grad[start : start + part]
        if first:
            high = table_ref[...].astype(BF16)
            low = (table_ref[...] - high.astype(F32)).astype(BF16)
            rest = jnp.zeros((16, 3 * half - 256), BF16)
            for place in range(places):
                sums[place, chunk:] = jnp.concatenate([high, low, rest], axis=1)
        else:
            for place in range(places):
                sums[place, :, 3 * half :] = more[place * chunk : (place + 1) * chunk]
        last_store = copy(sums, sums_to, sems.at[1])
        last_store.start()
        store.wait()
        last_store.wait()


def heads_back(
    projected, grad_mix, mixture, probs, inverse, cells, cells_t, lay, rows_t, weights, first, pairs, order, plane,
    table, more, after=()
):
    rows, width = grad_mix.shape
    model = rows_t.shape[0]
    blocks, all_pairs, half = rows // BQ, width // 128, 128 * pairs
    pair_spec = lambda i: pl.BlockSpec((rows, 128), lambda p: (0, i * all_pairs + first + p))
    whole = lambda *shape: pl.BlockSpec(shape, lambda p: (0, 0))
    anywhere = pl.BlockSpec(memory_space=pl.ANY)
    if first:
        shape = (plane, model // plane + 16, 3 * half)
    else:
        shape = (plane, model // plane, 3 * half + more.shape[1])
    vmem = lambda *shape: pltpu.VMEM(shape, BF16)
    starts = [i * width + 128 * first for i in range(3)]
    return pl.pallas_call(
        functools.partial(heads_back_kernel, order, first, starts),
        grid=(pairs,),
        in_specs=[pair_spec(0), pair_spec(1), pair_spec(2), pair_spec(0), pair_spec(0)]
        + [
            pl.BlockSpec((2, 1, rows), lambda p: (first + p, 0, 0)),
            whole(rows, CELLS),
            whole(FEAT_ROWS, rows),
            whole(CELLS, CELLS),
            whole(16, 128),
        ]
        + [anywhere] * (4 + len(after)),
        out_specs=[anywhere, anywhere, whole(16, 128)],
        out_shape=[
            jax.ShapeDtypeStruct((rows, model), BF16),
            jax.ShapeDtypeStruct(shape, BF16),
            jax.ShapeDtypeStruct((16, 128), F32),
        ],
        scratch_shapes=[
            vmem(2, DH + FEAT_ROWS, rows),
            vmem(128, rows),
            vmem(2, 128, rows),
            pltpu.VMEM((128, rows), F32),
            pltpu.VMEM((128, rows), F32),
            pltpu.VMEM((128, rows), F32),
            vmem(2, FEAT_ROWS, rows),
            pltpu.VMEM((2, WIN, BQ), F32),
            vmem(pairs, 2, blocks, rows, BQ),
            vmem(3, rows, half),
            vmem(model, rows),
            vmem(3, model, half),
            vmem(*more.shape),
            vmem(rows, model),
            vmem(*shape),
            pltpu.SemaphoreType.DMA((pairs, 2, blocks)),
            pltpu.SemaphoreType.DMA((5,)),
        ]
        + [pltpu.VMEM((rows, BQ), F32)] * 3,
        compiler_params=params(60),
        cost_estimate=pl.CostEstimate(
            flops=2 * pairs * rows * rows * 256 * 2 + 4 * rows * model * half,
            bytes_accessed=2 * pairs * rows * rows,
            transcendentals=0,
        ),
        name="heads_back",
    )(
        projected, projected, projected, grad_mix, mixture, inverse, cells, cells_t, lay,
        table, probs, rows_t, weights, more, *after,
    )


def ffn_kernel(first, count, extra, base, hidden, order, me, x_in, g_in, *refs):
    parts, refs = refs[:count], refs[count:]
    if not first:
        out_in, grad_in = refs[:2]
    refs = refs[extra:]
    out_to, grad_to, sums_to = refs[:3]
    x, g, w, rows_t, grads_t, act_all, gate_all, up_all, out, grad, sums = refs[3:14]
    sems, sum_sems, part_sems = refs[14:17]
    total, model = x.shape
    copy = pltpu.make_async_copy
    weight = lambda i: load_parts(
        me, parts, slice(base + i * hidden, base + (i + 1) * hidden), w.at[i], part_sems.at[i]
    )
    loads = [[copy(x_in, x, sems.at[0])], weight(0), weight(1), [copy(g_in, g, sems.at[3])], weight(2)]
    if not first:
        out_old, grad_old = refs[17:19]
        loads += [[copy(out_in, out_old, sems.at[5])], [copy(grad_in, grad_old, sems.at[6])]]
    for load in sum(loads, []):
        load.start()
    loads[0][0].wait()
    rows_t[...] = x[...].astype(F32).T.astype(BF16)
    for load in sum(loads[1:4], []):
        load.wait()
    grads_t[...] = g[...].astype(F32).T.astype(BF16)
    for load in sum(loads[4:], []):
        load.wait()
    slope = (2 / jnp.pi) ** 0.5
    for cut in range(2):
        rows = slice(cut * (total // 2), (cut + 1) * (total // 2))
        gate = nn(x[rows], w[0]).astype(BF16).astype(F32)
        up = nn(x[rows], w[1]).astype(BF16).astype(F32)
        grad_act = nn(g[rows], w[2])
        square = gate * gate
        tanh = jnp.tanh(gate * (slope + slope * 0.044715 * square))
        half = 0.5 + 0.5 * tanh
        value = gate * half
        deriv = half + (0.5 * gate) * (1.0 - tanh * tanh) * (slope + 3 * 0.044715 * slope * square)
        act_all[rows] = (value * up).astype(BF16)
        gate_all[rows] = (deriv * up * grad_act).astype(BF16)
        up_all[rows] = (value * grad_act).astype(BF16)
    for cut in range(2):
        rows = slice(cut * (total // 2), (cut + 1) * (total // 2))
        out_part = nt(act_all[rows], w[2])
        grad_part = nt(gate_all[rows], w[0]) + nt(up_all[rows], w[1])
        if not first:
            out_part = out_part + out_old[rows].astype(F32)
            grad_part = grad_part + grad_old[rows].astype(F32)
        out[rows] = out_part.astype(BF16)
        grad[rows] = grad_part.astype(BF16)
    stores = [copy(grad, grad_to, sems.at[0]), copy(out, out_to, sems.at[1])]
    for store in stores:
        store.start()
    part = model // len(order)
    for i, (left, right) in enumerate(((rows_t, gate_all), (rows_t, up_all), (grads_t, act_all))):
        sums[i] = nn(left[...], right[...]).astype(BF16)
        for k, row in enumerate(order):
            store = copy(
                sums.at[i, row : row + part],
                sums_to.at[k * part : (k + 1) * part, i * hidden : (i + 1) * hidden],
                sum_sems.at[i, k],
            )
            store.start()
            stores.append(store)
    for store in stores:
        store.wait()


def ffn(me, normed, grad_ffn, parts, base, hidden, order, before=()):
    rows, model = normed.shape
    first = not before
    extra = len(before)
    anywhere = pl.BlockSpec(memory_space=pl.ANY)
    part = jax.ShapeDtypeStruct((rows, model), BF16)
    vmem = lambda *shape: pltpu.VMEM(shape, BF16)
    return pl.pallas_call(
        functools.partial(ffn_kernel, first, len(parts), extra, base, hidden, order),
        in_specs=[SCALAR] + [anywhere] * (2 + len(parts) + extra),
        out_specs=[anywhere] * 3,
        out_shape=[part, part, jax.ShapeDtypeStruct((model, 3 * hidden), BF16)],
        scratch_shapes=[vmem(rows, model)] * 2
        + [vmem(3, model, hidden)]
        + [vmem(model, rows)] * 2
        + [vmem(rows, hidden)] * 3
        + [vmem(rows, model)] * 2
        + [vmem(3, model, hidden)]
        + [pltpu.SemaphoreType.DMA((7,)), pltpu.SemaphoreType.DMA((3, len(order)))]
        + [pltpu.SemaphoreType.DMA((3, PARTS))]
        + ([] if first else [vmem(rows, model)] * 2),
        compiler_params=params(60),
        cost_estimate=pl.CostEstimate(
            flops=18 * rows * model * hidden,
            bytes_accessed=12 * model * hidden + 8 * rows * model,
            transcendentals=rows * hidden,
        ),
        name="ffn_first" if first else "ffn_last",
    )(me, normed, grad_ffn, *parts, *before)


def rows_spec(columns, limit=None):
    if limit is None:
        return pl.BlockSpec((BQ, columns), lambda r: (r, 0))
    return pl.BlockSpec((BQ, columns), lambda r: (jnp.minimum(r, limit // BQ - 1), 0))


def fixed_spec(*shape):
    return pl.BlockSpec(shape, lambda r: (0,) * len(shape))


def is_text(count):
    row = lax.broadcasted_iota(jnp.int32, (BQ, 1), 0) + pl.program_id(0) * BQ
    return row < count[0]


def row_call(kernel, name, rows, in_specs, out, scratch, flops, *operands):
    out_specs, out_shape = zip(*out)
    return pl.pallas_call(
        kernel,
        grid=(rows // BQ,),
        in_specs=in_specs,
        out_specs=out_specs,
        out_shape=[jax.ShapeDtypeStruct(*o) for o in out_shape],
        scratch_shapes=scratch,
        compiler_params=params(60 if name in STREAMED else 20),
        cost_estimate=pl.CostEstimate(flops=flops, bytes_accessed=20 * rows * 1024, transcendentals=0),
        name=name,
    )(*operands)


def embed_kernel(count, text, spread, patches, rows):
    own = jnp.where(is_text(count), text[...].astype(F32), 0.0)
    rows[...] = (own + nn(spread[...], patches[...])).astype(rows.dtype)


def embed(count, text, spread, patches, kind=F32):
    rows, slots = spread.shape
    texts, model = text.shape
    return row_call(
        embed_kernel, "embed", rows,
        [SCALAR, rows_spec(model, texts), rows_spec(slots), fixed_spec(slots, model)],
        [(rows_spec(model), ((rows, model), kind))],
        [], 2 * rows * slots * model, count, text, spread, patches,
    )[0]


def norm(rows):
    inv = lax.rsqrt(jnp.mean(rows * rows, axis=1, keepdims=True) + EPS)
    return rows * inv, inv


def norm_back(grad_normed, rows, gain):
    unit, inv = norm(rows)
    grad_unit = grad_normed * gain
    return inv * (grad_unit - unit * jnp.mean(grad_unit * unit, axis=1, keepdims=True))


def project_kernel(count, me, rows_from, *refs):
    parts = refs[:count]
    projected_to, normed_to, weights_to, gains = refs[count : count + 4]
    rows, weights, projected, normed_t, sems, part_sems = refs[count + 4 :]
    copy = pltpu.make_async_copy
    load = copy(rows_from, rows, sems.at[0])
    loads = load_parts(me, parts, slice(0, weights.shape[1]), weights, part_sems)
    load.start()
    for each in loads:
        each.start()
    for each in loads:
        each.wait()
    store = copy(weights, weights_to, sems.at[1])
    store.start()
    length, width = projected.shape
    gains[...] = weights[:, width:].astype(F32).T[:8]
    load.wait()
    stores = [store]
    for i in range(2):
        part = slice(i * length // 2, (i + 1) * length // 2)
        normed = norm(rows[part])[0] * gains[:1]
        normed_t[:, part] = normed.T.astype(BF16)
        projected[part] = nn(normed.astype(BF16), weights[:, :width]).astype(BF16)
        stores.append(copy(projected.at[part], projected_to.at[part], sems.at[2 + i]))
        stores[-1].start()
    stores.append(copy(normed_t, normed_to, sems.at[4]))
    stores[-1].start()
    for store in stores:
        store.wait()


def project(me, rows, parts):
    length, model = rows.shape
    columns = parts[0].shape[-1]
    width = columns - 128
    anywhere = pl.BlockSpec(memory_space=pl.ANY)
    return pl.pallas_call(
        functools.partial(project_kernel, len(parts)),
        in_specs=[SCALAR] + [anywhere] * (1 + len(parts)),
        out_specs=[anywhere] * 3 + [pl.BlockSpec(memory_space=pltpu.VMEM)],
        out_shape=[
            jax.ShapeDtypeStruct((length, width), BF16),
            jax.ShapeDtypeStruct((model, length), BF16),
            jax.ShapeDtypeStruct((model, columns), BF16),
            jax.ShapeDtypeStruct((8, model), F32),
        ],
        scratch_shapes=[
            pltpu.VMEM((length, model), F32),
            pltpu.VMEM((model, columns), BF16),
            pltpu.VMEM((length, width), BF16),
            pltpu.VMEM((model, length), BF16),
            pltpu.SemaphoreType.DMA((5,)),
            pltpu.SemaphoreType.DMA((PARTS,)),
        ],
        compiler_params=params(40),
        cost_estimate=pl.CostEstimate(
            flops=2 * length * model * width, bytes_accessed=16 * length * model, transcendentals=0
        ),
        name="project",
    )(me, rows, *parts)


def mix_out_kernel(count, me, mixture_from, *refs):
    parts = refs[:count]
    out_to, weight_to, mixture, weight, out, sems, part_sems = refs[count:]
    copy = pltpu.make_async_copy
    loads = load_parts(me, parts, slice(0, weight.shape[1]), weight, part_sems)
    loads.append(copy(mixture_from, mixture, sems.at[0]))
    for each in loads:
        each.start()
    for each in loads:
        each.wait()
    stores = [copy(weight, weight_to, sems.at[1])]
    stores[0].start()
    length = mixture.shape[0]
    for i in range(2):
        part = slice(i * length // 2, (i + 1) * length // 2)
        out[part] = nt(mixture[part], weight[...]).astype(BF16)
        stores.append(copy(out.at[part], out_to.at[part], sems.at[2 + i]))
        stores[-1].start()
    for store in stores:
        store.wait()


def mix_out(me, mixture, parts, model):
    length, width = mixture.shape
    anywhere = pl.BlockSpec(memory_space=pl.ANY)
    vmem = lambda *shape: pltpu.VMEM(shape, BF16)
    return pl.pallas_call(
        functools.partial(mix_out_kernel, len(parts)),
        in_specs=[SCALAR] + [anywhere] * (1 + len(parts)),
        out_specs=[anywhere] * 2,
        out_shape=[
            jax.ShapeDtypeStruct((length, model), BF16),
            jax.ShapeDtypeStruct((model, width), BF16),
        ],
        scratch_shapes=[vmem(length, width), vmem(model, width), vmem(length, model)]
        + [pltpu.SemaphoreType.DMA((4,)), pltpu.SemaphoreType.DMA((PARTS,))],
        compiler_params=params(24),
        cost_estimate=pl.CostEstimate(
            flops=2 * length * model * width, bytes_accessed=4 * length * model, transcendentals=0
        ),
        name="mix_out",
    )(me, mixture, *parts)


def middle_kernel(rows, own, other, gains, hidden, normed):
    total = rows[...] + (own[...].astype(F32) + other[...].astype(F32))
    hidden[...] = total
    normed[...] = (norm(total)[0] * gains[1:2]).astype(BF16)


def middle(rows, own, other, gains):
    count, model = rows.shape
    return row_call(
        middle_kernel, "middle", count,
        [rows_spec(model)] * 3 + [fixed_spec(8, model)],
        [(rows_spec(model), ((count, model), F32)), (rows_spec(model), ((count, model), BF16))],
        [], 0, rows, own, other, gains,
    )


def after_kernel(order, hidden, own, other, grad_out, gains, weight, mixture, *refs):
    grad_attn, grad_mix, sums, acc = refs[-4:]
    step = pl.program_id(0)

    @pl.when(step == 0)
    def _():
        acc[...] = jnp.zeros(acc.shape, F32)

    grad = own[...].astype(F32) + other[...].astype(F32)
    grad = grad_out[...].astype(F32) + norm_back(grad, hidden[...], gains[1:2])
    low = grad.astype(BF16)
    grad_attn[...] = low
    grad_mix[...] = nn(low, weight[...]).astype(BF16)
    acc[...] += nn(grad.T.astype(BF16), mixture[...])

    @pl.when(step == pl.num_programs(0) - 1)
    def _():
        part = acc.shape[0] // len(order)
        for k, start in enumerate(order):
            sums[k * part : (k + 1) * part] = acc[start : start + part].astype(BF16)


def after_ffn(hidden, own, other, grad_out, gains, weights, mixture, order, after=()):
    rows, model = hidden.shape
    width = mixture.shape[1]
    return row_call(
        functools.partial(after_kernel, order), "after_ffn", rows,
        [rows_spec(model)] * 4
        + [fixed_spec(8, model), fixed_spec(model, width), rows_spec(width)]
        + [pl.BlockSpec(memory_space=pl.ANY)] * len(after),
        [
            (rows_spec(model), ((rows, model), BF16)),
            (rows_spec(width), ((rows, width), BF16)),
            (fixed_spec(model, width), ((model, width), BF16)),
        ],
        [pltpu.VMEM((model, width), F32)], 4 * rows * model * width,
        hidden, own, other, grad_out, gains, weights, mixture, *after,
    )


def last_kernel(count, rows, own, other, grad, gains, spread, *refs):
    text_grad, patch_grad, acc = refs[-3:]
    step = pl.program_id(0)

    @pl.when(step == 0)
    def _():
        acc[...] = jnp.zeros(acc.shape, F32)

    total = own[...].astype(F32) + other[...].astype(F32)
    total = grad[...].astype(F32) + norm_back(total, rows[...], gains[:1])

    @pl.when(step < pl.num_programs(0) - 1)
    def _():
        text_grad[...] = jnp.where(is_text(count), total, 0.0).astype(BF16)

    high = total.astype(BF16)
    low = (total - high.astype(F32)).astype(BF16)
    places = spread[...].astype(F32).T.astype(BF16)
    acc[...] += nn(places, high) + nn(places, low)

    @pl.when(step == pl.num_programs(0) - 1)
    def _():
        patch_grad[...] = acc[...].astype(BF16)


def last(count, rows, own, other, grad, gains, spread, texts, after=()):
    length, model = rows.shape
    slots = spread.shape[1]
    return row_call(
        last_kernel, "last", length,
        [SCALAR] + [rows_spec(model)] * 4 + [fixed_spec(8, model), rows_spec(slots)]
        + [pl.BlockSpec(memory_space=pl.ANY)] * len(after),
        [(rows_spec(model, texts), ((texts, model), BF16)), (fixed_spec(slots, model), ((slots, model), BF16))],
        [pltpu.VMEM((slots, model), F32)], 4 * length * model * slots,
        count, rows, own, other, grad, gains, spread, *after,
    )


def result_kernel(count, hidden, own, other, pick, *refs):
    text_out, patch_out, acc = refs[-3:]
    step = pl.program_id(0)

    @pl.when(step == 0)
    def _():
        acc[...] = jnp.zeros(acc.shape, F32)

    total = hidden[...] + (own[...].astype(F32) + other[...].astype(F32))

    @pl.when(step < pl.num_programs(0) - 1)
    def _():
        text_out[...] = jnp.where(is_text(count), total, 0.0).astype(BF16)

    acc[...] += nn(pick[...].astype(F32).T.astype(BF16), total.astype(BF16))

    @pl.when(step == pl.num_programs(0) - 1)
    def _():
        patch_out[...] = acc[...].astype(BF16)


def result(count, hidden, own, other, pick, texts, after=()):
    length, model = hidden.shape
    slots = pick.shape[1]
    return row_call(
        result_kernel, "result", length,
        [SCALAR] + [rows_spec(model)] * 3 + [rows_spec(slots)]
        + [pl.BlockSpec(memory_space=pl.ANY)] * len(after),
        [(rows_spec(model, texts), ((texts, model), BF16)), (fixed_spec(slots, model), ((slots, model), BF16))],
        [pltpu.VMEM((slots, model), F32)], 2 * length * model * slots,
        count, hidden, own, other, pick, *after,
    )


def finish_kernel(cuts, ffn_one, ffn_two, heads_a, heads, wq, wk, wv, w_gate, w_up, *outs):
    part, width = wq.shape
    half = width // 2
    start = 0
    for size, source in zip(cuts, (ffn_one, ffn_two)):
        for i, out in enumerate(outs[4:7]):
            out[:, start : start + size] = source[:, i * size : (i + 1) * size].astype(F32)
        start += size
    for i, out in enumerate(outs[:3]):
        out[:, :half] = heads_a[:, i * half : (i + 1) * half].astype(F32)
        out[:, half:] = heads[:, i * half : (i + 1) * half].astype(F32)
    outs[3][...] = heads_a[:, 3 * half :].astype(F32)
    total = lambda w, out: jnp.sum(w[...].astype(F32) * out[...], axis=1, keepdims=True)
    one = total(wq, outs[0]) + total(wk, outs[1]) + total(wv, outs[2])
    two = total(w_gate, outs[4]) + total(w_up, outs[5])
    lane = lax.broadcasted_iota(jnp.int32, (part, 128), 1)
    outs[7][...] = jnp.where(lane == 0, one, jnp.where(lane == 1, two, 0.0))


def finish(sums, weights, cuts, width):
    part, hidden = weights[-1].shape
    shapes = [(part, width)] * 4 + [(part, hidden)] * 3 + [(part, 128)]
    return pl.pallas_call(
        functools.partial(finish_kernel, cuts),
        out_shape=[jax.ShapeDtypeStruct(shape, F32) for shape in shapes],
        compiler_params=params(20),
        name="finish",
    )(*sums, *weights)


def lay_index():
    cell = jnp.arange(CELLS, dtype=jnp.int32)
    row, col = cell // GRID, cell % GRID
    row_gap = jnp.minimum(jnp.abs(row[:, None] - row[None, :]), LQ - 1)
    col_gap = jnp.minimum(jnp.abs(col[:, None] - col[None, :]), LQ - 1)
    real = (cell < PATCHES)[:, None] & (cell < PATCHES)[None, :]
    return jnp.where(real, row_gap * LQ + col_gap, LQ * LQ)


def body(
    text_in, patch_in, cot_text, cot_patch, text_count, intersection, text_cell,
    wq, wk, wv, wo_t, gain_one, w_gate, w_up, w_down_t, gain_two, bias_table,
):
    chips = Chips()
    me = lax.axis_index("dp")
    text_slots, model = text_in.shape[1:]
    patch_slots = patch_in.shape[1]
    rows_count = text_slots + patch_slots
    live_slots = (PATCHES + 15) // 16 * 16
    width = wq.shape[1]
    hidden = w_gate.shape[1]

    count = lax.dynamic_slice_in_dim(text_count, me, 1, 0)
    place = lax.dynamic_index_in_dim(text_cell, me, 0, keepdims=False)
    slot = jnp.arange(rows_count, dtype=jnp.int32)
    is_text, live = slot < count, slot < count + PATCHES
    patch_id = jnp.arange(live_slots, dtype=jnp.int32)
    covers = jnp.zeros((rows_count, live_slots), F32)
    for k in range(intersection.shape[1]):
        listed = jnp.pad(intersection[0, k], (0, patch_slots))
        covers = covers + (listed[:, None] == patch_id).astype(F32)
    pick = ((slot - count)[:, None] == patch_id) & (patch_id < PATCHES)
    spread = jnp.where(is_text[:, None] & (patch_id < PATCHES), covers, pick.astype(F32))
    spread = spread.astype(BF16)
    pick = pick.astype(BF16)

    cell = jnp.pad(place[0] * GRID + place[1], (0, patch_slots))
    cell = jnp.where(is_text, cell, slot - count)
    feature = jnp.arange(CELLS, dtype=jnp.int32)
    key_tile = slot // 128 + TILE0
    cells = (live[:, None] & (cell[:, None] == feature) & (feature < PATCHES)).astype(BF16)
    cells = cells + (key_tile[:, None] == feature).astype(BF16)
    cells = cells + (~live[:, None] & (feature == DEAD)).astype(BF16)
    feature = feature[:FEAT_ROWS, None]
    cells_t = (live & (cell == feature) & (feature < PATCHES)) | (key_tile == feature)
    cells_t = cells_t.astype(BF16)
    lay = lay_index()
    table = bias_table.astype(F32)

    cut = hidden // 3 // 256 * 256 + 256
    gains = jnp.pad(jnp.stack([gain_one, gain_two], axis=1), ((0, 0), (0, 126)))
    sent = []
    qkv, layers, planes, corners = chips.gather_rows(
        jnp.concatenate([wq, wk, wv, gains], axis=1),
        aside=lambda layers: (sent.append(send_half(patch_in[0, :live_slots], layers)), sent[0])[1:],
    )
    sent = sent or [send_half(patch_in[0, :live_slots])]
    patches = join_halves(sent[0])
    heard = planes
    first_set, layers, planes, _ = chips.gather_rows(
        jnp.concatenate([wo_t, w_gate[:, :cut], w_up[:, :cut], w_down_t[:, :cut]], axis=1),
        planes, corners,
    )
    patch_cot = join_halves(send_half(cot_patch[0, :live_slots], layers))
    last_set = lax.all_gather(
        tie(jnp.concatenate([w_gate[:, cut:], w_up[:, cut:], w_down_t[:, cut:]], axis=1), *heard),
        "dp", axis=0, tiled=True,
    )
    rows = embed(count, text_in[0], spread, patches)
    grad_ffn = embed(count, cot_text[0], pick, patch_cot, BF16)

    place = me[None].astype(jnp.int32)
    projected, normed_t, qkv, gains = project(place, rows, qkv)
    half = width // 256
    seen = attend(table, projected, cells, lay, 0, half, width)
    mixture, probs, inverse = attend(table, projected, cells, lay, half, half, width, seen, (*planes, patch_cot))
    part, wo_all = mix_out(place, mixture, first_set, model)
    hidden_rows, normed_two = middle(rows, part, other_core(part), gains)

    order = chips.order(model)
    ffn_part, grad_part, grads_one = ffn(
        place, normed_two, grad_ffn, first_set, width, cut, order
    )
    ffn_part, grad_part, grads_two = ffn(
        place, normed_two, grad_ffn, (last_set,), 0, hidden - cut, order, (ffn_part, grad_part)
    )
    scatter = lambda a, groups: lax.psum_scatter(
        a, "dp", scatter_dimension=0, axis_index_groups=groups, tiled=True
    )
    sum_one, sum_two = scatter(grads_one, chips.planes), scatter(grads_two, chips.planes)
    grad_attn, grad_mix, wo_grad = after_ffn(
        hidden_rows, grad_part, other_core(grad_part), grad_ffn, gains, wo_all, mixture, order
    )
    sum_one = chips.exchange(tie(sum_one, grad_mix), chips.columns)
    args = (projected, grad_mix, mixture, probs, inverse, cells, cells_t, lay, normed_t, qkv)
    normed_a, grads_a, table_part = heads_back(
        *args, 0, half, order, chips.plane, jnp.zeros((16, 128), F32), wo_grad
    )
    ffn_part = tie(ffn_part, grad_mix)
    text_out, patch_out = result(
        count, hidden_rows, ffn_part, other_core(ffn_part), pick, text_slots, (normed_a,)
    )
    patch_sent = send_half(patch_out)
    sum_two = scatter(tie(sum_two, patch_out), chips.columns)
    sum_a = chips.exchange(tie(grads_a.reshape(model, -1), patch_out), chips.planes).astype(BF16)
    normed_part, grads_b, _ = heads_back(
        *args, half, half, order, chips.plane, table_part, normed_a, (sum_one, patch_out)
    )
    grads_b = tie(grads_b, sum_a)
    sum_a = scatter(tie(sum_a, normed_part), chips.columns)
    text_grad, patch_grad = last(
        count, rows, normed_part, other_core(normed_part), grad_attn, gains, spread, text_slots
    )
    patch_grad = send_half(patch_grad)
    sum_b = chips.trade(grads_b, chips.planes, (text_grad, patch_sent))
    chunk = model // chips.plane
    layers = chips.sizes[0]
    table_rows = split_table(sum_b[chunk:])
    sum_b = sum_b[:chunk].astype(BF16).reshape(layers, chunk // layers, -1)
    sum_b = jnp.concatenate([sum_b, jnp.broadcast_to(table_rows, (layers,) + table_rows.shape)], axis=1)
    sum_b = chips.trade(tie(sum_b, sum_two), chips.columns)
    sum_b, table_sum = sum_b[: chunk // layers], sum_b[chunk // layers :]
    table_sum = table_sum[:, :48] + table_sum[:, 128 : 128 + 48]
    table_sum = table_sum.reshape(16, 3, 16)[:, :, : table.shape[1]].transpose(1, 0, 2).reshape(table.shape)
    fill = lambda a: jnp.pad(a, ((0, patch_slots - live_slots), (0, 0)))
    patch_grad = fill(join_halves(tie(patch_grad, sum_b)))
    patch_out = fill(join_halves(tie(patch_sent, sum_b)))

    *sums, own = finish(
        (sum_one, sum_two, sum_a, sum_b), (wq, wk, wv, w_gate, w_up), (cut, hidden - cut), width
    )
    wq_sum, wk_sum, wv_sum, wo_sum, gate_sum, up_sum, down_sum = sums
    own = (own + other_core(own))[:, :2] / jnp.stack([gain_one, gain_two], axis=1).astype(F32)
    return (
        text_out[None], patch_out[None], text_grad[None], patch_grad[None],
        wq_sum, wk_sum, wv_sum, wo_sum, own[:, 0], gate_sum, up_sum, down_sum, own[:, 1],
        table_sum,
    )


def split_table(rows):
    values = rows[:, :128] + rows[:, 128:256]
    high = values.astype(BF16)
    low = (values - high.astype(F32)).astype(BF16)
    return jnp.concatenate([high, low, jnp.zeros((16, rows.shape[1] - 256), BF16)], axis=1)


def solution(mesh):
    page, weight, vector = P("dp", None, None), P("dp", "mp"), P("dp")
    return jax.shard_map(
        body,
        mesh=mesh,
        in_specs=(page,) * 4
        + (P(), page, P())
        + (weight,) * 4
        + (vector,)
        + (weight,) * 3
        + (vector, P(None, "mp")),
        out_specs=(page,) * 4
        + (weight,) * 4
        + (vector,)
        + (weight,) * 3
        + (vector, P(None, "mp")),
        check_vma=False,
    )
```
